32 devices in a mesh: dp: 8 (over z, core), mp: 4 (over y, x).
Axes of the slice: x: 2, y: 2, z: 4, core: 2. Of those that a mesh axis runs over, the one named last changes fastest.
Arguments:
- tokens: bfloat16 [32768, 1024], P(('dp', 'mp')), may hold values from -6 to 6
- action_ids: int32 [8, 16], P('dp'), may hold values from 0 to 7
- clip_lengths: int32 [8], P('dp'), may hold values from 4 to 16, as said below
- action_table: float32 [8, 1024], replicated, may hold values from -3 to 3
- norm_gains: float32 [3, 1024], replicated, may hold values from 0.5 to 1.5
- norm_shifts: float32 [3, 1024], replicated, may hold values from -2 to 2
- spatial_qkv: bfloat16 [3, 1024, 1024], P(None, None, 'mp'), may hold values from -0.1875 to 0.1875
- spatial_out: bfloat16 [1024, 1024], P('mp'), may hold values from -0.75 to 0.75
- temporal_qkv: bfloat16 [3, 1024, 1024], P(None, None, 'mp'), may hold values from -0.1875 to 0.1875
- temporal_out: bfloat16 [1024, 1024], P('mp'), may hold values from -0.375 to 0.375
- ff_in: bfloat16 [1024, 4096], P(None, 'mp'), may hold values from -0.1875 to 0.1875
- ff_out: bfloat16 [4096, 1024], P('mp'), may hold values from -0.09375 to 0.09375
- out_grad: bfloat16 [32768, 1024], P(('dp', 'mp')), may hold values from -6 to 6
Outputs:
- mixed: bfloat16 [32768, 1024], P(('dp', 'mp'))
- tokens_grad: float32 [32768, 1024], P(('dp', 'mp'))
- table_grad: float32 [8, 1024], replicated
- gains_grad: float32 [3, 1024], replicated
- shifts_grad: float32 [3, 1024], replicated
- spatial_qkv_grad: float32 [3, 1024, 1024], P(None, None, 'mp')
- spatial_out_grad: float32 [1024, 1024], P('mp')
- temporal_qkv_grad: float32 [3, 1024, 1024], P(None, None, 'mp')
- temporal_out_grad: float32 [1024, 1024], P('mp')
- ff_in_grad: float32 [1024, 4096], P(None, 'mp')
- ff_out_grad: float32 [4096, 1024], P('mp')
The draws below stay inside these ranges and needn't reach their ends.
Inputs may be any that keep to these rules, and one draw needn't show every extreme that they name: `clip_lengths`: some clip has all 16 frames and some clip has 4.
All inputs are finite; a program needn't handle non-finite values.
Results may differ from the reference program's by a relative error of at most 0.022.
Values may be sent and summed in bfloat16 or wider, within the bound.
No kernel may reach another device: no remote copies, remote signals or barrier semaphores. Data moves between devices by JAX's collectives and lax.ppermute only.
A program may use at most 320 MiB of HBM per device.

```python
import jax
import jax.numpy as jnp
from jax import lax

D = 1024
HEADS = 16
HEAD_DIM = 64
FF = 4096
FRAMES = 16
POS = 256
ACTIONS = 8
CLIPS = 8
TOKENS = 32768


def draw_clip_lengths(key, part):
    key = jax.random.fold_in(key, 7)
    key_lengths, key_pick = jax.random.split(key)
    lengths = jax.random.randint(key_lengths, (CLIPS,), 4, FRAMES + 1)
    order = jax.random.permutation(key_pick, CLIPS)
    positions = jnp.arange(CLIPS)
    lengths = jnp.where(positions == order[0], FRAMES, lengths)
    lengths = jnp.where(positions == order[1], 4, lengths)
    return lengths.astype(jnp.int32)


def with_ends(values, rng, low, top_value):
    extent = values.shape
    index_at = [jax.random.randint(jax.random.fold_in(rng, axis), (), 0, extent[axis]) for axis in range(len(extent))]
    values = values.at[tuple(index_at)].set(low)
    longest = extent.index(max(extent))
    index_at[longest] = (index_at[longest] + 1) % extent[longest]
    return values.at[tuple(index_at)].set(top_value)


def block_scale(rng, extent, cuts, least, largest):
    loudness = 1.0
    for position, shards_of in cuts:
        draws = jax.random.uniform(jax.random.fold_in(jax.random.fold_in(rng, 6), position), (shards_of,), jnp.float32, least / len(cuts), largest / len(cuts))
        loudness = loudness * jnp.repeat(jnp.exp(draws), extent[position] // shards_of).reshape((-1,) + (1,) * (len(extent) - 1 - position))
    return loudness


def normal_values(rng, shape, spread, limit, cuts=(), dtype=jnp.bfloat16):
    factor_of = block_scale(rng, shape, cuts, -0.22, 0.18) if cuts else 1.0
    drawn = jax.random.normal(rng, shape, jnp.float32) * spread * factor_of
    return jnp.minimum(jnp.maximum(drawn, -limit), limit).astype(dtype)


def setup_inputs(seed: int = 0) -> dict:
    key_list = jax.random.split(jax.random.key(seed), 14)
    tokens = normal_values(key_list[0], (TOKENS, D), 1.0, 6.0, ((0, 32),))
    action_ids = with_ends(jax.random.randint(key_list[1], (CLIPS, FRAMES), 0, ACTIONS), jax.random.fold_in(key_list[1], 1), 0, ACTIONS - 1).astype(jnp.int32)
    clip_lengths = draw_clip_lengths(jax.random.fold_in(key_list[13], 71), 0)
    action_table = normal_values(key_list[3], (ACTIONS, D), 0.5, 3.0, (), jnp.float32)
    norm_gains = jnp.clip(1.0 + 0.1 * jax.random.normal(key_list[4], (3, D), jnp.float32), 0.5, 1.5)
    norm_shifts = normal_values(key_list[5], (3, D), 0.3, 2.0, (), jnp.float32)
    spatial_qkv = normal_values(key_list[6], (3, D, HEADS * HEAD_DIM), D ** -0.5, 0.1875, ((2, 4),))
    spatial_out = normal_values(key_list[7], (HEADS * HEAD_DIM, D), (HEADS * HEAD_DIM * 16 // POS) ** -0.5, 0.75, ((0, 4),))
    temporal_qkv = normal_values(key_list[8], (3, D, HEADS * HEAD_DIM), D ** -0.5, 0.1875, ((2, 4),))
    temporal_out = normal_values(key_list[9], (HEADS * HEAD_DIM, D), (HEADS * HEAD_DIM // 4) ** -0.5, 0.375, ((0, 4),))
    ff_in = normal_values(key_list[10], (D, FF), D ** -0.5, 0.1875, ((1, 4),))
    ff_out = normal_values(key_list[11], (FF, D), FF ** -0.5, 0.09375, ((0, 4),))
    out_grad = normal_values(key_list[12], (TOKENS, D), 1.0, 6.0, ((0, 32),))
    return dict(tokens=tokens, action_ids=action_ids, clip_lengths=clip_lengths, action_table=action_table, norm_gains=norm_gains, norm_shifts=norm_shifts, spatial_qkv=spatial_qkv, spatial_out=spatial_out, temporal_qkv=temporal_qkv, temporal_out=temporal_out, ff_in=ff_in, ff_out=ff_out, out_grad=out_grad)


EPS = 1e-05

@jax.custom_vjp
def low(v):
    return lax.optimization_barrier(v.astype(jnp.bfloat16)).astype(jnp.float32)

@jax.custom_vjp
def low_back(v):
    return v

def low_keep(v):
    return (low(v), None)

def low_pass(kept, grad):
    return (grad,)

def back_keep(v):
    return (v, None)

def back_low(kept, grad):
    return (low(grad),)
low.defvjp(low_keep, low_pass)
low_back.defvjp(back_keep, back_low)

def product(left, right):
    return jnp.dot(left, right, precision=lax.Precision.HIGHEST)

def rounded(values):
    return low(low_back(values))

def layer_norm(hidden, gain_row, shift_row):
    average = lax.optimization_barrier(jnp.mean(hidden, axis=-1, keepdims=True))
    centred = hidden - average
    variance = lax.optimization_barrier(jnp.mean(centred * centred, axis=-1, keepdims=True))
    return centred * lax.rsqrt(variance + EPS) * gain_row + shift_row

def attend(normed, weight_qkv, weight_out, head_shape, patterns, frame_mask):
    row_count = normed.shape[0]
    sent = low(normed)
    queries = rounded(product(sent, weight_qkv[0])).reshape(head_shape)
    key_rows = rounded(product(sent, weight_qkv[1])).reshape(head_shape)
    values = rounded(product(sent, weight_qkv[2])).reshape(head_shape)
    logits = low_back(jnp.einsum(patterns[0], queries, key_rows, precision=lax.Precision.HIGHEST)) * HEAD_DIM ** (-0.5)
    logits = jnp.where(frame_mask, logits, -1000000000.0)
    attn_probs = low(jax.nn.softmax(logits, axis=-1))
    context = rounded(jnp.einsum(patterns[1], attn_probs, values, precision=lax.Precision.HIGHEST)).reshape(row_count, -1)
    return low_back(product(context, weight_out))

def block(clip_rows, action_table, norm_gains, norm_shifts, spatial_qkv, spatial_out, temporal_qkv, temporal_out, ff_in, ff_out, frame_ids, length):
    first = clip_rows + jnp.repeat(action_table[frame_ids], POS, axis=0)
    head_shape = (FRAMES, POS, HEADS, HEAD_DIM)
    second = first + attend(layer_norm(first, norm_gains[0], norm_shifts[0]), spatial_qkv, spatial_out, head_shape, ('fqhe,fkhe->fhqk', 'fhqk,fkhe->fqhe'), jnp.array(True))
    frame_q = lax.broadcasted_iota(jnp.int32, (FRAMES, FRAMES), 0)
    frame_k = lax.broadcasted_iota(jnp.int32, (FRAMES, FRAMES), 1)
    frame_mask = (frame_k <= frame_q) & (frame_k < length)
    third = second + attend(layer_norm(second, norm_gains[1], norm_shifts[1]), temporal_qkv, temporal_out, head_shape, ('qphe,kphe->phqk', 'phqk,kphe->qphe'), frame_mask)
    sent = low(layer_norm(third, norm_gains[2], norm_shifts[2]))
    pre_act = low_back(product(sent, ff_in))
    hidden = low(jax.nn.gelu(pre_act))
    return third + low_back(product(hidden, ff_out))

def reference(tokens, action_ids, clip_lengths, action_table, norm_gains, norm_shifts, spatial_qkv, spatial_out, temporal_qkv, temporal_out, ff_in, ff_out, out_grad):
    weights = tuple((w.astype(jnp.float32) for w in (action_table, norm_gains, norm_shifts, spatial_qkv, spatial_out, temporal_qkv, temporal_out, ff_in, ff_out)))
    clip_tokens = tokens.astype(jnp.float32).reshape(CLIPS, FRAMES * POS, D)
    clip_grads = out_grad.astype(jnp.float32).reshape(CLIPS, FRAMES * POS, D)

    def per_clip(totals, inputs_clip):
        clip_rows, grad_rows, frame_ids, length = inputs_clip

        def apply_block(rows_in, *params):
            return block(rows_in, *params, frame_ids, length)
        result, pull_back = jax.vjp(apply_block, clip_rows, *weights)
        grads = pull_back(grad_rows)
        totals = tuple((total + grad for total, grad in zip(totals, grads[1:])))
        return (totals, (result.astype(jnp.bfloat16), grads[0]))
    zeros_init = tuple((jnp.zeros_like(w) for w in weights))
    grad_sums, (results, input_grads) = lax.scan(per_clip, zeros_init, (clip_tokens, clip_grads, action_ids, clip_lengths))
    return (results.reshape(TOKENS, D), input_grads.reshape(TOKENS, D), grad_sums[0], grad_sums[1], grad_sums[2], grad_sums[3], grad_sums[4], grad_sums[5], grad_sums[6], grad_sums[7], grad_sums[8])
```

```python
import functools

import jax
import jax.numpy as jnp
from jax import lax
from jax.experimental import pallas as pl
from jax.experimental.pallas import tpu as pltpu
from jax.sharding import PartitionSpec as P

D = 1024
HEAD_DIM = 64
FRAMES = 16
POS = 256
ACTIONS = 8
EPS = 1e-05
BLOCK = 256
GROUP = BLOCK // FRAMES
BF16 = jnp.bfloat16
F32 = jnp.float32


def norm_rows(hidden, gain_row, shift_row):
    average = jnp.mean(hidden, axis=-1, keepdims=True)
    centred = hidden - average
    inverse = lax.rsqrt(jnp.mean(centred * centred, axis=-1, keepdims=True) + EPS)
    scaled = centred * inverse
    return scaled * gain_row + shift_row, scaled, inverse


def norm_back(gradient, scaled, inverse, gain_row):
    grad_gain = jnp.sum(gradient * scaled, axis=0)
    grad_shift = jnp.sum(gradient, axis=0)
    inner = gradient * gain_row
    grad_in = inverse * (
        inner
        - jnp.mean(inner, axis=-1, keepdims=True)
        - scaled * jnp.mean(inner * scaled, axis=-1, keepdims=True)
    )
    return grad_in, grad_gain, grad_shift


def flip(values, offset, axis="mp"):
    size = lax.axis_size(axis)
    return lax.ppermute(values, axis, [(i, i ^ offset) for i in range(size)])


def twin(values):
    return flip(values, 1, "dp")


def bits_of(reverse):
    bits = [1 << b for b in range(lax.axis_size("mp").bit_length() - 1)]
    return bits[::-1] if reverse else bits


def gather(piece, reverse):
    slots = {0: piece}
    for bit in bits_of(reverse):
        for slot in list(slots):
            slots[slot | bit] = flip(slots[slot], bit)
    return [slots[s] for s in range(len(slots))]


def add(left, right):
    return (left.astype(F32) + right.astype(F32)).astype(BF16)


def scatter(slots, reverse):
    slots = dict(enumerate(slots))
    for bit in bits_of(reverse):
        for slot in [s for s in slots if s & bit]:
            slots[slot ^ bit] = add(slots[slot ^ bit], flip(slots.pop(slot), bit))
    return slots[0]


def to_positions(rows):
    me, size = lax.axis_index("mp"), lax.axis_size("mp")
    frames_here = rows.shape[0] // POS
    here = POS // size
    view = rows.reshape(frames_here, POS, D)
    parts = []
    for slot in range(size):
        part = lax.dynamic_slice_in_dim(view, (me ^ slot) * here, here, axis=1)
        parts.append(flip(part, slot) if slot else part)
    whole = jnp.concatenate(parts, axis=0).reshape(FRAMES, here // GROUP, GROUP, D)
    return whole.transpose(1, 0, 2, 3).reshape(rows.shape)


def to_frames(rows):
    me, size = lax.axis_index("mp"), lax.axis_size("mp")
    frames_here = rows.shape[0] // POS
    here = POS // size
    view = rows.reshape(here // GROUP, size, frames_here, GROUP, D)
    whole = jnp.zeros((frames_here, POS, D), rows.dtype)
    for slot in range(size):
        part = view[:, slot]
        part = flip(part, slot) if slot else part
        part = part.transpose(1, 0, 2, 3).reshape(frames_here, here, D)
        whole = lax.dynamic_update_slice_in_dim(whole, part, (me ^ slot) * here, axis=1)
    return whole.reshape(rows.shape)


def nn(left, right):
    return lax.dot_general(left, right, (((1,), (0,)), ((), ())), preferred_element_type=F32)


def nt(left, right):
    return lax.dot_general(left, right, (((1,), (1,)), ((), ())), preferred_element_type=F32)


def tn(left, right):
    return lax.dot_general(left, right, (((0,), (0,)), ((), ())), preferred_element_type=F32)


def load_weights(pieces, qkv, out):
    half = pieces[0][1].shape[-1]
    width = half * len(pieces)

    @pl.when(pl.program_id(0) == 0)
    def _():
        for index, (qk, v, o) in enumerate(pieces):
            at = index * half
            qkv[:, at : at + half] = qk[0]
            qkv[:, width + at : width + at + half] = qk[1]
            qkv[:, 2 * width + at : 2 * width + at + half] = v[...]
            out[at : at + half, :] = o[...]


def head_lanes(shape, which):
    return lax.broadcasted_iota(jnp.int32, shape, 1) // HEAD_DIM == which


def probabilities(q_pair, k_pair, which, mask):
    q_head = jnp.where(head_lanes(q_pair.shape, which), q_pair * 0.125, 0).astype(BF16)
    logits = nt(q_head, k_pair)
    if mask is not None:
        logits = logits + mask
    raised = jnp.exp(logits - jnp.max(logits, axis=-1, keepdims=True))
    return raised / jnp.sum(raised, axis=-1, keepdims=True)


def attend_kernel(masked, parts, *refs):
    refs = list(refs)
    mask = refs.pop(0)[...] if masked else None
    n_ref = refs.pop(0)
    pieces = [tuple(refs.pop(0) for _ in range(3)) for _ in range(parts)]
    acc_ref, out_ref, qkv_ref, ctx_ref, w_qkv, w_out = refs
    load_weights(pieces, w_qkv, w_out)
    width = w_out.shape[0]
    qkv = nn(n_ref[...], w_qkv[...]).astype(BF16)
    qkv_ref[...] = qkv
    for at in range(0, width, 2 * HEAD_DIM):
        q = qkv[:, at : at + 128]
        k = qkv[:, width + at : width + at + 128]
        v = qkv[:, 2 * width + at : 2 * width + at + 128]
        heads = [nn(probabilities(q, k, h, mask).astype(BF16), v) for h in range(2)]
        ctx_ref[:, at : at + 128] = jnp.where(head_lanes(q.shape, 0), *heads).astype(BF16)
    out_ref[...] = acc_ref[...] + nn(ctx_ref[...], w_out[...])


def whole_spec(array):
    return pl.BlockSpec(array.shape, lambda i: (0,) * array.ndim)


def rows_spec(width):
    return pl.BlockSpec((BLOCK, width), lambda i: (i, 0))


def join(pieces):
    if pieces[0][1].shape[-1] % 128 == 0:
        return pieces
    qk, v, o = zip(*pieces)
    return [(jnp.concatenate(qk, 2), jnp.concatenate(v, 1), jnp.concatenate(o, 0))]


def attend_slot(normed, pieces, acc, mask):
    rows = normed.shape[0]
    pieces = join(pieces)
    flat = [x for piece in pieces for x in piece]
    width = sum(p[1].shape[-1] for p in pieces)
    first = [] if mask is None else [mask]
    args = first + [normed] + flat + [acc]
    specs = [whole_spec(x) for x in first] + [rows_spec(D)] + [whole_spec(x) for x in flat] + [rows_spec(D)]
    return pl.pallas_call(
        functools.partial(attend_kernel, mask is not None, len(pieces)),
        grid=(rows // BLOCK,),
        in_specs=specs,
        out_specs=[rows_spec(D), rows_spec(3 * width), rows_spec(width)],
        out_shape=[
            jax.ShapeDtypeStruct((rows, D), F32),
            jax.ShapeDtypeStruct((rows, 3 * width), BF16),
            jax.ShapeDtypeStruct((rows, width), BF16),
        ],
        scratch_shapes=[pltpu.VMEM((D, 3 * width), BF16), pltpu.VMEM((width, D), BF16)],
        compiler_params=pltpu.CompilerParams(vmem_limit_bytes=40 << 20),
        cost_estimate=pl.CostEstimate(
            flops=2 * rows * D * width * 4 + 4 * rows * BLOCK * width * 4,
            bytes_accessed=rows * D * 10 + D * width * 8 + rows * width * 8,
            transcendentals=rows * BLOCK * width // HEAD_DIM,
        ),
        name="attend",
    )(*args)


def back_kernel(masked, parts, steps, *refs):
    refs = list(refs)
    mask = refs.pop(0)[...] if masked else None
    n_ref, g_ref, qkv_ref, ctx_ref = (refs.pop(0) for _ in range(4))
    pieces = [tuple(refs.pop(0) for _ in range(3)) for _ in range(parts)]
    acc_ref, out_ref = refs.pop(0), refs.pop(0)
    grads = [tuple(refs.pop(0) for _ in range(3)) for _ in range(parts)]
    w_qkv, w_out, d_qkv = refs
    load_weights(pieces, w_qkv, w_out)
    width = w_out.shape[0]
    step = pl.program_id(0)
    rows = pl.ds(pl.multiple_of(step * BLOCK, BLOCK), BLOCK)
    d_ctx = nt(g_ref[rows, :], w_out[...]).astype(BF16)
    for at in range(0, width, 2 * HEAD_DIM):
        q = qkv_ref[:, at : at + 128]
        k = qkv_ref[:, width + at : width + at + 128]
        v = qkv_ref[:, 2 * width + at : 2 * width + at + 128]
        dc = d_ctx[:, at : at + 128]
        dq, dk, dv = [], [], []
        for h in range(2):
            p = probabilities(q, k, h, mask)
            d_p = nt(jnp.where(head_lanes(dc.shape, h), dc, 0).astype(BF16), v)
            total = jnp.sum(d_p * p, axis=-1, keepdims=True)
            ds = (p * (d_p - total) * 0.125).astype(BF16)
            dq.append(nn(ds, k))
            dk.append(tn(ds, q))
            dv.append(tn(p.astype(BF16), dc))
        for index, pair in enumerate((dq, dk, dv)):
            start = index * width + at
            d_qkv[rows, start : start + 128] = jnp.where(head_lanes(q.shape, 0), *pair).astype(BF16)
    out_ref[...] = acc_ref[...] + nt(d_qkv[rows, :], w_qkv[...])

    @pl.when(step == steps - 1)
    def _():
        half = width // parts
        for index, (d_qk, d_v, d_o) in enumerate(grads):
            at = index * half
            d_qk[0] = tn(n_ref[...], d_qkv[:, at : at + half]).astype(BF16)
            d_qk[1] = tn(n_ref[...], d_qkv[:, width + at : width + at + half]).astype(BF16)
            d_v[...] = tn(n_ref[...], d_qkv[:, 2 * width + at : 2 * width + at + half]).astype(BF16)
            d_o[...] = tn(ctx_ref[:, at : at + half], g_ref[...]).astype(BF16)


def back_slot(normed, grad, kept, pieces, acc, mask):
    rows = normed.shape[0]
    qkv, ctx = kept
    halves = len(pieces)
    pieces = join(pieces)
    flat = [x for piece in pieces for x in piece]
    width = ctx.shape[-1]
    first = [] if mask is None else [mask]
    args = first + [normed, grad, qkv, ctx] + flat + [acc]
    specs = (
        [whole_spec(x) for x in first]
        + [whole_spec(normed), whole_spec(grad), rows_spec(3 * width), whole_spec(ctx)]
        + [whole_spec(x) for x in flat]
        + [rows_spec(D)]
    )
    out = pl.pallas_call(
        functools.partial(back_kernel, mask is not None, len(pieces), rows // BLOCK),
        grid=(rows // BLOCK,),
        in_specs=specs,
        out_specs=[rows_spec(D)] + [whole_spec(x) for x in flat],
        out_shape=[jax.ShapeDtypeStruct((rows, D), F32)]
        + [jax.ShapeDtypeStruct(x.shape, BF16) for x in flat],
        scratch_shapes=[
            pltpu.VMEM((D, 3 * width), BF16),
            pltpu.VMEM((width, D), BF16),
            pltpu.VMEM((rows, 3 * width), BF16),
        ],
        compiler_params=pltpu.CompilerParams(vmem_limit_bytes=48 << 20),
        cost_estimate=pl.CostEstimate(
            flops=4 * rows * D * width * 4 + 10 * rows * BLOCK * width * 4,
            bytes_accessed=rows * D * 12 + D * width * 16 + rows * width * 8,
            transcendentals=rows * BLOCK * width // HEAD_DIM,
        ),
        name="attend_back",
    )(*args)
    grads = [tuple(out[1 + 3 * i : 4 + 3 * i]) for i in range(len(pieces))]
    if len(grads) != halves:
        (qk, v, o), = grads
        half = width // 2
        grads = [
            (qk[:, :, a : a + half], v[:, a : a + half], o[a : a + half]) for a in (0, half)
        ]
    return out[0], grads


def after(values, first):
    return lax.optimization_barrier((values, first))[0]


def own_half(array, axis):
    half = array.shape[axis] // 2
    return lax.dynamic_slice_in_dim(array, (lax.axis_index("dp") % 2) * half, half, axis=axis)


def attention_pieces(weight_qkv, weight_out):
    mine = own_half(weight_qkv, 2)
    return mine[:2], mine[2], own_half(weight_out, 0)


def gather_attention(pieces):
    qk = gather(pieces[0], False)
    v = gather(pieces[1], True)
    o = gather(pieces[2], True)
    return [[mine, tuple(twin(x) for x in mine)] for mine in zip(qk, v, o)]


def reduce_slots(slots, reverse):
    return scatter([add(mine, twin(other)) for mine, other in slots], reverse)


def over_clips(values):
    size = lax.axis_size("dp")
    groups = [list(range(core, size, 2)) for core in range(2)]
    return lax.psum(values, "dp", axis_index_groups=groups)


def both_halves(mine, axis):
    other = twin(mine)
    first = lax.axis_index("dp") % 2 == 0
    return jnp.concatenate(
        [jnp.where(first, mine, other), jnp.where(first, other, mine)], axis=axis
    ).astype(F32)


def attention_grads(slots):
    order = [False, True, True]
    sums = [
        reduce_slots([(slots[s][0][i], slots[s][1][i]) for s in range(len(slots))], order[i])
        for i in range(3)
    ]
    qk, v, o = over_clips(tuple(sums))
    return both_halves(jnp.concatenate([qk, v[None]], axis=0), 2), both_halves(o, 0)


def shards(
    tokens,
    action_ids,
    clip_lengths,
    action_table,
    norm_gains,
    norm_shifts,
    spatial_qkv,
    spatial_out,
    temporal_qkv,
    temporal_out,
    ff_in,
    ff_out,
    out_grad,
):
    rows_here = tokens.shape[0]
    frames_here = rows_here // POS
    me, size = lax.axis_index("mp"), lax.axis_size("mp")
    frame_ids = lax.dynamic_slice_in_dim(action_ids.reshape(-1), me * frames_here, frames_here)
    one_hot = (
        frame_ids[:, None] == lax.broadcasted_iota(jnp.int32, (frames_here, ACTIONS), 1)
    ).astype(F32)
    per_frame = jnp.dot(one_hot, action_table, precision=lax.Precision.HIGHEST)
    embedded = jnp.broadcast_to(per_frame[:, None, :], (frames_here, POS, D)).reshape(rows_here, D)

    row = jnp.arange(BLOCK)
    frame_of = ((row // GROUP // frames_here) ^ me) * frames_here + row // GROUP % frames_here
    allowed = (
        (row[:, None] % GROUP == row[None] % GROUP)
        & (frame_of[None] <= frame_of[:, None])
        & (frame_of[None] < clip_lengths[0])
    )
    mask = jnp.where(allowed, 0.0, -1e9).astype(F32)

    spatial = gather_attention(attention_pieces(spatial_qkv, spatial_out))
    pieces, _ = lax.optimization_barrier(
        (attention_pieces(temporal_qkv, temporal_out), spatial[size - 1][0])
    )
    temporal = gather_attention(pieces)
    ff_pieces, _ = lax.optimization_barrier(
        ((own_half(ff_in, 1), own_half(ff_out, 0)), temporal[size - 1][0])
    )
    ff_ins, ff_outs = gather(ff_pieces[0], False), gather(ff_pieces[1], True)
    grad_result = to_positions(out_grad)

    first = tokens.astype(F32) + embedded
    normed_a, scaled_a, inverse_a = norm_rows(first, norm_gains[0], norm_shifts[0])
    normed_a = normed_a.astype(BF16)
    second = first
    kept_a = []
    for slot in range(size):
        second, *kept = attend_slot(normed_a, spatial[slot], second, None)
        kept_a.append(kept)
    second = to_positions(second.astype(BF16)).astype(F32)
    normed_b, scaled_b, inverse_b = norm_rows(second, norm_gains[1], norm_shifts[1])
    normed_b = normed_b.astype(BF16)
    third = second
    kept_b = []
    for slot in range(size):
        third, *kept = attend_slot(normed_b, temporal[slot], third, mask)
        kept_b.append(kept)
    normed_c, scaled_c, inverse_c = norm_rows(third, norm_gains[2], norm_shifts[2])
    normed_c = normed_c.astype(BF16)

    result = third
    grad_normed = jnp.zeros((rows_here, D), F32)
    ff_in_slots, ff_out_slots = [], []
    for slot in range(size):
        ins, outs = [], []
        mine = (ff_ins[slot], ff_outs[slot])
        for w_in, w_out in (mine, tuple(twin(x) for x in mine)):
            pre_act = nn(normed_c, w_in)
            hidden, pull = jax.vjp(jax.nn.gelu, pre_act)
            hidden = hidden.astype(BF16)
            result = result + nn(hidden, w_out)
            grad_pre = pull(nt(grad_result, w_out))[0].astype(BF16)
            outs.append(tn(hidden, grad_result).astype(BF16))
            ins.append(tn(normed_c, grad_pre).astype(BF16))
            grad_normed = grad_normed + nt(grad_pre, w_in)
        ff_in_slots.append(ins)
        ff_out_slots.append(outs)
    mixed = to_frames(result.astype(BF16))
    sum_in, sum_out = over_clips((reduce_slots(ff_in_slots, False), reduce_slots(ff_out_slots, True)))
    grad_ff_in, grad_ff_out = both_halves(sum_in, 1), both_halves(sum_out, 0)

    grad_in, gain_c, shift_c = norm_back(grad_normed, scaled_c, inverse_c, norm_gains[2])
    grad_third = grad_result.astype(F32) + grad_in
    grad_sent = grad_third.astype(BF16)
    grad_normed = jnp.zeros((rows_here, D), F32)
    slots = [None] * size
    for slot in reversed(range(size)):
        grad_normed, slots[slot] = back_slot(
            normed_b, grad_sent, kept_b[slot], temporal[slot], grad_normed, mask
        )
    grad_tqkv, grad_tout = attention_grads(slots)
    grad_in, gain_b, shift_b = norm_back(grad_normed, scaled_b, inverse_b, norm_gains[1])
    grad_second = to_frames((grad_third + grad_in).astype(BF16))
    grad_normed = jnp.zeros((rows_here, D), F32)
    slots = [None] * size
    for slot in reversed(range(size)):
        grad_normed, slots[slot] = back_slot(
            normed_a, grad_second, kept_a[slot], spatial[slot], grad_normed, None
        )
    grad_sqkv, grad_sout = attention_grads(slots)
    grad_in, gain_a, shift_a = norm_back(grad_normed, scaled_a, inverse_a, norm_gains[0])
    grad_first = grad_second.astype(F32) + grad_in
    frame_grads = jnp.sum(grad_first.reshape(frames_here, POS, -1), axis=1)
    grad_table = jnp.dot(one_hot.T, frame_grads, precision=lax.Precision.HIGHEST)
    gains_sum, shifts_sum, table_sum = lax.psum(
        (jnp.stack([gain_a, gain_b, gain_c]), jnp.stack([shift_a, shift_b, shift_c]), grad_table),
        ("dp", "mp"),
    )
    return (
        mixed,
        grad_first,
        table_sum,
        gains_sum,
        shifts_sum,
        grad_sqkv,
        grad_sout,
        grad_tqkv,
        grad_tout,
        grad_ff_in,
        grad_ff_out,
    )


def solution(mesh):
    return jax.shard_map(
        shards,
        mesh=mesh,
        in_specs=(
            P(("dp", "mp"), None),
            P("dp", None),
            P("dp"),
            P(),
            P(),
            P(),
            P(None, None, "mp"),
            P("mp", None),
            P(None, None, "mp"),
            P("mp", None),
            P(None, "mp"),
            P("mp", None),
            P(("dp", "mp"), None),
        ),
        out_specs=(
            P(("dp", "mp"), None),
            P(("dp", "mp"), None),
            P(),
            P(),
            P(),
            P(None, None, "mp"),
            P("mp", None),
            P(None, None, "mp"),
            P("mp", None),
            P(None, "mp"),
            P("mp", None),
        ),
        check_vma=False,
    )
```

```python
import functools

import jax
import jax.numpy as jnp
from jax import lax
from jax.experimental import pallas as pl
from jax.experimental.pallas import tpu as pltpu
from jax.sharding import PartitionSpec as P

D = 1024
HEAD_DIM = 64
FRAMES = 16
POS = 256
ACTIONS = 8
EPS = 1e-05
BLOCK = 256
GROUP = BLOCK // FRAMES
VMEM = 60 << 20
COST = 1
BF16 = jnp.bfloat16
F32 = jnp.float32


def norm_rows(hidden, gain_row, shift_row):
    average = jnp.mean(hidden, axis=-1, keepdims=True)
    centred = hidden - average
    inverse = lax.rsqrt(jnp.mean(centred * centred, axis=-1, keepdims=True) + EPS)
    scaled = centred * inverse
    return scaled * gain_row + shift_row, scaled, inverse


def norm_back(gradient, scaled, inverse, gain_row):
    grad_gain = jnp.sum(gradient * scaled, axis=0)
    grad_shift = jnp.sum(gradient, axis=0)
    inner = gradient * gain_row
    grad_in = inverse * (
        inner
        - jnp.mean(inner, axis=-1, keepdims=True)
        - scaled * jnp.mean(inner * scaled, axis=-1, keepdims=True)
    )
    return grad_in, grad_gain, grad_shift


def flip(values, offset, axis="mp"):
    size = lax.axis_size(axis)
    return lax.ppermute(values, axis, [(i, i ^ offset) for i in range(size)])


def twin(values):
    return flip(values, 1, "dp")


def bits_of(count, reverse):
    bits = [1 << b for b in range(count.bit_length() - 1)]
    return bits[::-1] if reverse else bits


def gather(piece, reverse, axis="mp", unit=1):
    slots = {0: piece}
    for bit in bits_of(lax.axis_size(axis) // unit, reverse):
        for slot in list(slots):
            slots[slot | bit] = flip(slots[slot], bit * unit, axis)
    return [slots[s] for s in range(len(slots))]


def add(left, right):
    return (left.astype(F32) + right.astype(F32)).astype(BF16)


def scatter_step(slots, bit, axis="mp", unit=1):
    return {
        s: add(value, flip(slots[s | bit], bit * unit, axis)) for s, value in slots.items() if not s & bit
    }


def scatter(slots, reverse, axis="mp", unit=1):
    slots = dict(slots)
    for bit in bits_of(lax.axis_size(axis) // unit, reverse):
        slots = scatter_step(slots, bit, axis, unit)
    return slots[0]


def over_clips(values):
    me, size = lax.axis_index("dp") // 2, lax.axis_size("dp") // 2
    flat = values.reshape(-1, D)
    rows = flat.shape[0] // size
    own = {s: lax.dynamic_slice_in_dim(flat, (me ^ s) * rows, rows) for s in range(size)}
    parts = gather(scatter(own, True, "dp", 2), False, "dp", 2)
    whole = jnp.zeros_like(flat)
    for s, part in enumerate(parts):
        whole = lax.dynamic_update_slice_in_dim(whole, part, (me ^ s) * rows, 0)
    return whole.reshape(values.shape)


def over_all(values):
    for axis in ("dp", "mp"):
        for bit in bits_of(lax.axis_size(axis), False):
            values = values + flip(values, bit, axis)
    return values


def send_positions(rows):
    me, size = lax.axis_index("mp"), lax.axis_size("mp")
    here = POS // size
    view = rows.reshape(rows.shape[0] // POS, POS, D)
    parts = []
    for slot in range(size):
        part = lax.dynamic_slice_in_dim(view, (me ^ slot) * here, here, axis=1)
        parts.append(flip(part, slot) if slot else part)
    return parts


def join_positions(parts):
    here = parts[0].shape[1]
    whole = jnp.concatenate(parts, axis=0).reshape(FRAMES, here // GROUP, GROUP, D)
    return whole.transpose(1, 0, 2, 3).reshape(FRAMES * here, D)


def to_frames(rows):
    me, size = lax.axis_index("mp"), lax.axis_size("mp")
    frames_here = rows.shape[0] // POS
    here = POS // size
    view = rows.reshape(here // GROUP, size, frames_here, GROUP, D)
    whole = jnp.zeros((frames_here, POS, D), rows.dtype)
    for slot in range(size):
        part = view[:, slot]
        part = flip(part, slot) if slot else part
        part = part.transpose(1, 0, 2, 3).reshape(frames_here, here, D)
        whole = lax.dynamic_update_slice_in_dim(whole, part, (me ^ slot) * here, axis=1)
    return whole.reshape(rows.shape)


def nn(left, right):
    return lax.dot_general(left, right, (((1,), (0,)), ((), ())), preferred_element_type=F32)


def nt(left, right):
    return lax.dot_general(left, right, (((1,), (1,)), ((), ())), preferred_element_type=F32)


def tn(left, right):
    return lax.dot_general(left, right, (((0,), (0,)), ((), ())), preferred_element_type=F32)


def flatten(slots):
    return jax.tree.leaves(slots), jax.tree.map(lambda x: 0, slots)


def whole_spec(array):
    return pl.BlockSpec(array.shape, lambda i: (0,) * array.ndim, pipeline_mode=pl.Buffered(1))


def rows_spec(width):
    return pl.BlockSpec((BLOCK, width), lambda i: (i, 0))


def columns_spec(height):
    return pl.BlockSpec((height, BLOCK), lambda i: (0, i))


def rows_of(refs):
    return [ref.at[i] for ref in refs for i in range(ref.shape[0])]


def load_weights(slots, qkv, out):
    part = slots[0][0][0].shape[1]
    width = 2 * part

    @pl.when(pl.program_id(0) == 0)
    def _():
        for index, parts in enumerate(slots):
            for half, refs in enumerate(parts):
                *three, o = rows_of(refs)
                for which, ref in enumerate(three):
                    at = 3 * width * index + width * which + part * half
                    qkv[at : at + part, :] = ref[...]
                at = width * index + part * half
                out[at : at + part, :] = o[...]


def take(refs, shapes):
    return jax.tree.map(lambda _: refs.pop(0), shapes)


def heads_apart(rows):
    owner = lax.broadcasted_iota(jnp.int32, rows.shape, 0) // HEAD_DIM
    return jnp.concatenate(
        [jnp.where(owner == h, rows, 0).astype(BF16) for h in range(rows.shape[0] // HEAD_DIM)], axis=1
    )


def attend_kernel(masked, shapes, *refs):
    refs = list(refs)
    mask = refs.pop(0) if masked else None
    n_ref = refs.pop(0)
    slots, count = take(refs, shapes), len(shapes)
    acc_ref, out_ref, qkv_ref, ctx_ref, lse_ref, w_qkv, w_out = refs
    load_weights(slots, w_qkv, w_out)
    width = w_out.shape[0] // count
    heads = width // HEAD_DIM
    together = min(4, heads)
    group = together * HEAD_DIM
    for slot in range(count):
        base = 3 * width * slot
        qkv = nt(w_qkv[base : base + 3 * width, :], n_ref[...])
        qkv_ref[base : base + width, :] = (qkv[:width] * HEAD_DIM**-0.5).astype(BF16)
        qkv_ref[base + width : base + 3 * width, :] = qkv[width:].astype(BF16)
        keys = qkv[width : 2 * width].T.astype(BF16)
        for at in range(0, width, group):
            q = heads_apart(qkv_ref[base + at : base + at + group, :])
            logits = nn(keys[:, at : at + group], q)
            if masked:
                logits = logits + jnp.concatenate([mask[...]] * together, axis=1)
            highest = jnp.max(logits, axis=0, keepdims=True)
            raised = jnp.exp(logits - highest)
            total = jnp.sum(raised, axis=0, keepdims=True)
            log_total = highest + jnp.log(total)
            inverse = 1.0 / total
            raised = raised.astype(BF16)
            for head in range(together):
                columns = slice(head * BLOCK, (head + 1) * BLOCK)
                row = slot * heads + at // HEAD_DIM + head
                lse_ref[row : row + 1, :] = log_total[:, columns]
                start = base + 2 * width + at + head * HEAD_DIM
                values = qkv_ref[start : start + HEAD_DIM, :]
                start = slot * width + at + head * HEAD_DIM
                ctx_ref[start : start + HEAD_DIM, :] = (
                    nn(values, raised[:, columns]) * inverse[:, columns]
                ).astype(BF16)
    out_ref[...] = acc_ref[...] + tn(ctx_ref[...], w_out[...])


def attend_slots(normed, slots, acc, mask):
    rows = normed.shape[0]
    flat, shapes = flatten(slots)
    width = len(slots) * 2 * flat[0].shape[1]
    lse_rows = -(-width // HEAD_DIM // 8) * 8
    first = [] if mask is None else [mask]
    args = first + [normed] + flat + [acc]
    return pl.pallas_call(
        functools.partial(attend_kernel, mask is not None, shapes),
        grid=(rows // BLOCK,),
        in_specs=[whole_spec(x) for x in first]
        + [rows_spec(D)]
        + [whole_spec(x) for x in flat]
        + [rows_spec(D)],
        out_specs=[rows_spec(D), columns_spec(3 * width), columns_spec(width), columns_spec(lse_rows)],
        out_shape=[
            jax.ShapeDtypeStruct((rows, D), F32),
            jax.ShapeDtypeStruct((3 * width, rows), BF16),
            jax.ShapeDtypeStruct((width, rows), BF16),
            jax.ShapeDtypeStruct((lse_rows, rows), F32),
        ],
        scratch_shapes=[pltpu.VMEM((3 * width, D), BF16), pltpu.VMEM((width, D), BF16)],
        compiler_params=pltpu.CompilerParams(vmem_limit_bytes=VMEM),
        cost_estimate=pl.CostEstimate(
            flops=2 * rows * D * width * 4 // COST, bytes_accessed=1 << 20, transcendentals=0
        ),
        name="attend",
    )(*args)


def back_kernel(masked, shapes, steps, *refs):
    refs = list(refs)
    mask = refs.pop(0) if masked else None
    n_ref, g_ref, qkv_ref, ctx_ref, lse_ref = (refs.pop(0) for _ in range(5))
    slots, count = take(refs, shapes), len(shapes)
    acc_ref, out_ref = refs.pop(0), refs.pop(0)
    grads = take(refs, shapes)
    w_qkv, w_out, d_all = refs
    load_weights(slots, w_qkv, w_out)
    width = w_out.shape[0] // count
    heads = width // HEAD_DIM
    step = pl.program_id(0)
    rows = pl.ds(pl.multiple_of(step * BLOCK, BLOCK), BLOCK)
    together = min(4, heads)
    group = together * HEAD_DIM
    for slot in range(count):
        base = 3 * width * slot
        d_ctx = nt(w_out[slot * width : (slot + 1) * width, :], g_ref[rows, :]).astype(BF16)
        keys = qkv_ref[base + width : base + 2 * width, :].T
        values = qkv_ref[base + 2 * width : base + 3 * width, :].T
        for at in range(0, width, group):
            q = qkv_ref[base + at : base + at + group, :]
            d_group = d_ctx[at : at + group]
            logits = nn(keys[:, at : at + group], heads_apart(q))
            if masked:
                logits = logits + jnp.concatenate([mask[...]] * together, axis=1)
            d_p = nn(values[:, at : at + group], heads_apart(d_group))
            ctx = ctx_ref[slot * width + at : slot * width + at + group, rows]
            product = d_group.astype(F32) * ctx.astype(F32)
            split = [slice(h * HEAD_DIM, (h + 1) * HEAD_DIM) for h in range(together)]
            row = slot * heads + at // HEAD_DIM
            lse = jnp.concatenate([lse_ref[row + h : row + h + 1, :] for h in range(together)], axis=1)
            total = jnp.concatenate([jnp.sum(product[s], axis=0, keepdims=True) for s in split], axis=1)
            p = jnp.exp(logits - lse)
            ds = (p * (d_p - total)).astype(BF16)
            p = p.astype(BF16)
            for head in range(together):
                columns = slice(head * BLOCK, (head + 1) * BLOCK)
                start = base + at + head * HEAD_DIM
                key = qkv_ref[width + start : width + start + HEAD_DIM, :]
                d_all[start : start + HEAD_DIM, rows] = (
                    nn(key, ds[:, columns]) * HEAD_DIM**-0.5
                ).astype(BF16)
                start = start + width
                d_all[start : start + HEAD_DIM, rows] = nt(q[split[head]], ds[:, columns]).astype(BF16)
                start = start + width
                d_all[start : start + HEAD_DIM, rows] = nt(
                    d_group[split[head]], p[:, columns]
                ).astype(BF16)
    out_ref[...] = acc_ref[...] + tn(d_all[:, rows], w_qkv[...])

    @pl.when(step == steps - 1)
    def _():
        part = width // 2
        for at in range(0, D, BLOCK):
            columns = slice(at, at + BLOCK)
            d_w = nn(d_all[...], n_ref[:, columns]).astype(BF16)
            d_o = nn(ctx_ref[...], g_ref[:, columns]).astype(BF16)
            for index, parts in enumerate(grads):
                for half, refs_out in enumerate(parts):
                    *three, o = rows_of(refs_out)
                    for which, ref in enumerate(three):
                        at = 3 * width * index + width * which + part * half
                        ref[:, columns] = d_w[at : at + part]
                    at = width * index + part * half
                    o[:, columns] = d_o[at : at + part]


def back_slots(normed, grad, kept, slots, acc, mask):
    rows = normed.shape[0]
    qkv, ctx, lse = kept
    width = ctx.shape[0]
    flat, shapes = flatten(slots)
    first = [] if mask is None else [mask]
    args = first + [normed, grad, qkv, ctx, lse] + flat + [acc]
    out = pl.pallas_call(
        functools.partial(back_kernel, mask is not None, shapes, rows // BLOCK),
        grid=(rows // BLOCK,),
        in_specs=[whole_spec(x) for x in first]
        + [whole_spec(normed), whole_spec(grad)]
        + [columns_spec(3 * width), whole_spec(ctx), columns_spec(lse.shape[0])]
        + [whole_spec(x) for x in flat]
        + [rows_spec(D)],
        out_specs=[rows_spec(D)] + [whole_spec(x) for x in flat],
        out_shape=[jax.ShapeDtypeStruct((rows, D), F32)]
        + [jax.ShapeDtypeStruct(x.shape, BF16) for x in flat],
        scratch_shapes=[
            pltpu.VMEM((3 * width, D), BF16),
            pltpu.VMEM((width, D), BF16),
            pltpu.VMEM((3 * width, rows), BF16),
        ],
        compiler_params=pltpu.CompilerParams(vmem_limit_bytes=VMEM),
        cost_estimate=pl.CostEstimate(
            flops=4 * rows * D * width * 4 // COST, bytes_accessed=1 << 20, transcendentals=0
        ),
        name="attend_back",
    )(*args)
    return out[0], take(list(out[1:]), shapes)


def gelu_both(u):
    c, cube = (2.0 / 3.141592653589793) ** 0.5, 0.044715
    square = u * u
    t = jnp.tanh(c * u * (1.0 + cube * square))
    half = 0.5 * (1.0 + t)
    return u * half, half + 0.5 * u * (1.0 - t * t) * (c + 3.0 * c * cube * square)


def ff_kernel(shapes, steps, *refs):
    refs = list(refs)
    n_ref, g_ref = refs.pop(0), refs.pop(0)
    pieces = [rows_of(x) for x in take(refs, shapes)]
    mix_ref, dn_ref, mix_out, dn_out = (refs.pop(0) for _ in range(4))
    grads = [rows_of(x) for x in take(refs, shapes)]
    hid_all, du_all = refs
    part = hid_all.shape[0] // 2
    step = pl.program_id(0)
    rows = pl.ds(pl.multiple_of(step * BLOCK, BLOCK), BLOCK)
    mix, dn = mix_ref[...], dn_ref[...]
    for index, (w_in, w_out) in enumerate(pieces):
        low = slice(index * part, (index + 1) * part)
        value, slope = gelu_both(nt(w_in[...], n_ref[rows, :]))
        hidden = value.astype(BF16)
        du = (slope * nt(w_out[...], g_ref[rows, :])).astype(BF16)
        hid_all[low, rows] = hidden
        du_all[low, rows] = du
        mix = mix + tn(hidden, w_out[...])
        dn = dn + tn(du, w_in[...])
    mix_out[...] = mix
    dn_out[...] = dn

    @pl.when(step == steps - 1)
    def _():
        for at in range(0, D, BLOCK):
            columns = slice(at, at + BLOCK)
            for index, (d_in, d_out) in enumerate(grads):
                low = slice(index * part, (index + 1) * part)
                d_in[:, columns] = nn(du_all[low, :], n_ref[:, columns]).astype(BF16)
                d_out[:, columns] = nn(hid_all[low, :], g_ref[:, columns]).astype(BF16)


def ff_slot(normed, grad, pieces, mix, dn):
    rows = normed.shape[0]
    flat, shapes = flatten(pieces)
    width = 2 * flat[0].shape[1]
    out = pl.pallas_call(
        functools.partial(ff_kernel, shapes, rows // BLOCK),
        grid=(rows // BLOCK,),
        in_specs=[whole_spec(normed), whole_spec(grad)]
        + [whole_spec(x) for x in flat]
        + [rows_spec(D), rows_spec(D)],
        out_specs=[rows_spec(D), rows_spec(D)] + [whole_spec(x) for x in flat],
        out_shape=[jax.ShapeDtypeStruct((rows, D), F32)] * 2
        + [jax.ShapeDtypeStruct(x.shape, BF16) for x in flat],
        scratch_shapes=[pltpu.VMEM((width, rows), BF16), pltpu.VMEM((width, rows), BF16)],
        compiler_params=pltpu.CompilerParams(vmem_limit_bytes=VMEM),
        cost_estimate=pl.CostEstimate(
            flops=12 * rows * D * width // COST, bytes_accessed=1 << 20, transcendentals=0
        ),
        name="feed_forward",
    )(normed, grad, *flat, mix, dn)
    return out[0], out[1], take(list(out[2:]), shapes)


def after(values, first):
    return lax.optimization_barrier((values, first))[0]


def hold(values, flights):
    return lax.optimization_barrier((values, flights))


def halves_of(array, axis):
    half = array.shape[axis] // 2
    core = lax.axis_index("dp") % 2
    return [
        lax.dynamic_slice_in_dim(array, at * half, half, axis=axis) for at in (core, 1 - core)
    ]


def attention_pieces(weight_qkv, weight_out):
    qkv = weight_qkv.transpose(0, 2, 1)
    whole = jnp.concatenate([qkv, weight_out[None]], axis=0)
    return halves_of(whole, 1)


def ff_pieces(weight_in, weight_out):
    return halves_of(jnp.stack([weight_in.T, weight_out]), 1)


def low_high(piece):
    half = piece.shape[0] // 2
    return [piece[:half], piece[half:]]


def near(piece):
    if lax.axis_size("mp") == 4:
        return {1: [flip(piece, 1)], 2: [flip(piece, 2)]}
    return {}


def far(piece, slots):
    size = lax.axis_size("mp")
    if size == 4:
        return {3: [flip(low_high(slots[1][0])[0], 2), flip(low_high(slots[2][0])[1], 1)]}
    low, high = low_high(piece)
    return {s: [x, y] for s, (x, y) in enumerate(zip(gather(low, False), gather(high, True))) if s}


def twins(arrays):
    return [twin(x) for x in arrays]


def pair_sums(grads, received):
    return [add(x, y) for x, y in zip(both_routes(grads[0]), both_routes(received))]


def both_routes(arrays):
    return arrays if len(arrays) == 2 else low_high(arrays[0])


def send_far(sums):
    if lax.axis_size("mp") != 4:
        return []
    return [flip(sums[3][0], 1), flip(sums[3][1], 2)]


def send_plain(sums):
    if lax.axis_size("mp") != 4:
        return []
    return [flip(sums[1][0], 1), flip(sums[2][1], 2)]


def send_rest(sums, far_sums):
    if lax.axis_size("mp") != 4:
        return []
    low_two, high_one = far_sums
    return [flip(add(sums[1][1], high_one), 1), flip(add(sums[2][0], low_two), 2)]


def settle(sums, plain, rest):
    if lax.axis_size("mp") != 4:
        return [scatter({s: x[i] for s, x in sums.items()}, bool(i)) for i in range(2)]
    terms = [(sums[0][0], plain[0], rest[1]), (sums[0][1], plain[1], rest[0])]
    return [sum(x.astype(F32) for x in three).astype(BF16) for three in terms]


def both_halves(mine):
    other = twin(mine)
    first = lax.axis_index("dp") % 2 == 0
    return jnp.concatenate(
        [jnp.where(first, mine, other), jnp.where(first, other, mine)], axis=1
    ).astype(F32)


def attention_grads(whole):
    return whole[:3].transpose(0, 2, 1), whole[3]


def shards(
    tokens,
    action_ids,
    clip_lengths,
    action_table,
    norm_gains,
    norm_shifts,
    spatial_qkv,
    spatial_out,
    temporal_qkv,
    temporal_out,
    ff_in,
    ff_out,
    out_grad,
):
    rows_here = tokens.shape[0]
    frames_here = rows_here // POS
    me, size = lax.axis_index("mp"), lax.axis_size("mp")
    frame_ids = lax.dynamic_slice_in_dim(action_ids.reshape(-1), me * frames_here, frames_here)
    one_hot = (
        frame_ids[:, None] == lax.broadcasted_iota(jnp.int32, (frames_here, ACTIONS), 1)
    ).astype(F32)
    per_frame = jnp.dot(one_hot, action_table, precision=lax.Precision.HIGHEST)
    embedded = jnp.broadcast_to(per_frame[:, None, :], (frames_here, POS, D)).reshape(rows_here, D)

    row = jnp.arange(BLOCK)
    frame_of = ((row // GROUP // frames_here) ^ me) * frames_here + row // GROUP % frames_here
    allowed = (
        (row[:, None] % GROUP == row[None] % GROUP)
        & (frame_of[:, None] <= frame_of[None])
        & (frame_of[:, None] < clip_lengths[0])
    )
    mask = jnp.where(allowed, 0.0, -1e9).astype(F32)

    others = [[1, 2], [3]] if size == 4 else [list(range(1, size))]

    own, other = attention_pieces(spatial_qkv, spatial_out)
    close = near(own)
    first = tokens.astype(F32) + embedded
    normed_a, scaled_a, inverse_a = norm_rows(first, norm_gains[0], norm_shifts[0])
    normed_a = normed_a.astype(BF16)
    spatial = {0: [[own], [other]]}
    kept_a = {}
    second, *kept_a[0] = attend_slots(normed_a, [spatial[0]], first, None)
    (second, kept_a[0]), close = hold((second, kept_a[0]), close)
    distant = far(own, close)
    close = {s: [x, twins(x)] for s, x in close.items()}
    second, close = hold(second, close)
    if close:
        spatial |= close
        second, *kept_a[1] = attend_slots(normed_a, [spatial[s] for s in others[0]], second, None)
    second, distant = hold(second, distant)
    own, other = attention_pieces(*after((temporal_qkv, temporal_out), distant))
    distant = {s: [x, twins(x)] for s, x in distant.items()}
    close = near(own)
    second, distant = hold(second, distant)
    spatial |= distant
    second, *kept_a[3] = attend_slots(normed_a, [spatial[s] for s in others[-1]], second, None)

    second = join_positions(send_positions(second.astype(BF16))).astype(F32)
    normed_b, scaled_b, inverse_b = norm_rows(second, norm_gains[1], norm_shifts[1])
    normed_b = normed_b.astype(BF16)
    (second, normed_b), close = hold((second, normed_b), close)
    distant = far(own, close)
    close = {s: [x, twins(x)] for s, x in close.items()}
    temporal = {0: [[own], [other]]}
    kept_b = {}
    third, *kept_b[0] = attend_slots(normed_b, [temporal[0]], second, mask)
    third, (close, distant) = hold(third, (close, distant))
    grad_parts = send_positions(after(out_grad, third))
    distant = {s: [x, twins(x)] for s, x in distant.items()}
    if close:
        temporal |= close
        third, *kept_b[1] = attend_slots(normed_b, [temporal[s] for s in others[0]], third, mask)
    third, (distant, grad_parts) = hold(third, (distant, grad_parts))
    own, other = ff_pieces(*after((ff_in, ff_out), distant))
    close = near(own)
    temporal |= distant
    third, *kept_b[3] = attend_slots(normed_b, [temporal[s] for s in others[-1]], third, mask)

    grad_result = join_positions(grad_parts)
    normed_c, scaled_c, inverse_c = norm_rows(third, norm_gains[2], norm_shifts[2])
    normed_c = normed_c.astype(BF16)
    result, grad_normed = third, jnp.zeros((rows_here, D), F32)
    grads = {}

    def feed(slot, pieces, flights):
        nonlocal result, grad_normed
        result, grad_normed, grads[slot] = ff_slot(normed_c, grad_result, pieces, result, grad_normed)
        (result, grad_normed, grads[slot]), flights = hold((result, grad_normed, grads[slot]), flights)
        return flights

    def swap(slots):
        return {s: twins(grads[s][1]) for s in slots}

    received = {}
    if size == 4:
        close = feed(0, [[own], [other]], close)
        distant = far(own, close)
        twin_one, twin_two = twins(close[1]), twins(close[2])
        result, twin_one = hold(result, twin_one)
        distant, twin_two, got = feed(1, [close[1], twin_one], (distant, twin_two, swap([0])))
        received |= got
        twin_three, got = feed(2, [close[2], twin_two], (twins(distant[3]), swap([1])))
        received |= got
        received |= feed(3, [distant[3], twin_three], swap([2]))
    else:
        distant = feed(0, [[own], [other]], far(own, close))
        for slot in range(1, size):
            feed(slot, [distant[slot], twins(distant[slot])], [])
        received = swap(range(size - 1))
    received |= swap([size - 1])
    sums_c = {s: pair_sums(grads[s], received[s]) for s in range(size)}
    grad_in, gain_c, shift_c = norm_back(grad_normed, scaled_c, inverse_c, norm_gains[2])
    grad_third = grad_result.astype(F32) + grad_in
    grad_sent = grad_third.astype(BF16)

    def back(normed, gradient, kept, slots, mask, flights):
        grads, received, total = {}, {}, jnp.zeros((rows_here, D), F32)
        total, sums = hold(total, flights[0])
        steps = others + [[0]]
        for at, group in enumerate(steps):
            sent = flights[1][at]() if size == 4 else []
            swapped = {s: twins(grads[s][1]) for s in (steps[at - 1] if at else [])}
            key = 0 if group == [0] else 3 if group == others[-1] else 1
            total, found = back_slots(normed, gradient, kept[key], [slots[s] for s in group], total, mask)
            grads |= dict(zip(group, found))
            (total, grads), (sent, swapped) = hold((total, grads), (sent, swapped))
            received |= swapped
            if size == 4:
                flights[2].append(sent)
        received |= {0: twins(grads[0][1])}
        return total, {s: pair_sums(grads[s], received[s]) for s in range(size)}

    got = []
    plans = [lambda: send_far(sums_c), lambda: send_plain(sums_c), lambda: []]
    grad_normed, sums_b = back(normed_b, grad_sent, kept_b, temporal, mask, (sums_c, plans, got))
    far_c, plain_c = got[:2] if got else ([], [])
    grad_in, gain_b, shift_b = norm_back(grad_normed, scaled_b, inverse_b, norm_gains[1])
    grad_second = to_frames((grad_third + grad_in).astype(BF16))

    got = []
    plans = [
        lambda: send_rest(sums_c, far_c),
        lambda: send_far(sums_b),
        lambda: send_plain(sums_b),
    ]
    grad_normed, sums_a = back(normed_a, grad_second, kept_a, spatial, None, (sums_b, plans, got))
    rest_c, far_b, plain_b = got if got else ([], [], [])
    sum_c = settle(sums_c, plain_c, rest_c)
    size_dp = lax.axis_size("dp")
    sum_c = lax.psum(sum_c, "dp", axis_index_groups=[list(range(c, size_dp, 2)) for c in range(2)])
    rest_b = send_rest(sums_b, far_b)
    far_a = send_far(sums_a)
    sum_b = settle(sums_b, plain_b, rest_b)
    whole_b = over_clips(jnp.concatenate(sum_b, axis=0))
    plain_a = send_plain(after(sums_a, rest_b))
    rest_a = send_rest(sums_a, far_a)
    sum_a = settle(sums_a, plain_a, rest_a)
    whole_a = over_clips(jnp.concatenate(sum_a, axis=0))
    mixed = to_frames(after(result.astype(BF16), rest_a))

    whole = both_halves(jnp.concatenate(sum_c, axis=0))
    grad_ff_in, grad_ff_out = whole[0].T, whole[1]
    grad_tqkv, grad_tout = attention_grads(both_halves(whole_b))
    grad_sqkv, grad_sout = attention_grads(both_halves(whole_a))

    grad_in, gain_a, shift_a = norm_back(grad_normed, scaled_a, inverse_a, norm_gains[0])
    grad_first = grad_second.astype(F32) + grad_in
    frame_grads = jnp.sum(grad_first.reshape(frames_here, POS, -1), axis=1)
    grad_table = jnp.dot(one_hot.T, frame_grads, precision=lax.Precision.HIGHEST)
    small = over_all(
        jnp.concatenate(
            [jnp.stack([gain_a, gain_b, gain_c, shift_a, shift_b, shift_c]), grad_table], axis=0
        )
    )
    gains_sum, shifts_sum, table_sum = small[:3], small[3:6], small[6:]
    return (
        mixed,
        grad_first,
        table_sum,
        gains_sum,
        shifts_sum,
        grad_sqkv,
        grad_sout,
        grad_tqkv,
        grad_tout,
        grad_ff_in,
        grad_ff_out,
    )


def solution(mesh):
    return jax.shard_map(
        shards,
        mesh=mesh,
        in_specs=(
            P(("dp", "mp"), None),
            P("dp", None),
            P("dp"),
            P(),
            P(),
            P(),
            P(None, None, "mp"),
            P("mp", None),
            P(None, None, "mp"),
            P("mp", None),
            P(None, "mp"),
            P("mp", None),
            P(("dp", "mp"), None),
        ),
        out_specs=(
            P(("dp", "mp"), None),
            P(("dp", "mp"), None),
            P(),
            P(),
            P(),
            P(None, None, "mp"),
            P("mp", None),
            P(None, None, "mp"),
            P("mp", None),
            P(None, "mp"),
            P("mp", None),
        ),
        check_vma=False,
    )
```

```python
import functools

import jax
import jax.numpy as jnp
from jax import lax
from jax.experimental import pallas as pl
from jax.experimental.pallas import tpu as pltpu
from jax.sharding import PartitionSpec as P

D = 1024
HEAD_DIM = 64
FRAMES = 16
POS = 256
ACTIONS = 8
EPS = 1e-05
BLOCK = 256
GROUP = BLOCK // FRAMES
VMEM = 60 << 20
COST = 1
LSE_ROWS = 8
BF16 = jnp.bfloat16
F32 = jnp.float32


def norm_rows(hidden, gain_row, shift_row):
    average = jnp.mean(hidden, axis=-1, keepdims=True)
    centred = hidden - average
    inverse = lax.rsqrt(jnp.mean(centred * centred, axis=-1, keepdims=True) + EPS)
    scaled = centred * inverse
    return scaled * gain_row + shift_row, scaled, inverse


def norm_back(gradient, scaled, inverse, gain_row):
    grad_gain = jnp.sum(gradient * scaled, axis=0)
    grad_shift = jnp.sum(gradient, axis=0)
    inner = gradient * gain_row
    grad_in = inverse * (
        inner
        - jnp.mean(inner, axis=-1, keepdims=True)
        - scaled * jnp.mean(inner * scaled, axis=-1, keepdims=True)
    )
    return grad_in, grad_gain, grad_shift


def flip(values, offset, axis="mp"):
    size = lax.axis_size(axis)
    return lax.ppermute(values, axis, [(i, i ^ offset) for i in range(size)])


def twin(values):
    return flip(values, 1, "dp")


def bits_of(count, reverse):
    bits = [1 << b for b in range(count.bit_length() - 1)]
    return bits[::-1] if reverse else bits


def gather(piece, reverse, axis="mp", unit=1):
    slots = {0: piece}
    for bit in bits_of(lax.axis_size(axis) // unit, reverse):
        for slot in list(slots):
            slots[slot | bit] = flip(slots[slot], bit * unit, axis)
    return [slots[s] for s in range(len(slots))]


def add(left, right):
    return (left.astype(F32) + right.astype(F32)).astype(BF16)


def scatter_step(slots, bit, axis="mp", unit=1):
    return {
        s: add(value, flip(slots[s | bit], bit * unit, axis)) for s, value in slots.items() if not s & bit
    }


def scatter(slots, reverse, axis="mp", unit=1):
    slots = dict(slots)
    for bit in bits_of(lax.axis_size(axis) // unit, reverse):
        slots = scatter_step(slots, bit, axis, unit)
    return slots[0]


def clip_offsets():
    return [bit * 2 for bit in bits_of(lax.axis_size("dp") // 2, False)]


def even_clips():
    return lax.axis_index("dp") // 2 % 2 == 0


def clips_first(low, high):
    even = even_clips()
    return jnp.where(even, low, high), flip(jnp.where(even, high, low), clip_offsets()[0], "dp")


def clips_next(mine, arrived):
    mine = add(mine, arrived)
    offsets = clip_offsets()[1:]
    for offset in offsets[:-1]:
        mine = add(mine, flip(mine, offset, "dp"))
    return mine, flip(mine, offsets[-1], "dp")


def clips_last(mine, arrived):
    mine = add(mine, arrived)
    return mine, flip(mine, clip_offsets()[0], "dp")


def clips_joined(mine, other):
    even = even_clips()
    return jnp.concatenate([jnp.where(even, mine, other), jnp.where(even, other, mine)], axis=0)


def over_all(values):
    for axis in ("dp", "mp"):
        for bit in bits_of(lax.axis_size(axis), False):
            values = values + flip(values, bit, axis)
    return values


def send_positions(rows):
    me, size = lax.axis_index("mp"), lax.axis_size("mp")
    here = POS // size
    view = rows.reshape(rows.shape[0] // POS, POS, D)
    parts = []
    for slot in range(size):
        part = lax.dynamic_slice_in_dim(view, (me ^ slot) * here, here, axis=1)
        parts.append(flip(part, slot) if slot else part)
    return parts


def join_positions(parts):
    here = parts[0].shape[1]
    whole = jnp.concatenate(parts, axis=0).reshape(FRAMES, here // GROUP, GROUP, D)
    return whole.transpose(1, 0, 2, 3).reshape(FRAMES * here, D)


def to_frames(rows):
    me, size = lax.axis_index("mp"), lax.axis_size("mp")
    frames_here = rows.shape[0] // POS
    here = POS // size
    view = rows.reshape(here // GROUP, size, frames_here, GROUP, D)
    whole = jnp.zeros((frames_here, POS, D), rows.dtype)
    for slot in range(size):
        part = view[:, slot]
        part = flip(part, slot) if slot else part
        part = part.transpose(1, 0, 2, 3).reshape(frames_here, here, D)
        whole = lax.dynamic_update_slice_in_dim(whole, part, (me ^ slot) * here, axis=1)
    return whole.reshape(rows.shape)


def nn(left, right):
    return lax.dot_general(left, right, (((1,), (0,)), ((), ())), preferred_element_type=F32)


def nt(left, right):
    return lax.dot_general(left, right, (((1,), (1,)), ((), ())), preferred_element_type=F32)


def tn(left, right):
    return lax.dot_general(left, right, (((0,), (0,)), ((), ())), preferred_element_type=F32)


def flatten(slots):
    return jax.tree.leaves(slots), jax.tree.map(lambda x: 0, slots)


def whole_spec(array):
    return pl.BlockSpec(array.shape, lambda i: (0,) * array.ndim, pipeline_mode=pl.Buffered(1))


def rows_spec(width):
    return pl.BlockSpec((BLOCK, width), lambda i: (i, 0))


def columns_spec(height, index=0):
    return pl.BlockSpec((height, BLOCK), lambda i: (index, i))


def part_spec(shape, index):
    return pl.BlockSpec(shape, lambda i: (index, 0), pipeline_mode=pl.Buffered(1))


def rows_of(refs):
    return [ref.at[i] for ref in refs for i in range(ref.shape[0])]


def load_weights(slots, qkv, out):
    part = slots[0][0][0].shape[1]
    width = 2 * part

    @pl.when(pl.program_id(0) == 0)
    def _():
        for index, parts in enumerate(slots):
            for half, refs in enumerate(parts):
                *three, o = rows_of(refs)
                for which, ref in enumerate(three):
                    at = 3 * width * index + width * which + part * half
                    qkv[at : at + part, :] = ref[...]
                at = width * index + part * half
                out[at : at + part, :] = o[...]


def take(refs, shapes):
    return jax.tree.map(lambda _: refs.pop(0), shapes)


def heads_apart(rows):
    owner = lax.broadcasted_iota(jnp.int32, rows.shape, 0) // HEAD_DIM
    return jnp.concatenate(
        [jnp.where(owner == h, rows, 0).astype(BF16) for h in range(rows.shape[0] // HEAD_DIM)], axis=1
    )


def attend_kernel(masked, shapes, *refs):
    refs = list(refs)
    mask = refs.pop(0) if masked else None
    n_ref = refs.pop(0)
    slots, count = take(refs, shapes), len(shapes)
    acc_ref, out_ref, qkv_ref, ctx_ref, lse_ref, w_qkv, w_out = refs
    load_weights(slots, w_qkv, w_out)
    width = w_out.shape[0] // count
    heads = width // HEAD_DIM
    together = min(4, heads)
    group = together * HEAD_DIM
    for slot in range(count):
        base = 3 * width * slot
        qkv = nt(w_qkv[base : base + 3 * width, :], n_ref[...])
        qkv_ref[base : base + width, :] = (qkv[:width] * HEAD_DIM**-0.5).astype(BF16)
        qkv_ref[base + width : base + 3 * width, :] = qkv[width:].astype(BF16)
        keys = qkv[width : 2 * width].T.astype(BF16)
        for at in range(0, width, group):
            q = heads_apart(qkv_ref[base + at : base + at + group, :])
            logits = nn(keys[:, at : at + group], q)
            if masked:
                logits = logits + jnp.concatenate([mask[...]] * together, axis=1)
            highest = jnp.max(logits, axis=0, keepdims=True)
            raised = jnp.exp(logits - highest)
            total = jnp.sum(raised, axis=0, keepdims=True)
            log_total = highest + jnp.log(total)
            inverse = 1.0 / total
            raised = raised.astype(BF16)
            for head in range(together):
                columns = slice(head * BLOCK, (head + 1) * BLOCK)
                row = slot * LSE_ROWS + at // HEAD_DIM + head
                lse_ref[row : row + 1, :] = log_total[:, columns]
                start = base + 2 * width + at + head * HEAD_DIM
                values = qkv_ref[start : start + HEAD_DIM, :]
                start = slot * width + at + head * HEAD_DIM
                ctx_ref[start : start + HEAD_DIM, :] = (
                    nn(values, raised[:, columns]) * inverse[:, columns]
                ).astype(BF16)
    out_ref[...] = acc_ref[...] + tn(ctx_ref[...], w_out[...])


def attend_slots(normed, slots, acc, mask):
    rows = normed.shape[0]
    flat, shapes = flatten(slots)
    width = len(slots) * 2 * flat[0].shape[1]
    lse_rows = LSE_ROWS * len(slots)
    first = [] if mask is None else [mask]
    args = first + [normed] + flat + [acc]
    return pl.pallas_call(
        functools.partial(attend_kernel, mask is not None, shapes),
        grid=(rows // BLOCK,),
        in_specs=[whole_spec(x) for x in first]
        + [rows_spec(D)]
        + [whole_spec(x) for x in flat]
        + [rows_spec(D)],
        out_specs=[rows_spec(D), columns_spec(3 * width), columns_spec(width), columns_spec(lse_rows)],
        out_shape=[
            jax.ShapeDtypeStruct((rows, D), F32),
            jax.ShapeDtypeStruct((3 * width, rows), BF16),
            jax.ShapeDtypeStruct((width, rows), BF16),
            jax.ShapeDtypeStruct((lse_rows, rows), F32),
        ],
        scratch_shapes=[pltpu.VMEM((3 * width, D), BF16), pltpu.VMEM((width, D), BF16)],
        compiler_params=pltpu.CompilerParams(vmem_limit_bytes=VMEM),
        cost_estimate=pl.CostEstimate(
            flops=2 * rows * D * width * 4 // COST, bytes_accessed=1 << 20, transcendentals=0
        ),
        name="attend",
    )(*args)


def back_kernel(masked, shapes, steps, *refs):
    refs = list(refs)
    mask = refs.pop(0) if masked else None
    n_ref, g_ref, qkv_ref, ctx_ref, lse_ref = (refs.pop(0) for _ in range(5))
    slots, count = take(refs, shapes), len(shapes)
    acc_ref, out_ref = refs.pop(0), refs.pop(0)
    grads = [[refs.pop(0) for _ in range(2)] for _ in range(count)]
    w_qkv, w_out, d_all = refs
    load_weights(slots, w_qkv, w_out)
    width = w_out.shape[0] // count
    heads = width // HEAD_DIM
    step = pl.program_id(0)
    rows = pl.ds(pl.multiple_of(step * BLOCK, BLOCK), BLOCK)
    together = min(4, heads)
    group = together * HEAD_DIM
    for slot in range(count):
        base = 3 * width * slot
        d_ctx = nt(w_out[slot * width : (slot + 1) * width, :], g_ref[rows, :]).astype(BF16)
        keys = qkv_ref[base + width : base + 2 * width, :].T
        values = qkv_ref[base + 2 * width : base + 3 * width, :].T
        for at in range(0, width, group):
            q = qkv_ref[base + at : base + at + group, :]
            d_group = d_ctx[at : at + group]
            logits = nn(keys[:, at : at + group], heads_apart(q))
            if masked:
                logits = logits + jnp.concatenate([mask[...]] * together, axis=1)
            d_p = nn(values[:, at : at + group], heads_apart(d_group))
            ctx = ctx_ref[slot * width + at : slot * width + at + group, rows]
            product = d_group.astype(F32) * ctx.astype(F32)
            split = [slice(h * HEAD_DIM, (h + 1) * HEAD_DIM) for h in range(together)]
            row = slot * LSE_ROWS + at // HEAD_DIM
            lse = jnp.concatenate([lse_ref[row + h : row + h + 1, :] for h in range(together)], axis=1)
            total = jnp.concatenate([jnp.sum(product[s], axis=0, keepdims=True) for s in split], axis=1)
            p = jnp.exp(logits - lse)
            ds = (p * (d_p - total)).astype(BF16)
            p = p.astype(BF16)
            for head in range(together):
                columns = slice(head * BLOCK, (head + 1) * BLOCK)
                start = base + at + head * HEAD_DIM
                key = qkv_ref[width + start : width + start + HEAD_DIM, :]
                d_all[start : start + HEAD_DIM, rows] = (
                    nn(key, ds[:, columns]) * HEAD_DIM**-0.5
                ).astype(BF16)
                start = start + width
                d_all[start : start + HEAD_DIM, rows] = nt(q[split[head]], ds[:, columns]).astype(BF16)
                start = start + width
                d_all[start : start + HEAD_DIM, rows] = nt(
                    d_group[split[head]], p[:, columns]
                ).astype(BF16)
    out_ref[...] = acc_ref[...] + tn(d_all[:, rows], w_qkv[...])

    @pl.when(step == steps - 1)
    def _():
        part = width // 2
        for at in range(0, D, BLOCK):
            columns = slice(at, at + BLOCK)
            d_w = nn(d_all[...], n_ref[:, columns]).astype(BF16)
            d_o = nn(ctx_ref[...], g_ref[:, columns]).astype(BF16)
            for index, parts in enumerate(grads):
                for half, ref_out in enumerate(parts):
                    *three, o = rows_of([ref_out])
                    for which, ref in enumerate(three):
                        at = 3 * width * index + width * which + part * half
                        ref[:, columns] = d_w[at : at + part]
                    at = width * index + part * half
                    o[:, columns] = d_o[at : at + part]


def back_slots(normed, grad, kept, slots, acc, mask):
    rows = normed.shape[0]
    (qkv, ctx, lse), place = kept
    flat, shapes = flatten(slots)
    part = flat[0].shape[1]
    width = len(slots) * 2 * part
    grads = [jax.ShapeDtypeStruct((4, part, D), BF16)] * (2 * len(slots))
    lse_rows, index = LSE_ROWS * len(slots), place // len(slots)
    first = [] if mask is None else [mask]
    args = first + [normed, grad, qkv, ctx, lse] + flat + [acc]
    out = pl.pallas_call(
        functools.partial(back_kernel, mask is not None, shapes, rows // BLOCK),
        grid=(rows // BLOCK,),
        in_specs=[whole_spec(x) for x in first]
        + [whole_spec(normed), whole_spec(grad)]
        + [columns_spec(3 * width, index), part_spec((width, rows), index), columns_spec(lse_rows, index)]
        + [whole_spec(x) for x in flat]
        + [rows_spec(D)],
        out_specs=[rows_spec(D)] + [whole_spec(x) for x in grads],
        out_shape=[jax.ShapeDtypeStruct((rows, D), F32)] + grads,
        scratch_shapes=[
            pltpu.VMEM((3 * width, D), BF16),
            pltpu.VMEM((width, D), BF16),
            pltpu.VMEM((3 * width, rows), BF16),
        ],
        compiler_params=pltpu.CompilerParams(vmem_limit_bytes=VMEM),
        cost_estimate=pl.CostEstimate(
            flops=4 * rows * D * width * 4 // COST, bytes_accessed=1 << 20, transcendentals=0
        ),
        name="attend_back",
    )(*args)
    return out[0], [out[at : at + 2] for at in range(1, len(out), 2)]


def gelu_both(u):
    c, cube = (2.0 / 3.141592653589793) ** 0.5, 0.044715
    square = u * u
    t = jnp.tanh(c * u * (1.0 + cube * square))
    half = 0.5 * (1.0 + t)
    return u * half, half + 0.5 * u * (1.0 - t * t) * (c + 3.0 * c * cube * square)


def ff_kernel(shapes, steps, *refs):
    refs = list(refs)
    n_ref, g_ref = refs.pop(0), refs.pop(0)
    pieces = [rows_of(x) for x in take(refs, shapes)]
    mix_ref, dn_ref, mix_out, dn_out = (refs.pop(0) for _ in range(4))
    grads = [rows_of([refs.pop(0)]) for _ in range(2)]
    hid_all, du_all = refs
    part = hid_all.shape[0] // 2
    step = pl.program_id(0)
    rows = pl.ds(pl.multiple_of(step * BLOCK, BLOCK), BLOCK)
    mix, dn = mix_ref[...], dn_ref[...]
    for index, (w_in, w_out) in enumerate(pieces):
        low = slice(index * part, (index + 1) * part)
        value, slope = gelu_both(nt(w_in[...], n_ref[rows, :]))
        hidden = value.astype(BF16)
        du = (slope * nt(w_out[...], g_ref[rows, :])).astype(BF16)
        hid_all[low, rows] = hidden
        du_all[low, rows] = du
        mix = mix + tn(hidden, w_out[...])
        dn = dn + tn(du, w_in[...])
    mix_out[...] = mix
    dn_out[...] = dn

    @pl.when(step == steps - 1)
    def _():
        for at in range(0, D, BLOCK):
            columns = slice(at, at + BLOCK)
            for index, (d_in, d_out) in enumerate(grads):
                low = slice(index * part, (index + 1) * part)
                d_in[:, columns] = nn(du_all[low, :], n_ref[:, columns]).astype(BF16)
                d_out[:, columns] = nn(hid_all[low, :], g_ref[:, columns]).astype(BF16)


def ff_slot(normed, grad, pieces, mix, dn):
    rows = normed.shape[0]
    flat, shapes = flatten(pieces)
    part = flat[0].shape[1]
    width = 2 * part
    grads = [jax.ShapeDtypeStruct((2, part, D), BF16)] * 2
    out = pl.pallas_call(
        functools.partial(ff_kernel, shapes, rows // BLOCK),
        grid=(rows // BLOCK,),
        in_specs=[whole_spec(normed), whole_spec(grad)]
        + [whole_spec(x) for x in flat]
        + [rows_spec(D), rows_spec(D)],
        out_specs=[rows_spec(D), rows_spec(D)] + [whole_spec(x) for x in grads],
        out_shape=[jax.ShapeDtypeStruct((rows, D), F32)] * 2 + grads,
        scratch_shapes=[pltpu.VMEM((width, rows), BF16), pltpu.VMEM((width, rows), BF16)],
        compiler_params=pltpu.CompilerParams(vmem_limit_bytes=VMEM),
        cost_estimate=pl.CostEstimate(
            flops=12 * rows * D * width // COST, bytes_accessed=1 << 20, transcendentals=0
        ),
        name="feed_forward",
    )(normed, grad, *flat, mix, dn)
    return out[0], out[1], out[2:]


def after(values, first):
    return lax.optimization_barrier((values, first))[0]


def hold(values, flights):
    return lax.optimization_barrier((values, flights))


def halves_of(array, axis):
    half = array.shape[axis] // 2
    core = lax.axis_index("dp") % 2
    return [
        lax.dynamic_slice_in_dim(array, at * half, half, axis=axis) for at in (core, 1 - core)
    ]


def attention_pieces(weight_qkv, weight_out):
    qkv = weight_qkv.transpose(0, 2, 1)
    whole = jnp.concatenate([qkv, weight_out[None]], axis=0)
    return halves_of(whole, 1)


def ff_pieces(weight_in, weight_out):
    return halves_of(jnp.stack([weight_in.T, weight_out]), 1)


def low_high(piece):
    half = piece.shape[0] // 2
    return [piece[:half], piece[half:]]


def near(piece):
    if lax.axis_size("mp") == 4:
        return {1: [flip(piece, 1)], 2: [flip(piece, 2)]}
    return {}


def far(piece, slots):
    size = lax.axis_size("mp")
    if size == 4:
        return {3: [flip(low_high(slots[1][0])[0], 2), flip(low_high(slots[2][0])[1], 1)]}
    low, high = low_high(piece)
    return {s: [x, y] for s, (x, y) in enumerate(zip(gather(low, False), gather(high, True))) if s}


def twins(arrays):
    return [twin(x) for x in arrays]


def pair_sums(grads, received):
    return [add(x, y) for x, y in zip(low_high(grads[0]), low_high(received))]


def send_far(sums):
    if lax.axis_size("mp") != 4:
        return []
    return [flip(sums[3][0], 1), flip(sums[3][1], 2)]


def send_plain(sums):
    if lax.axis_size("mp") != 4:
        return []
    return [flip(sums[1][0], 1), flip(sums[2][1], 2)]


def send_rest(sums, far_sums):
    if lax.axis_size("mp") != 4:
        return []
    low_two, high_one = far_sums
    return [flip(add(sums[1][1], high_one), 1), flip(add(sums[2][0], low_two), 2)]


def send_both(sums, far_sums):
    if lax.axis_size("mp") != 4:
        return []
    low_two, high_one = far_sums
    ahead = jnp.concatenate([sums[1][0], add(sums[1][1], high_one)], axis=0)
    across = jnp.concatenate([add(sums[2][0], low_two), sums[2][1]], axis=0)
    return [flip(ahead, 1), flip(across, 2)]


def settle_both(sums, both):
    if lax.axis_size("mp") != 4:
        return settle(sums, [], [])
    (low_one, high_one), (low_two, high_two) = low_high(both[0]), low_high(both[1])
    return settle(sums, [low_one, high_two], [high_one, low_two])


def settle(sums, plain, rest):
    if lax.axis_size("mp") != 4:
        return [scatter({s: x[i] for s, x in sums.items()}, bool(i)) for i in range(2)]
    terms = [(sums[0][0], plain[0], rest[1]), (sums[0][1], plain[1], rest[0])]
    return [sum(x.astype(F32) for x in three).astype(BF16) for three in terms]


def both_halves(mine):
    other = twin(mine)
    first = lax.axis_index("dp") % 2 == 0
    return jnp.concatenate(
        [jnp.where(first, mine, other), jnp.where(first, other, mine)], axis=1
    ).astype(F32)


def attention_grads(whole):
    return whole[:3].transpose(0, 2, 1), whole[3]


def shards(
    tokens,
    action_ids,
    clip_lengths,
    action_table,
    norm_gains,
    norm_shifts,
    spatial_qkv,
    spatial_out,
    temporal_qkv,
    temporal_out,
    ff_in,
    ff_out,
    out_grad,
):
    rows_here = tokens.shape[0]
    frames_here = rows_here // POS
    me, size = lax.axis_index("mp"), lax.axis_size("mp")
    frame_ids = lax.dynamic_slice_in_dim(action_ids.reshape(-1), me * frames_here, frames_here)
    one_hot = (
        frame_ids[:, None] == lax.broadcasted_iota(jnp.int32, (frames_here, ACTIONS), 1)
    ).astype(F32)
    per_frame = jnp.dot(one_hot, action_table, precision=lax.Precision.HIGHEST)
    embedded = jnp.broadcast_to(per_frame[:, None, :], (frames_here, POS, D)).reshape(rows_here, D)

    row = jnp.arange(BLOCK)
    frame_of = ((row // GROUP // frames_here) ^ me) * frames_here + row // GROUP % frames_here
    allowed = (
        (row[:, None] % GROUP == row[None] % GROUP)
        & (frame_of[:, None] <= frame_of[None])
        & (frame_of[:, None] < clip_lengths[0])
    )
    mask = jnp.where(allowed, 0.0, -1e9).astype(F32)

    others = [[1, 2], [3]] if size == 4 else [list(range(1, size))]

    own, other = attention_pieces(spatial_qkv, spatial_out)
    close = near(own)
    first = tokens.astype(F32) + embedded
    normed_a, scaled_a, inverse_a = norm_rows(first, norm_gains[0], norm_shifts[0])
    normed_a = normed_a.astype(BF16)
    temporal_own, temporal_other = attention_pieces(*after((temporal_qkv, temporal_out), normed_a))
    spatial = {0: [[own], [other]]}
    kept_a = {}
    second, *kept = attend_slots(normed_a, [spatial[0]], first, None)
    kept_a[0] = (kept, 0)
    (second, temporal_own, temporal_other), close = hold((second, temporal_own, temporal_other), close)
    distant = far(own, close)
    near_b = near(temporal_own)
    close = {s: [x, twins(x)] for s, x in close.items()}
    second, close = hold(second, close)
    if close:
        spatial |= close
        second, *kept = attend_slots(normed_a, [spatial[s] for s in others[0]], second, None)
        kept_a[1] = (kept, 0)
    second, distant = hold(second, distant)
    distant = {s: [x, twins(x)] for s, x in distant.items()}
    second, distant = hold(second, distant)
    spatial |= distant
    second, *kept = attend_slots(normed_a, [spatial[s] for s in others[-1]], second, None)
    kept_a[3] = (kept, 0)
    second, near_b = hold(second, near_b)

    distant = far(temporal_own, near_b)
    near_b = {s: [x, twins(x)] for s, x in near_b.items()}
    parts = send_positions(second.astype(BF16))
    own, other = ff_pieces(*after((ff_in, ff_out), parts[0]))
    parts, (own, other, near_b, distant) = hold(parts, (own, other, near_b, distant))
    distant = {s: [x, twins(x)] for s, x in distant.items()}
    second = join_positions(parts).astype(F32)
    normed_b, scaled_b, inverse_b = norm_rows(second, norm_gains[1], norm_shifts[1])
    normed_b = normed_b.astype(BF16)
    (second, normed_b), distant = hold((second, normed_b), distant)
    temporal = {0: [[temporal_own], [temporal_other]]} | near_b | distant
    grad_parts = send_positions(after(out_grad, parts))
    order_b = [s for group in others for s in group] + [0]
    third, *kept = attend_slots(normed_b, [temporal[s] for s in order_b], second, mask)
    kept_b = {1: (kept, 0), 3: (kept, size - 2 if size == 4 else 0), 0: (kept, size - 1)}
    third, grad_parts = hold(third, grad_parts)
    close = near(after(own, grad_parts))

    grad_result = join_positions(grad_parts)
    normed_c, scaled_c, inverse_c = norm_rows(third, norm_gains[2], norm_shifts[2])
    normed_c = normed_c.astype(BF16)
    result, grad_normed = third, jnp.zeros((rows_here, D), F32)
    grads = {}

    def feed(slot, pieces, flights):
        nonlocal result, grad_normed
        result, grad_normed, grads[slot] = ff_slot(normed_c, grad_result, pieces, result, grad_normed)
        (result, grad_normed, grads[slot]), flights = hold((result, grad_normed, grads[slot]), flights)
        return flights

    def swap(slots):
        return {s: twin(grads[s][1]) for s in slots}

    received, sums_c, plain_c = {}, {}, []

    def sum_up(*slots):
        for s in slots:
            sums_c[s] = pair_sums(grads[s], received[s])

    if size == 4:
        close = feed(0, [[own], [other]], close)
        distant = far(own, close)
        twin_one, twin_two = twins(close[1]), twins(close[2])
        result, twin_one = hold(result, twin_one)
        distant, twin_two, got = feed(1, [close[1], twin_one], (distant, twin_two, swap([0])))
        received |= got
        twin_three, got = feed(2, [close[2], twin_two], (twins(distant[3]), swap([1])))
        received |= got | swap([2])
        sum_up(0, 1, 2)
        result, sums_c = hold(result, sums_c)
        plain_c = feed(3, [distant[3], twin_three], send_plain(sums_c))
    else:
        distant = feed(0, [[own], [other]], far(own, close))
        for slot in range(1, size):
            feed(slot, [distant[slot], twins(distant[slot])], [])
        received = swap(range(size - 1))
        sum_up(*range(size - 1))
    received |= swap([size - 1])
    sum_up(size - 1)
    grad_in, gain_c, shift_c = norm_back(grad_normed, scaled_c, inverse_c, norm_gains[2])
    grad_third = grad_result.astype(F32) + grad_in
    grad_sent = grad_third.astype(BF16)

    def back(normed, gradient, kept, slots, mask, steps, sums, plans):
        grads, received, got = {}, {}, []
        total, sums = hold(jnp.zeros((rows_here, D), F32), sums)
        for at, group in enumerate(steps):
            flights = plans[at](sums, got, total) if size == 4 else []
            swapped = {s: twin(grads[s][1]) for s in (steps[at - 1] if at else [])}
            key = 0 if group == [0] else 3 if group == others[-1] else 1
            total, found = back_slots(normed, gradient, kept[key], [slots[s] for s in group], total, mask)
            grads |= dict(zip(group, found))
            (total, grads), (flights, swapped) = hold((total, grads), (flights, swapped))
            received |= swapped
            for s in swapped:
                plans[-1][s] = pair_sums(grads[s], received[s])
            got.append(flights)
        last = steps[-1][0]
        plans[-1][last] = pair_sums(grads[last], twin(grads[last][1]))
        return total, got

    sums_b, sums_a = {}, {}
    grad_normed, got = back(
        normed_b, grad_sent, kept_b, temporal, mask, others + [[0]], sums_c,
        [
            lambda sums, got, total: send_far(sums),
            lambda sums, got, total: [],
            lambda sums, got, total: send_rest(sums, got[0]),
            sums_b,
        ],
    )
    rest_c = got[2] if size == 4 else []
    grad_in, gain_b, shift_b = norm_back(grad_normed, scaled_b, inverse_b, norm_gains[1])
    grad_second = to_frames((grad_third + grad_in).astype(BF16))
    sum_c, on_way_c = clips_first(*settle(sums_c, plain_c, rest_c))
    (grad_second, sum_c), on_way_c = hold((grad_second, sum_c), on_way_c)
    sum_c, on_way_c = clips_next(sum_c, on_way_c)

    def second_flights(sums, got, total):
        nonlocal sum_c, on_way_c
        return on_way_c, send_both(sums, got[0])

    def third_flights(sums, got, total):
        nonlocal sum_b, on_way_b
        sum_b, on_way_b = clips_first(*settle_both(sums, got[1][1]))
        return send_far(sums_a), on_way_b

    steps = others[::-1] + [[0]]
    sum_b = on_way_b = None
    grad_normed, got = back(
        normed_a, grad_second, kept_a, spatial, None, steps, sums_b,
        [lambda sums, got, total: send_far(sums), second_flights, third_flights, sums_a],
    )
    far_a = []
    if size == 4:
        on_way_c = got[1][0]
        far_a, on_way_b = got[2]
    else:
        sum_b, on_way_b = clips_first(*settle(sums_b, [], []))
    sum_c, on_way_c = clips_last(sum_c, on_way_c)
    both_a = send_both(sums_a, far_a)
    sum_b, on_way_b = clips_next(sum_b, on_way_b)
    whole_c = clips_joined(sum_c, on_way_c)
    sum_a, on_way_a = clips_first(*settle_both(sums_a, both_a))
    mixed = to_frames(after(result.astype(BF16), sum_a))
    sum_b, on_way_b = clips_last(sum_b, on_way_b)
    whole_b = clips_joined(sum_b, on_way_b)
    sum_a, on_way_a = clips_next(sum_a, on_way_a)
    sum_a, on_way_a = clips_last(sum_a, on_way_a)
    whole_a = clips_joined(sum_a, on_way_a)

    whole = both_halves(whole_c)
    grad_ff_in, grad_ff_out = whole[0].T, whole[1]
    grad_tqkv, grad_tout = attention_grads(both_halves(whole_b))
    grad_sqkv, grad_sout = attention_grads(both_halves(whole_a))

    grad_in, gain_a, shift_a = norm_back(grad_normed, scaled_a, inverse_a, norm_gains[0])
    grad_first = grad_second.astype(F32) + grad_in
    frame_grads = jnp.sum(grad_first.reshape(frames_here, POS, -1), axis=1)
    grad_table = jnp.dot(one_hot.T, frame_grads, precision=lax.Precision.HIGHEST)
    small = over_all(
        jnp.concatenate(
            [jnp.stack([gain_a, gain_b, gain_c, shift_a, shift_b, shift_c]), grad_table], axis=0
        )
    )
    gains_sum, shifts_sum, table_sum = small[:3], small[3:6], small[6:]
    return (
        mixed,
        grad_first,
        table_sum,
        gains_sum,
        shifts_sum,
        grad_sqkv,
        grad_sout,
        grad_tqkv,
        grad_tout,
        grad_ff_in,
        grad_ff_out,
    )


def solution(mesh):
    return jax.shard_map(
        shards,
        mesh=mesh,
        in_specs=(
            P(("dp", "mp"), None),
            P("dp", None),
            P("dp"),
            P(),
            P(),
            P(),
            P(None, None, "mp"),
            P("mp", None),
            P(None, None, "mp"),
            P("mp", None),
            P(None, "mp"),
            P("mp", None),
            P(("dp", "mp"), None),
        ),
        out_specs=(
            P(("dp", "mp"), None),
            P(("dp", "mp"), None),
            P(),
            P(),
            P(),
            P(None, None, "mp"),
            P("mp", None),
            P(None, None, "mp"),
            P("mp", None),
            P(None, "mp"),
            P("mp", None),
        ),
        check_vma=False,
    )
```

```python
import functools

import jax
import jax.numpy as jnp
from jax import lax
from jax.experimental import pallas as pl
from jax.experimental.pallas import tpu as pltpu
from jax.sharding import PartitionSpec as P

D = 1024
HEAD_DIM = 64
FRAMES = 16
POS = 256
ACTIONS = 8
EPS = 1e-05
BLOCK = 256
GROUP = BLOCK // FRAMES
VMEM = 34 << 20
VMEM_LAST = 60 << 20
COST = 1
LSE_ROWS = 8
BF16 = jnp.bfloat16
F32 = jnp.float32


def norm_rows(hidden, gain_row, shift_row):
    average = jnp.mean(hidden, axis=-1, keepdims=True)
    centred = hidden - average
    inverse = lax.rsqrt(jnp.mean(centred * centred, axis=-1, keepdims=True) + EPS)
    scaled = centred * inverse
    return scaled * gain_row + shift_row, scaled, inverse


def norm_back(gradient, hidden, gain_row):
    _, scaled, inverse = norm_rows(hidden, 1.0, 0.0)
    grad_gain = jnp.sum(gradient * scaled, axis=0, keepdims=True)
    grad_shift = jnp.sum(gradient, axis=0, keepdims=True)
    inner = gradient * gain_row
    grad_in = inverse * (
        inner
        - jnp.mean(inner, axis=-1, keepdims=True)
        - scaled * jnp.mean(inner * scaled, axis=-1, keepdims=True)
    )
    return grad_in, grad_gain, grad_shift


def flip(values, offset, axis="mp"):
    size = lax.axis_size(axis)
    return lax.ppermute(values, axis, [(i, i ^ offset) for i in range(size)])


def twin(values):
    return flip(values, 1, "dp")


def bits_of(count, reverse):
    bits = [1 << b for b in range(count.bit_length() - 1)]
    return bits[::-1] if reverse else bits


def gather(piece, reverse, axis="mp", unit=1):
    slots = {0: piece}
    for bit in bits_of(lax.axis_size(axis) // unit, reverse):
        for slot in list(slots):
            slots[slot | bit] = flip(slots[slot], bit * unit, axis)
    return [slots[s] for s in range(len(slots))]


def add(left, right):
    return (left.astype(F32) + right.astype(F32)).astype(BF16)


def scatter_step(slots, bit, axis="mp", unit=1):
    return {
        s: add(value, flip(slots[s | bit], bit * unit, axis)) for s, value in slots.items() if not s & bit
    }


def scatter(slots, reverse, axis="mp", unit=1):
    slots = dict(slots)
    for bit in bits_of(lax.axis_size(axis) // unit, reverse):
        slots = scatter_step(slots, bit, axis, unit)
    return slots[0]


def clip_offsets():
    return [bit * 2 for bit in bits_of(lax.axis_size("dp") // 2, False)]


def even_clips():
    return lax.axis_index("dp") // 2 % 2 == 0


def clips_first(low, high):
    even = even_clips()
    return jnp.where(even, low, high), flip(jnp.where(even, high, low), clip_offsets()[0], "dp")


def clips_between(mine, arrived):
    mine = add(mine, arrived)
    for offset in clip_offsets()[1:-1]:
        mine = add(mine, flip(mine, offset, "dp"))
    return mine


def send_far_clips(mine):
    return flip(mine, clip_offsets()[-1], "dp")


def clips_next(mine, arrived):
    mine = clips_between(mine, arrived)
    return mine, send_far_clips(mine)


def clips_last(mine, arrived):
    mine = add(mine, arrived)
    return mine, flip(mine, clip_offsets()[0], "dp")


def clips_joined(mine, other):
    even = even_clips()
    return jnp.concatenate([jnp.where(even, mine, other), jnp.where(even, other, mine)], axis=0)


def over_all(values, steps):
    for axis, offset in steps:
        values = values + flip(values, offset, axis)
    return values


def send_positions(rows):
    me, size = lax.axis_index("mp"), lax.axis_size("mp")
    here = POS // size
    view = rows.reshape(rows.shape[0] // POS, POS, D)
    parts = []
    for slot in range(size):
        part = lax.dynamic_slice_in_dim(view, (me ^ slot) * here, here, axis=1)
        parts.append(flip(part, slot) if slot else part)
    return parts


def join_positions(parts):
    here = parts[0].shape[1]
    whole = jnp.concatenate(parts, axis=0).reshape(FRAMES, here // GROUP, GROUP, D)
    return whole.transpose(1, 0, 2, 3).reshape(FRAMES * here, D)


def send_frames(rows):
    size = lax.axis_size("mp")
    frames_here = FRAMES // size
    view = rows.reshape(rows.shape[0] // BLOCK, size, frames_here, GROUP, D)
    return [flip(view[:, slot], slot) if slot else view[:, slot] for slot in range(size)]


def join_frames(parts):
    me = lax.axis_index("mp")
    groups, frames_here = parts[0].shape[:2]
    here = groups * GROUP
    whole = jnp.zeros((frames_here, POS, D), parts[0].dtype)
    for slot, part in enumerate(parts):
        part = part.transpose(1, 0, 2, 3).reshape(frames_here, here, D)
        whole = lax.dynamic_update_slice_in_dim(whole, part, (me ^ slot) * here, axis=1)
    return whole.reshape(frames_here * POS, D)


def nn(left, right):
    return lax.dot_general(left, right, (((1,), (0,)), ((), ())), preferred_element_type=F32)


def nt(left, right):
    return lax.dot_general(left, right, (((1,), (1,)), ((), ())), preferred_element_type=F32)


def tn(left, right):
    return lax.dot_general(left, right, (((0,), (0,)), ((), ())), preferred_element_type=F32)


def flatten(slots):
    return jax.tree.leaves(slots), jax.tree.map(lambda x: 0, slots)


def whole_spec(array):
    return pl.BlockSpec(array.shape, lambda i: (0,) * array.ndim, pipeline_mode=pl.Buffered(1))


def rows_spec(width):
    return pl.BlockSpec((BLOCK, width), lambda i: (i, 0))


def columns_spec(height, index=0):
    return pl.BlockSpec((height, BLOCK), lambda i: (index, i))


def part_spec(shape, index):
    return pl.BlockSpec(shape, lambda i: (index, 0), pipeline_mode=pl.Buffered(1))


def rows_of(refs):
    return [ref.at[i] for ref in refs for i in range(ref.shape[0])]


def load_weights(slots, qkv, out):
    part = slots[0][0][0].shape[1]
    width = 2 * part

    @pl.when(pl.program_id(0) == 0)
    def _():
        for index, parts in enumerate(slots):
            for half, refs in enumerate(parts):
                *three, o = rows_of(refs)
                for which, ref in enumerate(three):
                    at = 3 * width * index + width * which + part * half
                    qkv[at : at + part, :] = ref[...]
                at = width * index + part * half
                out[at : at + part, :] = o[...]


def take(refs, shapes):
    return jax.tree.map(lambda _: refs.pop(0), shapes)


def heads_apart(rows):
    owner = lax.broadcasted_iota(jnp.int32, rows.shape, 0) // HEAD_DIM
    return jnp.concatenate(
        [jnp.where(owner == h, rows, 0).astype(BF16) for h in range(rows.shape[0] // HEAD_DIM)], axis=1
    )


def attend_kernel(masked, shapes, senders, *refs):
    refs = list(refs)
    mask = refs.pop(0) if masked else None
    if senders:
        norms = refs.pop(0)
        arrived = [refs.pop(0) for _ in range(senders)]
    else:
        n_ref = refs.pop(0)
    slots, count = take(refs, shapes), len(shapes)
    acc_ref = None if senders else refs.pop(0)
    out_ref, qkv_ref, ctx_ref, lse_ref = (refs.pop(0) for _ in range(4))
    if senders:
        h_ref, n_ref, next_ref = (refs.pop(0) for _ in range(3))
    w_qkv, w_out = refs
    if senders:
        hidden = jnp.concatenate([x[...].reshape(-1, D) for x in arrived], axis=0)
        h_ref[...] = hidden
        hidden = hidden.astype(F32)
        n_ref[...] = norm_rows(hidden, norms[0:1], norms[1:2])[0].astype(BF16)
    else:
        hidden = acc_ref[...]
    load_weights(slots, w_qkv, w_out)
    width = w_out.shape[0] // count
    heads = width // HEAD_DIM
    together = min(4, heads)
    group = together * HEAD_DIM
    for slot in range(count):
        base = 3 * width * slot
        qkv = nt(w_qkv[base : base + 3 * width, :], n_ref[...])
        qkv_ref[base : base + width, :] = (qkv[:width] * HEAD_DIM**-0.5).astype(BF16)
        qkv_ref[base + width : base + 3 * width, :] = qkv[width:].astype(BF16)
        keys = qkv[width : 2 * width].T.astype(BF16)
        for at in range(0, width, group):
            q = heads_apart(qkv_ref[base + at : base + at + group, :])
            logits = nn(keys[:, at : at + group], q)
            if masked:
                logits = logits + jnp.concatenate([mask[...]] * together, axis=1)
            highest = jnp.max(logits, axis=0, keepdims=True)
            raised = jnp.exp(logits - highest)
            total = jnp.sum(raised, axis=0, keepdims=True)
            log_total = highest + jnp.log(total)
            inverse = 1.0 / total
            raised = raised.astype(BF16)
            for head in range(together):
                columns = slice(head * BLOCK, (head + 1) * BLOCK)
                row = slot * LSE_ROWS + at // HEAD_DIM + head
                lse_ref[row : row + 1, :] = log_total[:, columns]
                start = base + 2 * width + at + head * HEAD_DIM
                values = qkv_ref[start : start + HEAD_DIM, :]
                start = slot * width + at + head * HEAD_DIM
                ctx_ref[start : start + HEAD_DIM, :] = (
                    nn(values, raised[:, columns]) * inverse[:, columns]
                ).astype(BF16)
    hidden = hidden + tn(ctx_ref[...], w_out[...])
    out_ref[...] = hidden.astype(out_ref.dtype)
    if senders:
        next_ref[...] = norm_rows(hidden, norms[2:3], norms[3:4])[0].astype(BF16)


def attend_slots(normed, slots, acc, mask, out_type=F32):
    return attend_call(normed.shape[0], [normed], slots, [acc], mask, [], out_type)


def attend_arrived(arrived, norms, slots, mask):
    rows = sum(x.shape[0] * x.shape[1] for x in arrived)
    return attend_call(rows, arrived, slots, [], mask, [norms], F32)


def attend_call(rows, inputs, slots, acc, mask, norms, out_type):
    flat, shapes = flatten(slots)
    width = len(slots) * 2 * flat[0].shape[1]
    lse_rows = LSE_ROWS * len(slots)
    first = ([] if mask is None else [mask]) + norms
    args = first + inputs + flat + acc
    arrived_spec = [pl.BlockSpec((x.shape[0], GROUP, D), lambda i: (0, i, 0)) for x in inputs]
    return pl.pallas_call(
        functools.partial(attend_kernel, mask is not None, shapes, len(inputs) if norms else 0),
        grid=(rows // BLOCK,),
        in_specs=[whole_spec(x) for x in first]
        + (arrived_spec if norms else [rows_spec(D)])
        + [whole_spec(x) for x in flat]
        + [rows_spec(D)] * len(acc),
        out_specs=[rows_spec(D), columns_spec(3 * width), columns_spec(width), columns_spec(lse_rows)]
        + [rows_spec(D)] * (3 * len(norms)),
        out_shape=[
            jax.ShapeDtypeStruct((rows, D), out_type),
            jax.ShapeDtypeStruct((3 * width, rows), BF16),
            jax.ShapeDtypeStruct((width, rows), BF16),
            jax.ShapeDtypeStruct((lse_rows, rows), F32),
        ]
        + [jax.ShapeDtypeStruct((rows, D), BF16)] * (3 * len(norms)),
        scratch_shapes=[pltpu.VMEM((3 * width, D), BF16), pltpu.VMEM((width, D), BF16)],
        compiler_params=pltpu.CompilerParams(vmem_limit_bytes=VMEM),
        cost_estimate=pl.CostEstimate(
            flops=2 * rows * D * width * 4 // COST, bytes_accessed=1 << 20, transcendentals=0
        ),
        name="attend",
    )(*args)


def finish(refs, gradient):
    gain, h_ref, past, *totals, sums, block_sums = refs

    @pl.when(pl.program_id(0) == 0)
    def _():
        sums[...] = jnp.zeros_like(sums)

    grad_in, grad_gain, grad_shift = norm_back(gradient, h_ref[...].astype(F32), gain[...])
    sums[0:1] += grad_gain
    sums[1:2] += grad_shift
    grad_in = past[...].astype(F32) + grad_in
    for total in totals:
        total[...] = grad_in.astype(total.dtype)
    block_sums[...] = jnp.broadcast_to(jnp.sum(grad_in, axis=0, keepdims=True), block_sums.shape)


def finish_specs(rows, types):
    steps = rows // BLOCK
    once = pl.BlockSpec((8, D), lambda i: (0, 0))
    return (
        [pl.BlockSpec((1, D), lambda i: (0, 0)), rows_spec(D), rows_spec(D)],
        [rows_spec(D)] * len(types) + [once, pl.BlockSpec((8, D), lambda i: (i, 0))],
        [jax.ShapeDtypeStruct((rows, D), t) for t in types]
        + [jax.ShapeDtypeStruct((8, D), F32), jax.ShapeDtypeStruct((8 * steps, D), F32)],
    )


def back_kernel(masked, shapes, steps, types, *refs):
    refs = list(refs)
    mask = refs.pop(0) if masked else None
    n_ref, g_ref, qkv_ref, ctx_ref, lse_ref = (refs.pop(0) for _ in range(5))
    slots, count = take(refs, shapes), len(shapes)
    acc_ref = refs.pop(0)
    last = [refs.pop(0) for _ in range(3)] if types else []
    last += [refs.pop(0) for _ in range(len(types) + 2 if types else 1)]
    grads = [refs.pop(0) for _ in range(2)]
    w_qkv, w_out, d_all = refs
    load_weights(slots, w_qkv, w_out)
    width = w_out.shape[0] // count
    heads = width // HEAD_DIM
    step = pl.program_id(0)
    rows = pl.ds(pl.multiple_of(step * BLOCK, BLOCK), BLOCK)
    together = min(4, heads)
    group = together * HEAD_DIM
    for slot in range(count):
        base = 3 * width * slot
        d_ctx = nt(w_out[slot * width : (slot + 1) * width, :], g_ref[rows, :]).astype(BF16)
        keys = qkv_ref[base + width : base + 2 * width, :].T
        values = qkv_ref[base + 2 * width : base + 3 * width, :].T
        for at in range(0, width, group):
            q = qkv_ref[base + at : base + at + group, :]
            d_group = d_ctx[at : at + group]
            logits = nn(keys[:, at : at + group], heads_apart(q))
            if masked:
                logits = logits + jnp.concatenate([mask[...]] * together, axis=1)
            d_p = nn(values[:, at : at + group], heads_apart(d_group))
            ctx = ctx_ref[slot * width + at : slot * width + at + group, rows]
            product = d_group.astype(F32) * ctx.astype(F32)
            split = [slice(h * HEAD_DIM, (h + 1) * HEAD_DIM) for h in range(together)]
            row = slot * LSE_ROWS + at // HEAD_DIM
            lse = jnp.concatenate([lse_ref[row + h : row + h + 1, :] for h in range(together)], axis=1)
            total = jnp.concatenate([jnp.sum(product[s], axis=0, keepdims=True) for s in split], axis=1)
            p = jnp.exp(logits - lse)
            ds = (p * (d_p - total)).astype(BF16)
            p = p.astype(BF16)
            for head in range(together):
                columns = slice(head * BLOCK, (head + 1) * BLOCK)
                start = base + at + head * HEAD_DIM
                key = qkv_ref[width + start : width + start + HEAD_DIM, :]
                d_all[start : start + HEAD_DIM, rows] = (
                    nn(key, ds[:, columns]) * HEAD_DIM**-0.5
                ).astype(BF16)
                start = start + width
                d_all[start : start + HEAD_DIM, rows] = nt(q[split[head]], ds[:, columns]).astype(BF16)
                start = start + width
                d_all[start : start + HEAD_DIM, rows] = nt(
                    d_group[split[head]], p[:, columns]
                ).astype(BF16)
    total = acc_ref[...] + tn(d_all[:, rows], w_qkv[...])
    if types:
        finish(last, total)
    else:
        last[0][...] = total

    @pl.when(step == steps - 1)
    def _():
        part = width // 2
        for at in range(0, D, BLOCK):
            columns = slice(at, at + BLOCK)
            d_w = nn(d_all[...], n_ref[:, columns]).astype(BF16)
            d_o = nn(ctx_ref[...], g_ref[:, columns]).astype(BF16)
            for index in range(count):
                for half, ref in enumerate(grads):
                    for which in range(3):
                        at = 3 * width * index + width * which + part * half
                        ref[4 * index + which, :, columns] = d_w[at : at + part]
                    at = width * index + part * half
                    ref[4 * index + 3, :, columns] = d_o[at : at + part]


def back_slots(normed, grad, kept, slots, acc, mask, last=(), types=()):
    rows = normed.shape[0]
    (qkv, ctx, lse), place = kept
    flat, shapes = flatten(slots)
    part = flat[0].shape[1]
    width = len(slots) * 2 * part
    grads = [jax.ShapeDtypeStruct((4 * len(slots), part, D), BF16)] * 2
    lse_rows, index = LSE_ROWS * len(slots), place // len(slots)
    masked = mask is not None
    first = [mask] if masked else []
    args = first + [normed, grad, qkv, ctx, lse] + flat + [acc] + list(last)
    taken, given, shapes_given = finish_specs(rows, types)
    if not types:
        taken, given, shapes_given = [], [rows_spec(D)], [jax.ShapeDtypeStruct((rows, D), F32)]
    out = pl.pallas_call(
        functools.partial(back_kernel, masked, shapes, rows // BLOCK, types),
        grid=(rows // BLOCK,),
        in_specs=[whole_spec(x) for x in first]
        + [whole_spec(normed), whole_spec(grad)]
        + [columns_spec(3 * width, index), part_spec((width, rows), index), columns_spec(lse_rows, index)]
        + [whole_spec(x) for x in flat]
        + [rows_spec(D)]
        + taken,
        out_specs=given + [whole_spec(x) for x in grads],
        out_shape=shapes_given + grads,
        scratch_shapes=[
            pltpu.VMEM((3 * width, D), BF16),
            pltpu.VMEM((width, D), BF16),
            pltpu.VMEM((3 * width, rows), BF16),
        ],
        compiler_params=pltpu.CompilerParams(vmem_limit_bytes=VMEM_LAST if types and masked else VMEM),
        cost_estimate=pl.CostEstimate(
            flops=4 * rows * D * width * 4 // COST, bytes_accessed=1 << 20, transcendentals=0
        ),
        name="attend_back",
    )(*args)
    return out[:-2] if types else out[0], out[-2:]


def gelu_both(u):
    c, cube = (2.0 / 3.141592653589793) ** 0.5, 0.044715
    square = u * u
    t = jnp.tanh(c * u * (1.0 + cube * square))
    half = 0.5 * (1.0 + t)
    return u * half, half + 0.5 * u * (1.0 - t * t) * (c + 3.0 * c * cube * square)


def ff_kernel(shapes, steps, types, *refs):
    refs = list(refs)
    n_ref, g_ref = refs.pop(0), refs.pop(0)
    pieces = [rows_of(x) for x in take(refs, shapes)]
    mix_ref, dn_ref = refs.pop(0), refs.pop(0)
    last = [refs.pop(0) for _ in range(3)] if types else []
    mix_out = refs.pop(0)
    last += [refs.pop(0) for _ in range(len(types) + 2 if types else 1)]
    grads = [rows_of([refs.pop(0)]) for _ in range(2)]
    hid_all, du_all = refs
    part = hid_all.shape[0] // 2
    step = pl.program_id(0)
    rows = pl.ds(pl.multiple_of(step * BLOCK, BLOCK), BLOCK)
    mix, dn = mix_ref[...], dn_ref[...]
    for index, (w_in, w_out) in enumerate(pieces):
        low = slice(index * part, (index + 1) * part)
        value, slope = gelu_both(nt(w_in[...], n_ref[rows, :]))
        hidden = value.astype(BF16)
        du = (slope * nt(w_out[...], g_ref[rows, :])).astype(BF16)
        hid_all[low, rows] = hidden
        du_all[low, rows] = du
        mix = mix + tn(hidden, w_out[...])
        dn = dn + tn(du, w_in[...])
    mix_out[...] = mix.astype(mix_out.dtype)
    if types:
        finish(last, dn)
    else:
        last[0][...] = dn

    @pl.when(step == steps - 1)
    def _():
        for at in range(0, D, BLOCK):
            columns = slice(at, at + BLOCK)
            for index, (d_in, d_out) in enumerate(grads):
                low = slice(index * part, (index + 1) * part)
                d_in[:, columns] = nn(du_all[low, :], n_ref[:, columns]).astype(BF16)
                d_out[:, columns] = nn(hid_all[low, :], g_ref[:, columns]).astype(BF16)


def ff_slot(normed, grad, pieces, mix, dn, last=(), types=()):
    rows = normed.shape[0]
    flat, shapes = flatten(pieces)
    part = flat[0].shape[1]
    width = 2 * part
    grads = [jax.ShapeDtypeStruct((2, part, D), BF16)] * 2
    taken, given, shapes_given = finish_specs(rows, types)
    if not types:
        taken, given, shapes_given = [], [rows_spec(D)], [jax.ShapeDtypeStruct((rows, D), F32)]
    out = pl.pallas_call(
        functools.partial(ff_kernel, shapes, rows // BLOCK, types),
        grid=(rows // BLOCK,),
        in_specs=[whole_spec(normed), whole_spec(grad)]
        + [whole_spec(x) for x in flat]
        + [rows_spec(D), rows_spec(D)]
        + taken,
        out_specs=[rows_spec(D)] + given + [whole_spec(x) for x in grads],
        out_shape=[jax.ShapeDtypeStruct((rows, D), BF16 if types else F32)] + shapes_given + grads,
        scratch_shapes=[pltpu.VMEM((width, rows), BF16), pltpu.VMEM((width, rows), BF16)],
        compiler_params=pltpu.CompilerParams(vmem_limit_bytes=VMEM),
        cost_estimate=pl.CostEstimate(
            flops=12 * rows * D * width // COST, bytes_accessed=1 << 20, transcendentals=0
        ),
        name="feed_forward",
    )(normed, grad, *flat, mix, dn, *last)
    return out[0], out[1:-2] if types else out[1], out[-2:]


def after(values, first):
    return lax.optimization_barrier((values, first))[0]


def hold(values, flights):
    return lax.optimization_barrier((values, flights))


def halves_of(array, axis):
    half = array.shape[axis] // 2
    core = lax.axis_index("dp") % 2
    return [
        lax.dynamic_slice_in_dim(array, at * half, half, axis=axis) for at in (core, 1 - core)
    ]


def attention_pieces(weight_qkv, weight_out):
    qkv = weight_qkv.transpose(0, 2, 1)
    whole = jnp.concatenate([qkv, weight_out[None]], axis=0)
    return halves_of(whole, 1)


def ff_pieces(weight_in, weight_out):
    return halves_of(jnp.stack([weight_in.T, weight_out]), 1)


def low_high(piece):
    half = piece.shape[0] // 2
    return [piece[:half], piece[half:]]


def near(piece):
    if lax.axis_size("mp") == 4:
        return {1: [flip(piece, 1)], 2: [flip(piece, 2)]}
    return {}


def far(piece, slots):
    size = lax.axis_size("mp")
    if size == 4:
        return {3: [flip(low_high(slots[1][0])[0], 2), flip(low_high(slots[2][0])[1], 1)]}
    low, high = low_high(piece)
    return {s: [x, y] for s, (x, y) in enumerate(zip(gather(low, False), gather(high, True))) if s}


def twins(arrays):
    return [twin(x) for x in arrays]


def pair_sums(grads, received):
    return [add(x, y) for x, y in zip(low_high(grads[0]), low_high(received))]


def send_far(sums):
    if lax.axis_size("mp") != 4:
        return []
    return [flip(sums[3][0], 1), flip(sums[3][1], 2)]


def send_plain(sums):
    if lax.axis_size("mp") != 4:
        return []
    return [flip(sums[1][0], 1), flip(sums[2][1], 2)]


def send_rest(sums, far_sums):
    if lax.axis_size("mp") != 4:
        return []
    low_two, high_one = far_sums
    return [flip(add(sums[1][1], high_one), 1), flip(add(sums[2][0], low_two), 2)]


def send_both(sums, far_sums):
    if lax.axis_size("mp") != 4:
        return []
    low_two, high_one = far_sums
    ahead = jnp.concatenate([sums[1][0], add(sums[1][1], high_one)], axis=0)
    across = jnp.concatenate([add(sums[2][0], low_two), sums[2][1]], axis=0)
    return [flip(ahead, 1), flip(across, 2)]


def settle_both(sums, both):
    if lax.axis_size("mp") != 4:
        return settle(sums, [], [])
    (low_one, high_one), (low_two, high_two) = low_high(both[0]), low_high(both[1])
    return settle(sums, [low_one, high_two], [high_one, low_two])


def settle(sums, plain, rest):
    if lax.axis_size("mp") != 4:
        return [scatter({s: x[i] for s, x in sums.items()}, bool(i)) for i in range(2)]
    terms = [(sums[0][0], plain[0], rest[1]), (sums[0][1], plain[1], rest[0])]
    return [sum(x.astype(F32) for x in three).astype(BF16) for three in terms]


def both_halves(mine, other):
    first = lax.axis_index("dp") % 2 == 0
    return jnp.concatenate(
        [jnp.where(first, mine, other), jnp.where(first, other, mine)], axis=1
    ).astype(F32)


def attention_grads(whole):
    return whole[:3].transpose(0, 2, 1), whole[3]


def shards(
    tokens,
    action_ids,
    clip_lengths,
    action_table,
    norm_gains,
    norm_shifts,
    spatial_qkv,
    spatial_out,
    temporal_qkv,
    temporal_out,
    ff_in,
    ff_out,
    out_grad,
):
    rows_here = tokens.shape[0]
    frames_here = rows_here // POS
    me, size = lax.axis_index("mp"), lax.axis_size("mp")
    frame_ids = lax.dynamic_slice_in_dim(action_ids.reshape(-1), me * frames_here, frames_here)
    one_hot = (
        frame_ids[:, None] == lax.broadcasted_iota(jnp.int32, (frames_here, ACTIONS), 1)
    ).astype(F32)
    per_frame = jnp.dot(one_hot, action_table, precision=lax.Precision.HIGHEST)
    embedded = jnp.broadcast_to(per_frame[:, None, :], (frames_here, POS, D)).reshape(rows_here, D)

    row = jnp.arange(BLOCK)
    frame_of = ((row // GROUP // frames_here) ^ me) * frames_here + row // GROUP % frames_here
    allowed = (
        (row[:, None] % GROUP == row[None] % GROUP)
        & (frame_of[:, None] <= frame_of[None])
        & (frame_of[:, None] < clip_lengths[0])
    )
    mask = jnp.where(allowed, 0.0, -1e9).astype(F32)

    others = [[1, 2], [3]] if size == 4 else [list(range(1, size))]

    own, other = attention_pieces(spatial_qkv, spatial_out)
    close = near(own)
    first = tokens.astype(F32) + embedded
    normed_a = norm_rows(first, norm_gains[0], norm_shifts[0])[0].astype(BF16)
    temporal_own, temporal_other = attention_pieces(*after((temporal_qkv, temporal_out), normed_a))
    spatial = {0: [[own], [other]]}
    kept_a = {}
    second, *kept = attend_slots(normed_a, [spatial[0]], first, None)
    kept_a[0] = (kept, 0)
    (second, temporal_own, temporal_other), close = hold((second, temporal_own, temporal_other), close)
    distant = far(own, close)
    near_b = near(temporal_own)
    close = {s: [x, twins(x)] for s, x in close.items()}
    second, close = hold(second, close)
    if close:
        spatial |= close
        second, *kept = attend_slots(normed_a, [spatial[s] for s in others[0]], second, None)
        kept_a[1] = (kept, 0)
    second, distant = hold(second, distant)
    distant = {s: [x, twins(x)] for s, x in distant.items()}
    second, distant = hold(second, distant)
    spatial |= distant
    second, *kept = attend_slots(normed_a, [spatial[s] for s in others[-1]], second, None, BF16)
    kept_a[3] = (kept, 0)
    second, near_b = hold(second, near_b)

    distant = far(temporal_own, near_b)
    near_b = {s: [x, twins(x)] for s, x in near_b.items()}
    parts = send_positions(second)
    own, other = ff_pieces(*after((ff_in, ff_out), parts[0]))
    parts, (own, other, near_b, distant) = hold(parts, (own, other, near_b, distant))
    grad_parts = send_positions(after(out_grad, parts))
    distant = {s: [x, twins(x)] for s, x in distant.items()}
    (parts, own, other), distant = hold((parts, own, other), distant)
    close = near(own)
    temporal = {0: [[temporal_own], [temporal_other]]} | near_b | distant
    order_b = [s for group in others for s in group] + [0]
    norms = jnp.concatenate([norm_gains[1:2], norm_shifts[1:2], norm_gains[2:], norm_shifts[2:]], axis=0)
    third, *kept, second, normed_b, normed_c = attend_arrived(
        parts, norms, [temporal[s] for s in order_b], mask
    )
    kept_b = {1: (kept, 0), 3: (kept, size - 2 if size == 4 else 0), 0: (kept, size - 1)}
    (third, normed_c), grad_parts = hold((third, normed_c), grad_parts)

    grad_result = join_positions(grad_parts)
    result, grad_normed = third, jnp.zeros((rows_here, D), F32)
    grads = {}

    def feed(slot, pieces, flights):
        nonlocal result, grad_normed
        last, types = ((norm_gains[2:], third, grad_result), (F32, BF16)) if slot == size - 1 else ((), ())
        result, grad_normed, grads[slot] = ff_slot(
            normed_c, grad_result, pieces, result, grad_normed, last, types
        )
        (result, grad_normed, grads[slot]), flights = hold((result, grad_normed, grads[slot]), flights)
        return flights

    def swap(slots):
        return {s: twin(grads[s][1]) for s in slots}

    received, sums_c, plain_c = {}, {}, []

    def sum_up(*slots):
        for s in slots:
            sums_c[s] = pair_sums(grads[s], received[s])

    if size == 4:
        close = feed(0, [[own], [other]], close)
        distant = far(own, close)
        twin_one, twin_two = twins(close[1]), twins(close[2])
        result, twin_one = hold(result, twin_one)
        distant, twin_two, got = feed(1, [close[1], twin_one], (distant, twin_two, swap([0])))
        received |= got
        twin_three, got = feed(2, [close[2], twin_two], (twins(distant[3]), swap([1])))
        received |= got | swap([2])
        sum_up(0, 1, 2)
        result, (sums_c[1][0], sums_c[2][1]) = hold(result, (sums_c[1][0], sums_c[2][1]))
        plain_c = feed(3, [distant[3], twin_three], send_plain(sums_c))
    else:
        distant = feed(0, [[own], [other]], far(own, close))
        for slot in range(1, size):
            feed(slot, [distant[slot], twins(distant[slot])], [])
        received = swap(range(size - 1))
        sum_up(*range(size - 1))
    received |= swap([size - 1])
    sum_up(size - 1)
    grad_third, grad_sent, norm_sums_c, _ = grad_normed

    def back(normed, gradient, kept, slots, mask, steps, sums, plans, last, types):
        mine, received, got, sums_here = {}, {}, [], plans[-1]
        total = jnp.zeros((rows_here, D), F32)
        if size == 4:
            total, sums[3] = hold(total, sums[3])
        swapped = {}
        for at, group in enumerate(steps):
            flights = plans[at](sums, got) if size == 4 else []
            key = 0 if group == [0] else 3 if group == others[-1] else 1
            end = (last, types) if at == len(steps) - 1 else ()
            total, found = back_slots(
                normed, gradient, kept[key], [slots[s] for s in group], total, mask, *end
            )
            (total, found), (flights, swapped) = hold((total, found), (flights, swapped))
            for place, s in enumerate(swapped and steps[at - 1]):
                one = slice(4 * place, 4 * place + 4)
                sums_here[s] = pair_sums([mine[at - 1][one]], swapped[0][one])
            mine[at] = found[0]
            swapped = [twin(found[1])]
            got.append(flights)
        sums_here[0] = pair_sums([found[0]], swapped[0])
        return total, got

    sums_b, sums_a = {}, {}
    (grad_second, norm_sums_b, _), got = back(
        normed_b, grad_sent, kept_b, temporal, mask, others + [[0]], sums_c,
        [
            lambda sums, got: send_far(sums),
            lambda sums, got: [],
            lambda sums, got: send_rest(sums, got[0]),
            sums_b,
        ],
        (norm_gains[1:2], second, grad_third), (BF16,),
    )
    rest_c = got[2] if size == 4 else []
    parts = send_frames(grad_second)
    sum_c, on_way_c = clips_first(*settle(sums_c, plain_c, rest_c))
    (parts, sum_c), on_way_c = hold((parts, sum_c), on_way_c)
    sum_c = clips_between(sum_c, on_way_c)
    grad_second = join_frames(parts)
    quarter = sum_c.shape[1] // 4
    cuts = [0, quarter, 3 * quarter, 4 * quarter]
    pieces_c = [sum_c[:, low:high] for low, high in zip(cuts, cuts[1:])]

    def first_flights(sums, got):
        return send_far(sums), send_far_clips(pieces_c[0])

    def second_flights(sums, got):
        return send_both(sums, got[0][0]), send_far_clips(after(pieces_c[1], got[0][1]))

    def third_flights(sums, got):
        nonlocal sum_b, on_way_b
        sum_b, on_way_b = clips_first(*settle_both(sums, got[1][0]))
        return send_far(sums_a), on_way_b, send_far_clips(after(pieces_c[2], got[1][1]))

    steps = others[::-1] + [[0]]
    sum_b = on_way_b = None
    (grad_first, norm_sums_a, frame_grads), got = back(
        normed_a, grad_second, kept_a, spatial, None, steps, sums_b,
        [first_flights, second_flights, third_flights, sums_a],
        (norm_gains[:1], first, grad_second), (F32,),
    )
    far_a = []
    if size == 4:
        far_a, on_way_b, last_c = got[2]
        on_way_c = jnp.concatenate([got[0][1], got[1][1], last_c], axis=1)
    else:
        sum_b, on_way_b = clips_first(*settle(sums_b, [], []))
        on_way_c = send_far_clips(sum_c)

    small = jnp.concatenate(
        [x[i : i + 1] for i in range(2) for x in (norm_sums_a, norm_sums_b, norm_sums_c)]
        + [jnp.dot(one_hot.T, frame_grads[::8], precision=lax.Precision.HIGHEST)],
        axis=0,
    )
    both_a = send_both(sums_a, far_a)
    sum_c, on_way_c = clips_last(sum_c, on_way_c)
    sum_b, on_way_b = clips_next(sum_b, on_way_b)
    small = over_all(small, [("dp", 1)])
    (small, sum_b, sum_c, sums_a[0]), (both_a, on_way_b, on_way_c) = hold(
        (small, sum_b, sum_c, sums_a[0]), (both_a, on_way_b, on_way_c)
    )
    sum_a, on_way_a = clips_first(*settle_both(sums_a, both_a))
    whole_c = clips_joined(sum_c, on_way_c)
    other_c = twin(whole_c)
    small = over_all(small, [("mp", x) for x in bits_of(size, False)])
    small = over_all(small, [("dp", x) for x in clip_offsets()[::-1]])
    (small, sum_a, sum_b, result), (on_way_a, other_c) = hold(
        (small, sum_a, sum_b, result), (on_way_a, other_c)
    )
    sum_a, on_way_a = clips_next(sum_a, on_way_a)
    sum_b, on_way_b = clips_last(sum_b, on_way_b)
    parts = send_frames(result)
    whole = both_halves(whole_c, other_c)
    grad_ff_in, grad_ff_out = whole[0].T, whole[1]
    (grad_ff_in, grad_ff_out, sum_a, sum_b), (on_way_a, on_way_b, parts) = hold(
        (grad_ff_in, grad_ff_out, sum_a, sum_b), (on_way_a, on_way_b, parts)
    )
    sum_a, on_way_a = clips_last(sum_a, on_way_a)
    whole_b = clips_joined(sum_b, on_way_b)
    grad_tqkv, grad_tout = attention_grads(both_halves(whole_b, twin(whole_b)))
    mixed = join_frames(parts)
    (grad_tqkv, grad_tout, mixed, sum_a), on_way_a = hold(
        (grad_tqkv, grad_tout, mixed, sum_a), on_way_a
    )
    whole_a = clips_joined(sum_a, on_way_a)
    grad_sqkv, grad_sout = attention_grads(both_halves(whole_a, twin(whole_a)))
    gains_sum, shifts_sum, table_sum = small[:3], small[3:6], small[6:]
    return (
        mixed,
        grad_first,
        table_sum,
        gains_sum,
        shifts_sum,
        grad_sqkv,
        grad_sout,
        grad_tqkv,
        grad_tout,
        grad_ff_in,
        grad_ff_out,
    )


def solution(mesh):
    return jax.shard_map(
        shards,
        mesh=mesh,
        in_specs=(
            P(("dp", "mp"), None),
            P("dp", None),
            P("dp"),
            P(),
            P(),
            P(),
            P(None, None, "mp"),
            P("mp", None),
            P(None, None, "mp"),
            P("mp", None),
            P(None, "mp"),
            P("mp", None),
            P(("dp", "mp"), None),
        ),
        out_specs=(
            P(("dp", "mp"), None),
            P(("dp", "mp"), None),
            P(),
            P(),
            P(),
            P(None, None, "mp"),
            P("mp", None),
            P(None, None, "mp"),
            P("mp", None),
            P(None, "mp"),
            P("mp", None),
        ),
        check_vma=False,
    )
```

```python
import functools

import jax
import jax.numpy as jnp
from jax import lax
from jax.experimental import pallas as pl
from jax.experimental.pallas import tpu as pltpu
from jax.sharding import PartitionSpec as P

D = 1024
HEAD_DIM = 64
FRAMES = 16
POS = 256
ACTIONS = 8
EPS = 1e-05
BLOCK = 256
GROUP = BLOCK // FRAMES
VMEM = 34 << 20
VMEM_LAST = 60 << 20
COST = 1
LSE_ROWS = 8
BF16 = jnp.bfloat16
F32 = jnp.float32


def norm_rows(hidden, gain_row, shift_row):
    average = jnp.mean(hidden, axis=-1, keepdims=True)
    centred = hidden - average
    inverse = lax.rsqrt(jnp.mean(centred * centred, axis=-1, keepdims=True) + EPS)
    scaled = centred * inverse
    return scaled * gain_row + shift_row, scaled, inverse


def norm_back(gradient, hidden, gain_row):
    _, scaled, inverse = norm_rows(hidden, 1.0, 0.0)
    grad_gain = jnp.sum(gradient * scaled, axis=0, keepdims=True)
    grad_shift = jnp.sum(gradient, axis=0, keepdims=True)
    inner = gradient * gain_row
    grad_in = inverse * (
        inner
        - jnp.mean(inner, axis=-1, keepdims=True)
        - scaled * jnp.mean(inner * scaled, axis=-1, keepdims=True)
    )
    return grad_in, grad_gain, grad_shift


def flip(values, offset, axis="mp"):
    size = lax.axis_size(axis)
    return lax.ppermute(values, axis, [(i, i ^ offset) for i in range(size)])


def twin(values):
    return flip(values, 1, "dp")


def bits_of(count, reverse):
    bits = [1 << b for b in range(count.bit_length() - 1)]
    return bits[::-1] if reverse else bits


def gather(piece, reverse, axis="mp", unit=1):
    slots = {0: piece}
    for bit in bits_of(lax.axis_size(axis) // unit, reverse):
        for slot in list(slots):
            slots[slot | bit] = flip(slots[slot], bit * unit, axis)
    return [slots[s] for s in range(len(slots))]


def add(left, right):
    return (left.astype(F32) + right.astype(F32)).astype(BF16)


def scatter_step(slots, bit, axis="mp", unit=1):
    return {
        s: add(value, flip(slots[s | bit], bit * unit, axis)) for s, value in slots.items() if not s & bit
    }


def scatter(slots, reverse, axis="mp", unit=1):
    slots = dict(slots)
    for bit in bits_of(lax.axis_size(axis) // unit, reverse):
        slots = scatter_step(slots, bit, axis, unit)
    return slots[0]


def clip_offsets():
    return [bit * 2 for bit in bits_of(lax.axis_size("dp") // 2, False)]


def even_clips():
    return lax.axis_index("dp") // 2 % 2 == 0


def clips_first(low, high):
    even = even_clips()
    return jnp.where(even, low, high), flip(jnp.where(even, high, low), clip_offsets()[0], "dp")


def clips_between(mine, arrived):
    mine = add(mine, arrived)
    for offset in clip_offsets()[1:-1]:
        mine = add(mine, flip(mine, offset, "dp"))
    return mine


def send_far_clips(mine):
    return flip(mine, clip_offsets()[-1], "dp")


def clips_next(mine, arrived):
    mine = clips_between(mine, arrived)
    return mine, send_far_clips(mine)


def clips_last(mine, arrived):
    mine = add(mine, arrived)
    return mine, flip(mine, clip_offsets()[0], "dp")


def clips_joined(mine, other):
    even = even_clips()
    return jnp.concatenate([jnp.where(even, mine, other), jnp.where(even, other, mine)], axis=0)


def over_all(values, steps):
    for axis, offset in steps:
        values = values + flip(values, offset, axis)
    return values


def send_positions(rows):
    me, size = lax.axis_index("mp"), lax.axis_size("mp")
    here = POS // size
    view = rows.reshape(rows.shape[0] // POS, POS, D)
    parts = []
    for slot in range(size):
        part = lax.dynamic_slice_in_dim(view, (me ^ slot) * here, here, axis=1)
        parts.append(flip(part, slot) if slot else part)
    return parts


def join_positions(parts):
    here = parts[0].shape[1]
    whole = jnp.concatenate(parts, axis=0).reshape(FRAMES, here // GROUP, GROUP, D)
    return whole.transpose(1, 0, 2, 3).reshape(FRAMES * here, D)


def send_frames(rows):
    size = lax.axis_size("mp")
    frames_here = FRAMES // size
    view = rows.reshape(rows.shape[0] // BLOCK, size, frames_here, GROUP, D)
    return [flip(view[:, slot], slot) if slot else view[:, slot] for slot in range(size)]


def join_frames(parts):
    me = lax.axis_index("mp")
    groups, frames_here = parts[0].shape[:2]
    here = groups * GROUP
    whole = jnp.zeros((frames_here, POS, D), parts[0].dtype)
    for slot, part in enumerate(parts):
        part = part.transpose(1, 0, 2, 3).reshape(frames_here, here, D)
        whole = lax.dynamic_update_slice_in_dim(whole, part, (me ^ slot) * here, axis=1)
    return whole.reshape(frames_here * POS, D)


def nn(left, right):
    return lax.dot_general(left, right, (((1,), (0,)), ((), ())), preferred_element_type=F32)


def nt(left, right):
    return lax.dot_general(left, right, (((1,), (1,)), ((), ())), preferred_element_type=F32)


def tn(left, right):
    return lax.dot_general(left, right, (((0,), (0,)), ((), ())), preferred_element_type=F32)


def flatten(slots):
    return jax.tree.leaves(slots), jax.tree.map(lambda x: 0, slots)


def whole_spec(array):
    return pl.BlockSpec(array.shape, lambda i: (0,) * array.ndim, pipeline_mode=pl.Buffered(1))


def rows_spec(width):
    return pl.BlockSpec((BLOCK, width), lambda i: (i, 0))


def columns_spec(height, index=0):
    return pl.BlockSpec((height, BLOCK), lambda i: (index, i))


def part_spec(shape, index):
    return pl.BlockSpec(shape, lambda i: (index, 0), pipeline_mode=pl.Buffered(1))


def rows_of(refs):
    return [ref.at[i] for ref in refs for i in range(ref.shape[0])]


def load_weights(slots, qkv, out):
    part = slots[0][0][0].shape[1]
    width = 2 * part

    @pl.when(pl.program_id(0) == 0)
    def _():
        for index, parts in enumerate(slots):
            for half, refs in enumerate(parts):
                *three, o = rows_of(refs)
                for which, ref in enumerate(three):
                    at = 3 * width * index + width * which + part * half
                    qkv[at : at + part, :] = ref[...]
                at = width * index + part * half
                out[at : at + part, :] = o[...]


def take(refs, shapes):
    return jax.tree.map(lambda _: refs.pop(0), shapes)


def heads_apart(rows):
    owner = lax.broadcasted_iota(jnp.int32, rows.shape, 0) // HEAD_DIM
    return jnp.concatenate(
        [jnp.where(owner == h, rows, 0).astype(BF16) for h in range(rows.shape[0] // HEAD_DIM)], axis=1
    )


def attend_kernel(masked, shapes, senders, *refs):
    refs = list(refs)
    mask = refs.pop(0) if masked else None
    if senders:
        norms = refs.pop(0)
        arrived = [refs.pop(0) for _ in range(senders)]
    else:
        n_ref = refs.pop(0)
    slots, count = take(refs, shapes), len(shapes)
    acc_ref = None if senders else refs.pop(0)
    out_ref, qkv_ref, ctx_ref, lse_ref = (refs.pop(0) for _ in range(4))
    if senders:
        h_ref, n_ref, next_ref = (refs.pop(0) for _ in range(3))
    w_qkv, w_out = refs
    if senders:
        hidden = jnp.concatenate([x[...].reshape(-1, D) for x in arrived], axis=0)
        h_ref[...] = hidden
        hidden = hidden.astype(F32)
        n_ref[...] = norm_rows(hidden, norms[0:1], norms[1:2])[0].astype(BF16)
    else:
        hidden = acc_ref[...]
    load_weights(slots, w_qkv, w_out)
    width = w_out.shape[0] // count
    heads = width // HEAD_DIM
    together = min(4, heads)
    group = together * HEAD_DIM
    for slot in range(count):
        base = 3 * width * slot
        qkv = nt(w_qkv[base : base + 3 * width, :], n_ref[...])
        qkv_ref[base : base + width, :] = (qkv[:width] * HEAD_DIM**-0.5).astype(BF16)
        qkv_ref[base + width : base + 3 * width, :] = qkv[width:].astype(BF16)
        keys = qkv[width : 2 * width].T.astype(BF16)
        for at in range(0, width, group):
            q = heads_apart(qkv_ref[base + at : base + at + group, :])
            logits = nn(keys[:, at : at + group], q)
            if masked:
                logits = logits + jnp.concatenate([mask[...]] * together, axis=1)
            highest = jnp.max(logits, axis=0, keepdims=True)
            raised = jnp.exp(logits - highest)
            total = jnp.sum(raised, axis=0, keepdims=True)
            log_total = highest + jnp.log(total)
            inverse = 1.0 / total
            raised = raised.astype(BF16)
            for head in range(together):
                columns = slice(head * BLOCK, (head + 1) * BLOCK)
                row = slot * LSE_ROWS + at // HEAD_DIM + head
                lse_ref[row : row + 1, :] = log_total[:, columns]
                start = base + 2 * width + at + head * HEAD_DIM
                values = qkv_ref[start : start + HEAD_DIM, :]
                start = slot * width + at + head * HEAD_DIM
                ctx_ref[start : start + HEAD_DIM, :] = (
                    nn(values, raised[:, columns]) * inverse[:, columns]
                ).astype(BF16)
    hidden = hidden + tn(ctx_ref[...], w_out[...])
    out_ref[...] = hidden.astype(out_ref.dtype)
    if senders:
        next_ref[...] = norm_rows(hidden, norms[2:3], norms[3:4])[0].astype(BF16)


def attend_slots(normed, slots, acc, mask, out_type=F32):
    return attend_call(normed.shape[0], [normed], slots, [acc], mask, [], out_type)


def attend_arrived(arrived, norms, slots, mask):
    rows = sum(x.shape[0] * x.shape[1] for x in arrived)
    return attend_call(rows, arrived, slots, [], mask, [norms], F32)


def attend_call(rows, inputs, slots, acc, mask, norms, out_type):
    flat, shapes = flatten(slots)
    width = len(slots) * 2 * flat[0].shape[1]
    lse_rows = LSE_ROWS * len(slots)
    first = ([] if mask is None else [mask]) + norms
    args = first + inputs + flat + acc
    arrived_spec = [pl.BlockSpec((x.shape[0], GROUP, D), lambda i: (0, i, 0)) for x in inputs]
    return pl.pallas_call(
        functools.partial(attend_kernel, mask is not None, shapes, len(inputs) if norms else 0),
        grid=(rows // BLOCK,),
        in_specs=[whole_spec(x) for x in first]
        + (arrived_spec if norms else [rows_spec(D)])
        + [whole_spec(x) for x in flat]
        + [rows_spec(D)] * len(acc),
        out_specs=[rows_spec(D), columns_spec(3 * width), columns_spec(width), columns_spec(lse_rows)]
        + [rows_spec(D)] * (3 * len(norms)),
        out_shape=[
            jax.ShapeDtypeStruct((rows, D), out_type),
            jax.ShapeDtypeStruct((3 * width, rows), BF16),
            jax.ShapeDtypeStruct((width, rows), BF16),
            jax.ShapeDtypeStruct((lse_rows, rows), F32),
        ]
        + [jax.ShapeDtypeStruct((rows, D), BF16)] * (3 * len(norms)),
        scratch_shapes=[pltpu.VMEM((3 * width, D), BF16), pltpu.VMEM((width, D), BF16)],
        compiler_params=pltpu.CompilerParams(vmem_limit_bytes=VMEM),
        cost_estimate=pl.CostEstimate(
            flops=2 * rows * D * width * 4 // COST, bytes_accessed=1 << 20, transcendentals=0
        ),
        name="attend",
    )(*args)


def finish(refs, gradient):
    gain, h_ref, past, *totals, sums, block_sums = refs

    @pl.when(pl.program_id(0) == 0)
    def _():
        sums[...] = jnp.zeros_like(sums)

    grad_in, grad_gain, grad_shift = norm_back(gradient, h_ref[...].astype(F32), gain[...])
    sums[0:1] += grad_gain
    sums[1:2] += grad_shift
    grad_in = past[...].astype(F32) + grad_in
    for total in totals:
        total[...] = grad_in.astype(total.dtype)
    block_sums[...] = jnp.broadcast_to(jnp.sum(grad_in, axis=0, keepdims=True), block_sums.shape)


def finish_specs(rows, types):
    steps = rows // BLOCK
    once = pl.BlockSpec((8, D), lambda i: (0, 0))
    return (
        [pl.BlockSpec((1, D), lambda i: (0, 0)), rows_spec(D), rows_spec(D)],
        [rows_spec(D)] * len(types) + [once, pl.BlockSpec((8, D), lambda i: (i, 0))],
        [jax.ShapeDtypeStruct((rows, D), t) for t in types]
        + [jax.ShapeDtypeStruct((8, D), F32), jax.ShapeDtypeStruct((8 * steps, D), F32)],
    )


def back_kernel(masked, shapes, steps, types, *refs):
    refs = list(refs)
    mask = refs.pop(0) if masked else None
    n_ref, g_ref, qkv_ref, ctx_ref, lse_ref = (refs.pop(0) for _ in range(5))
    slots, count = take(refs, shapes), len(shapes)
    acc_ref = refs.pop(0)
    last = [refs.pop(0) for _ in range(3)] if types else []
    last += [refs.pop(0) for _ in range(len(types) + 2 if types else 1)]
    grads = [refs.pop(0) for _ in range(2)]
    w_qkv, w_out, d_all = refs
    load_weights(slots, w_qkv, w_out)
    width = w_out.shape[0] // count
    heads = width // HEAD_DIM
    step = pl.program_id(0)
    rows = pl.ds(pl.multiple_of(step * BLOCK, BLOCK), BLOCK)
    together = min(4, heads)
    group = together * HEAD_DIM
    for slot in range(count):
        base = 3 * width * slot
        d_ctx = nt(w_out[slot * width : (slot + 1) * width, :], g_ref[rows, :]).astype(BF16)
        keys = qkv_ref[base + width : base + 2 * width, :].T
        values = qkv_ref[base + 2 * width : base + 3 * width, :].T
        for at in range(0, width, group):
            q = qkv_ref[base + at : base + at + group, :]
            d_group = d_ctx[at : at + group]
            logits = nn(keys[:, at : at + group], heads_apart(q))
            if masked:
                logits = logits + jnp.concatenate([mask[...]] * together, axis=1)
            d_p = nn(values[:, at : at + group], heads_apart(d_group))
            ctx = ctx_ref[slot * width + at : slot * width + at + group, rows]
            product = d_group.astype(F32) * ctx.astype(F32)
            split = [slice(h * HEAD_DIM, (h + 1) * HEAD_DIM) for h in range(together)]
            row = slot * LSE_ROWS + at // HEAD_DIM
            lse = jnp.concatenate([lse_ref[row + h : row + h + 1, :] for h in range(together)], axis=1)
            total = jnp.concatenate([jnp.sum(product[s], axis=0, keepdims=True) for s in split], axis=1)
            p = jnp.exp(logits - lse)
            ds = (p * (d_p - total)).astype(BF16)
            p = p.astype(BF16)
            for head in range(together):
                columns = slice(head * BLOCK, (head + 1) * BLOCK)
                start = base + at + head * HEAD_DIM
                key = qkv_ref[width + start : width + start + HEAD_DIM, :]
                d_all[start : start + HEAD_DIM, rows] = (
                    nn(key, ds[:, columns]) * HEAD_DIM**-0.5
                ).astype(BF16)
                start = start + width
                d_all[start : start + HEAD_DIM, rows] = nt(q[split[head]], ds[:, columns]).astype(BF16)
                start = start + width
                d_all[start : start + HEAD_DIM, rows] = nt(
                    d_group[split[head]], p[:, columns]
                ).astype(BF16)
    total = acc_ref[...] + tn(d_all[:, rows], w_qkv[...])
    if types:
        finish(last, total)
    else:
        last[0][...] = total

    @pl.when(step == steps - 1)
    def _():
        part = width // 2
        for at in range(0, D, BLOCK):
            columns = slice(at, at + BLOCK)
            d_w = nn(d_all[...], n_ref[:, columns]).astype(BF16)
            d_o = nn(ctx_ref[...], g_ref[:, columns]).astype(BF16)
            for index in range(count):
                for half, ref in enumerate(grads):
                    for which in range(3):
                        at = 3 * width * index + width * which + part * half
                        ref[4 * index + which, :, columns] = d_w[at : at + part]
                    at = width * index + part * half
                    ref[4 * index + 3, :, columns] = d_o[at : at + part]


def back_slots(normed, grad, kept, slots, acc, mask, last=(), types=()):
    rows = normed.shape[0]
    (qkv, ctx, lse), place = kept
    flat, shapes = flatten(slots)
    part = flat[0].shape[1]
    width = len(slots) * 2 * part
    grads = [jax.ShapeDtypeStruct((4 * len(slots), part, D), BF16)] * 2
    lse_rows, index = LSE_ROWS * len(slots), place // len(slots)
    masked = mask is not None
    first = [mask] if masked else []
    args = first + [normed, grad, qkv, ctx, lse] + flat + [acc] + list(last)
    taken, given, shapes_given = finish_specs(rows, types)
    if not types:
        taken, given, shapes_given = [], [rows_spec(D)], [jax.ShapeDtypeStruct((rows, D), F32)]
    out = pl.pallas_call(
        functools.partial(back_kernel, masked, shapes, rows // BLOCK, types),
        grid=(rows // BLOCK,),
        in_specs=[whole_spec(x) for x in first]
        + [whole_spec(normed), whole_spec(grad)]
        + [columns_spec(3 * width, index), part_spec((width, rows), index), columns_spec(lse_rows, index)]
        + [whole_spec(x) for x in flat]
        + [rows_spec(D)]
        + taken,
        out_specs=given + [whole_spec(x) for x in grads],
        out_shape=shapes_given + grads,
        scratch_shapes=[
            pltpu.VMEM((3 * width, D), BF16),
            pltpu.VMEM((width, D), BF16),
            pltpu.VMEM((3 * width, rows), BF16),
        ],
        compiler_params=pltpu.CompilerParams(vmem_limit_bytes=VMEM_LAST if types and masked else VMEM),
        cost_estimate=pl.CostEstimate(
            flops=4 * rows * D * width * 4 // COST, bytes_accessed=1 << 20, transcendentals=0
        ),
        name="attend_back",
    )(*args)
    return out[:-2] if types else out[0], out[-2:]


def gelu_both(u):
    c, cube = (2.0 / 3.141592653589793) ** 0.5, 0.044715
    square = u * u
    t = jnp.tanh(c * u * (1.0 + cube * square))
    half = 0.5 * (1.0 + t)
    return u * half, half + 0.5 * u * (1.0 - t * t) * (c + 3.0 * c * cube * square)


def ff_kernel(shapes, steps, types, *refs):
    refs = list(refs)
    n_ref, g_ref = refs.pop(0), refs.pop(0)
    pieces = [rows_of(x) for x in take(refs, shapes)]
    mix_ref, dn_ref = refs.pop(0), refs.pop(0)
    last = [refs.pop(0) for _ in range(3)] if types else []
    mix_out = refs.pop(0)
    last += [refs.pop(0) for _ in range(len(types) + 2 if types else 1)]
    grads = [rows_of([refs.pop(0)]) for _ in range(2)]
    hid_all, du_all = refs
    part = hid_all.shape[0] // 2
    step = pl.program_id(0)
    rows = pl.ds(pl.multiple_of(step * BLOCK, BLOCK), BLOCK)
    mix, dn = mix_ref[...], dn_ref[...]
    for index, (w_in, w_out) in enumerate(pieces):
        low = slice(index * part, (index + 1) * part)
        value, slope = gelu_both(nt(w_in[...], n_ref[rows, :]))
        hidden = value.astype(BF16)
        du = (slope * nt(w_out[...], g_ref[rows, :])).astype(BF16)
        hid_all[low, rows] = hidden
        du_all[low, rows] = du
        mix = mix + tn(hidden, w_out[...])
        dn = dn + tn(du, w_in[...])
    mix_out[...] = mix.astype(mix_out.dtype)
    if types:
        finish(last, dn)
    else:
        last[0][...] = dn

    @pl.when(step == steps - 1)
    def _():
        for at in range(0, D, BLOCK):
            columns = slice(at, at + BLOCK)
            for index, (d_in, d_out) in enumerate(grads):
                low = slice(index * part, (index + 1) * part)
                d_in[:, columns] = nn(du_all[low, :], n_ref[:, columns]).astype(BF16)
                d_out[:, columns] = nn(hid_all[low, :], g_ref[:, columns]).astype(BF16)


def ff_slot(normed, grad, pieces, mix, dn, last=(), types=()):
    rows = normed.shape[0]
    flat, shapes = flatten(pieces)
    part = flat[0].shape[1]
    width = 2 * part
    grads = [jax.ShapeDtypeStruct((2, part, D), BF16)] * 2
    taken, given, shapes_given = finish_specs(rows, types)
    if not types:
        taken, given, shapes_given = [], [rows_spec(D)], [jax.ShapeDtypeStruct((rows, D), F32)]
    out = pl.pallas_call(
        functools.partial(ff_kernel, shapes, rows // BLOCK, types),
        grid=(rows // BLOCK,),
        in_specs=[whole_spec(normed), whole_spec(grad)]
        + [whole_spec(x) for x in flat]
        + [rows_spec(D), rows_spec(D)]
        + taken,
        out_specs=[rows_spec(D)] + given + [whole_spec(x) for x in grads],
        out_shape=[jax.ShapeDtypeStruct((rows, D), BF16 if types else F32)] + shapes_given + grads,
        scratch_shapes=[pltpu.VMEM((width, rows), BF16), pltpu.VMEM((width, rows), BF16)],
        compiler_params=pltpu.CompilerParams(vmem_limit_bytes=VMEM),
        cost_estimate=pl.CostEstimate(
            flops=12 * rows * D * width // COST, bytes_accessed=1 << 20, transcendentals=0
        ),
        name="feed_forward",
    )(normed, grad, *flat, mix, dn, *last)
    return out[0], out[1:-2] if types else out[1], out[-2:]


def after(values, first):
    return lax.optimization_barrier((values, first))[0]


def hold(values, flights):
    return lax.optimization_barrier((values, flights))


def halves_of(array, axis):
    half = array.shape[axis] // 2
    core = lax.axis_index("dp") % 2
    return [
        lax.dynamic_slice_in_dim(array, at * half, half, axis=axis) for at in (core, 1 - core)
    ]


def attention_pieces(weight_qkv, weight_out):
    qkv = weight_qkv.transpose(0, 2, 1)
    whole = jnp.concatenate([qkv, weight_out[None]], axis=0)
    return halves_of(whole, 1)


def ff_pieces(weight_in, weight_out):
    return halves_of(jnp.stack([weight_in.T, weight_out]), 1)


def low_high(piece):
    half = piece.shape[0] // 2
    return [piece[:half], piece[half:]]


def near(piece):
    if lax.axis_size("mp") == 4:
        return {1: [flip(piece, 1)], 2: [flip(piece, 2)]}
    return {}


def far(piece, slots):
    size = lax.axis_size("mp")
    if size == 4:
        return {3: [flip(low_high(slots[1][0])[0], 2), flip(low_high(slots[2][0])[1], 1)]}
    low, high = low_high(piece)
    return {s: [x, y] for s, (x, y) in enumerate(zip(gather(low, False), gather(high, True))) if s}


def twins(arrays):
    return [twin(x) for x in arrays]


def pair_sums(grads, received):
    return [add(x, y) for x, y in zip(low_high(grads[0]), low_high(received))]


def send_far(sums):
    if lax.axis_size("mp") != 4:
        return []
    return [flip(sums[3][0], 1), flip(sums[3][1], 2)]


def send_plain(sums):
    if lax.axis_size("mp") != 4:
        return []
    return [flip(sums[1][0], 1), flip(sums[2][1], 2)]


def send_rest(sums, far_sums):
    if lax.axis_size("mp") != 4:
        return []
    low_two, high_one = far_sums
    return [flip(add(sums[1][1], high_one), 1), flip(add(sums[2][0], low_two), 2)]


def send_both(sums, far_sums):
    if lax.axis_size("mp") != 4:
        return []
    low_two, high_one = far_sums
    ahead = jnp.concatenate([sums[1][0], add(sums[1][1], high_one)], axis=0)
    across = jnp.concatenate([add(sums[2][0], low_two), sums[2][1]], axis=0)
    return [flip(ahead, 1), flip(across, 2)]


def settle_both(sums, both):
    if lax.axis_size("mp") != 4:
        return settle(sums, [], [])
    (low_one, high_one), (low_two, high_two) = low_high(both[0]), low_high(both[1])
    return settle(sums, [low_one, high_two], [high_one, low_two])


def settle(sums, plain, rest):
    if lax.axis_size("mp") != 4:
        return [scatter({s: x[i] for s, x in sums.items()}, bool(i)) for i in range(2)]
    terms = [(sums[0][0], plain[0], rest[1]), (sums[0][1], plain[1], rest[0])]
    return [sum(x.astype(F32) for x in three).astype(BF16) for three in terms]


def halves_kernel(core, mine, other, transposed, straight):
    count, half = mine.shape[0] - 1, mine.shape[1]
    first = core[0] == 0
    for which in range(count + 1):
        parts = [x[which].astype(F32) for x in (mine, other)]
        parts = [jnp.where(first, *parts), jnp.where(first, *parts[::-1])]
        if which < count:
            transposed[which] = jnp.concatenate([x.T for x in parts], axis=1)
        else:
            for at, part in enumerate(parts):
                straight[at * half : (at + 1) * half, :] = part


def both_halves(mine, other):
    count, half = mine.shape[0] - 1, mine.shape[1]
    taken = pl.BlockSpec((count + 1, half, BLOCK), lambda i: (0, 0, i))
    return pl.pallas_call(
        halves_kernel,
        grid=(D // BLOCK,),
        in_specs=[pl.BlockSpec(memory_space=pltpu.SMEM), taken, taken],
        out_specs=[
            pl.BlockSpec((count, BLOCK, 2 * half), lambda i: (0, i, 0)),
            pl.BlockSpec((2 * half, BLOCK), lambda i: (0, i)),
        ],
        out_shape=[
            jax.ShapeDtypeStruct((count, D, 2 * half), F32),
            jax.ShapeDtypeStruct((2 * half, D), F32),
        ],
        compiler_params=pltpu.CompilerParams(vmem_limit_bytes=VMEM),
        cost_estimate=pl.CostEstimate(flops=1 << 20, bytes_accessed=1 << 20, transcendentals=0),
        name="halves",
    )((lax.axis_index("dp") % 2).reshape(1), mine, other)


def shards(
    tokens,
    action_ids,
    clip_lengths,
    action_table,
    norm_gains,
    norm_shifts,
    spatial_qkv,
    spatial_out,
    temporal_qkv,
    temporal_out,
    ff_in,
    ff_out,
    out_grad,
):
    rows_here = tokens.shape[0]
    frames_here = rows_here // POS
    me, size = lax.axis_index("mp"), lax.axis_size("mp")
    frame_ids = lax.dynamic_slice_in_dim(action_ids.reshape(-1), me * frames_here, frames_here)
    one_hot = (
        frame_ids[:, None] == lax.broadcasted_iota(jnp.int32, (frames_here, ACTIONS), 1)
    ).astype(F32)
    per_frame = jnp.dot(one_hot, action_table, precision=lax.Precision.HIGHEST)
    embedded = jnp.broadcast_to(per_frame[:, None, :], (frames_here, POS, D)).reshape(rows_here, D)

    row = jnp.arange(BLOCK)
    frame_of = ((row // GROUP // frames_here) ^ me) * frames_here + row // GROUP % frames_here
    allowed = (
        (row[:, None] % GROUP == row[None] % GROUP)
        & (frame_of[:, None] <= frame_of[None])
        & (frame_of[:, None] < clip_lengths[0])
    )
    mask = jnp.where(allowed, 0.0, -1e9).astype(F32)

    others = [[1, 2], [3]] if size == 4 else [list(range(1, size))]

    own, other = attention_pieces(spatial_qkv, spatial_out)
    close = near(own)
    first = tokens.astype(F32) + embedded
    normed_a = norm_rows(first, norm_gains[0], norm_shifts[0])[0].astype(BF16)
    temporal_own, temporal_other = attention_pieces(*after((temporal_qkv, temporal_out), normed_a))
    spatial = {0: [[own], [other]]}
    kept_a = {}
    second, *kept = attend_slots(normed_a, [spatial[0]], first, None)
    kept_a[0] = (kept, 0)
    (second, temporal_own, temporal_other), close = hold((second, temporal_own, temporal_other), close)
    distant = far(own, close)
    near_b = near(temporal_own)
    close = {s: [x, twins(x)] for s, x in close.items()}
    second, close = hold(second, close)
    if close:
        spatial |= close
        second, *kept = attend_slots(normed_a, [spatial[s] for s in others[0]], second, None)
        kept_a[1] = (kept, 0)
    second, distant = hold(second, distant)
    distant = {s: [x, twins(x)] for s, x in distant.items()}
    second, distant = hold(second, distant)
    spatial |= distant
    second, *kept = attend_slots(normed_a, [spatial[s] for s in others[-1]], second, None, BF16)
    kept_a[3] = (kept, 0)
    second, near_b = hold(second, near_b)

    distant = far(temporal_own, near_b)
    near_b = {s: [x, twins(x)] for s, x in near_b.items()}
    parts = send_positions(second)
    own, other = ff_pieces(*after((ff_in, ff_out), parts[0]))
    parts, (own, other, near_b, distant) = hold(parts, (own, other, near_b, distant))
    grad_parts = send_positions(after(out_grad, parts))
    distant = {s: [x, twins(x)] for s, x in distant.items()}
    (parts, own, other), distant = hold((parts, own, other), distant)
    close = near(own)
    temporal = {0: [[temporal_own], [temporal_other]]} | near_b | distant
    order_b = [s for group in others for s in group] + [0]
    norms = jnp.concatenate([norm_gains[1:2], norm_shifts[1:2], norm_gains[2:], norm_shifts[2:]], axis=0)
    third, *kept, second, normed_b, normed_c = attend_arrived(
        parts, norms, [temporal[s] for s in order_b], mask
    )
    kept_b = [(kept, 0), (kept, 2)] if size == 4 else [(kept, 0), (kept, size - 1)]
    (third, normed_c), grad_parts = hold((third, normed_c), grad_parts)

    grad_result = join_positions(grad_parts)
    result, grad_normed = third, jnp.zeros((rows_here, D), F32)
    grads = {}

    def feed(slot, pieces, flights):
        nonlocal result, grad_normed
        last, types = ((norm_gains[2:], third, grad_result), (F32, BF16)) if slot == size - 1 else ((), ())
        result, grad_normed, grads[slot] = ff_slot(
            normed_c, grad_result, pieces, result, grad_normed, last, types
        )
        (result, grad_normed, grads[slot]), flights = hold((result, grad_normed, grads[slot]), flights)
        return flights

    def swap(slots):
        return {s: twin(grads[s][1]) for s in slots}

    received, sums_c, plain_c = {}, {}, []

    def sum_up(*slots):
        for s in slots:
            sums_c[s] = pair_sums(grads[s], received[s])

    if size == 4:
        close = feed(0, [[own], [other]], close)
        distant = far(own, close)
        twin_one, twin_two = twins(close[1]), twins(close[2])
        result, twin_one = hold(result, twin_one)
        distant, twin_two, got = feed(1, [close[1], twin_one], (distant, twin_two, swap([0])))
        received |= got
        twin_three, got = feed(2, [close[2], twin_two], (twins(distant[3]), swap([1])))
        received |= got | swap([2])
        sum_up(0, 1, 2)
        result, (sums_c[1][0], sums_c[2][1]) = hold(result, (sums_c[1][0], sums_c[2][1]))
        plain_c = feed(3, [distant[3], twin_three], send_plain(sums_c))
    else:
        distant = feed(0, [[own], [other]], far(own, close))
        for slot in range(1, size):
            feed(slot, [distant[slot], twins(distant[slot])], [])
        received = swap(range(size - 1))
        sum_up(*range(size - 1))
    received |= swap([size - 1])
    sum_up(size - 1)
    grad_third, grad_sent, norm_sums_c, _ = grad_normed

    def back(normed, gradient, kept, slots, mask, steps, sums, plans, last, types):
        mine, received, got, sums_here = {}, {}, [], plans[-1]
        total = jnp.zeros((rows_here, D), F32)
        if size == 4:
            total, sums[3] = hold(total, sums[3])
        swapped = {}
        for at, group in enumerate(steps):
            flights = plans[at](sums, got) if size == 4 else []
            end = (last, types) if at == len(steps) - 1 else ()
            total, found = back_slots(
                normed, gradient, kept[at], [slots[s] for s in group], total, mask, *end
            )
            (total, found), (flights, swapped) = hold((total, found), (flights, swapped))
            for place, s in enumerate(swapped and steps[at - 1]):
                one = slice(4 * place, 4 * place + 4)
                sums_here[s] = pair_sums([mine[at - 1][one]], swapped[0][one])
            mine[at] = found[0]
            swapped = [twin(found[1])]
            got.append(flights)
        for place, s in enumerate(steps[-1]):
            one = slice(4 * place, 4 * place + 4)
            sums_here[s] = pair_sums([found[0][one]], swapped[0][one])
        return total, got

    sums_b, sums_a = {}, {}
    (grad_second, norm_sums_b, _), got = back(
        normed_b, grad_sent, kept_b, temporal, mask, [[1, 2], [3, 0]] if size == 4 else others + [[0]], sums_c,
        [lambda sums, got: send_far(sums), lambda sums, got: send_rest(sums, got[0]), sums_b],
        (norm_gains[1:2], second, grad_third), (BF16,),
    )
    rest_c = got[1] if size == 4 else []
    parts = send_frames(grad_second)
    sum_c, on_way_c = clips_first(*settle(sums_c, plain_c, rest_c))
    (parts, sum_c, sums_b), on_way_c = hold((parts, sum_c, sums_b), on_way_c)
    sum_c = clips_between(sum_c, on_way_c)
    grad_second = join_frames(parts)
    cut = sum_c.shape[1] * 3 // 8
    pieces_c = [sum_c[:, :cut], sum_c[:, cut:]]

    def first_flights(sums, got):
        return send_far(sums), send_far_clips(pieces_c[0])

    def second_flights(sums, got):
        return send_both(sums, got[0][0]), send_far_clips(after(pieces_c[1], got[0][1]))

    def third_flights(sums, got):
        nonlocal sum_c
        sum_c, on_way = clips_last(sum_c, jnp.concatenate([got[0][1], got[1][1]], axis=1))
        return send_far(sums_a), on_way

    steps = others[::-1] + [[0]]
    kept_a = [kept_a[3], kept_a[1], kept_a[0]] if size == 4 else [kept_a[3], kept_a[0]]
    (grad_first, norm_sums_a, frame_grads), got = back(
        normed_a, grad_second, kept_a, spatial, None, steps, sums_b,
        [first_flights, second_flights, third_flights, sums_a],
        (norm_gains[:1], first, grad_second), (F32,),
    )
    if size == 4:
        far_a, on_way_c = got[2]
        both_b = got[1][0]
    else:
        far_a = both_b = []
        sum_c, on_way_c = clips_last(sum_c, send_far_clips(sum_c))

    small = jnp.concatenate(
        [x[i : i + 1] for i in range(2) for x in (norm_sums_a, norm_sums_b, norm_sums_c)]
        + [jnp.dot(one_hot.T, frame_grads[::8], precision=lax.Precision.HIGHEST)],
        axis=0,
    )
    both_a = send_both(sums_a, far_a)
    sum_b, on_way_b = clips_first(*settle_both(sums_b, both_b))
    sum_b = clips_between(sum_b, on_way_b)
    cut = sum_b.shape[1] // 2
    first_b = send_far_clips(sum_b[:, :cut])
    small = over_all(small, [("dp", 1)])
    (small, sum_b, sums_a[0]), (both_a, first_b) = hold((small, sum_b, sums_a[0]), (both_a, first_b))
    sum_a, on_way_a = clips_first(*settle_both(sums_a, both_a))
    last_b = send_far_clips(sum_b[:, cut:])
    whole_c = clips_joined(sum_c, on_way_c)
    other_c = twin(whole_c)
    small = over_all(small, [("mp", x) for x in bits_of(size, False)])
    small = over_all(small, [("dp", x) for x in clip_offsets()[1:]])
    (small, sum_a, sum_b, result), (on_way_a, other_c, last_b) = hold(
        (small, sum_a, sum_b, result), (on_way_a, other_c, last_b)
    )
    sum_a, on_way_a = clips_next(sum_a, on_way_a)
    sum_b, on_way_b = clips_last(sum_b, jnp.concatenate([first_b, last_b], axis=1))
    parts = send_frames(result)
    grad_ff_in, grad_ff_out = both_halves(whole_c, other_c)
    (grad_ff_in, grad_ff_out, sum_a, sum_b), (on_way_a, on_way_b, parts) = hold(
        (grad_ff_in, grad_ff_out, sum_a, sum_b), (on_way_a, on_way_b, parts)
    )
    sum_a, on_way_a = clips_last(sum_a, on_way_a)
    whole_b = clips_joined(sum_b, on_way_b)
    grad_tqkv, grad_tout = both_halves(whole_b, twin(whole_b))
    mixed = join_frames(parts)
    small = over_all(after(small, sum_a), [("dp", clip_offsets()[0])])
    (small, grad_tqkv, grad_tout, mixed, sum_a), on_way_a = hold(
        (small, grad_tqkv, grad_tout, mixed, sum_a), on_way_a
    )
    whole_a = clips_joined(sum_a, on_way_a)
    grad_sqkv, grad_sout = both_halves(whole_a, twin(whole_a))
    grad_ff_in = grad_ff_in[0]
    gains_sum, shifts_sum, table_sum = small[:3], small[3:6], small[6:]
    return (
        mixed,
        grad_first,
        table_sum,
        gains_sum,
        shifts_sum,
        grad_sqkv,
        grad_sout,
        grad_tqkv,
        grad_tout,
        grad_ff_in,
        grad_ff_out,
    )


def solution(mesh):
    return jax.shard_map(
        shards,
        mesh=mesh,
        in_specs=(
            P(("dp", "mp"), None),
            P("dp", None),
            P("dp"),
            P(),
            P(),
            P(),
            P(None, None, "mp"),
            P("mp", None),
            P(None, None, "mp"),
            P("mp", None),
            P(None, "mp"),
            P("mp", None),
            P(("dp", "mp"), None),
        ),
        out_specs=(
            P(("dp", "mp"), None),
            P(("dp", "mp"), None),
            P(),
            P(),
            P(),
            P(None, None, "mp"),
            P("mp", None),
            P(None, None, "mp"),
            P("mp", None),
            P(None, "mp"),
            P("mp", None),
        ),
        check_vma=False,
    )
```

```python
import functools

import jax
import jax.numpy as jnp
from jax import lax
from jax.experimental import pallas as pl
from jax.experimental.pallas import tpu as pltpu
from jax.sharding import PartitionSpec as P

D = 1024
HEAD_DIM = 64
FRAMES = 16
POS = 256
ACTIONS = 8
EPS = 1e-05
BLOCK = 256
GROUP = BLOCK // FRAMES
VMEM = 34 << 20
VMEM_LAST = 60 << 20
COST = 1
LSE_ROWS = 8
BF16 = jnp.bfloat16
F32 = jnp.float32


def norm_rows(hidden, gain_row, shift_row):
    average = jnp.mean(hidden, axis=-1, keepdims=True)
    centred = hidden - average
    inverse = lax.rsqrt(jnp.mean(centred * centred, axis=-1, keepdims=True) + EPS)
    scaled = centred * inverse
    return scaled * gain_row + shift_row, scaled, inverse


def norm_back(gradient, hidden, gain_row):
    _, scaled, inverse = norm_rows(hidden, 1.0, 0.0)
    grad_gain = jnp.sum(gradient * scaled, axis=0, keepdims=True)
    grad_shift = jnp.sum(gradient, axis=0, keepdims=True)
    inner = gradient * gain_row
    grad_in = inverse * (
        inner
        - jnp.mean(inner, axis=-1, keepdims=True)
        - scaled * jnp.mean(inner * scaled, axis=-1, keepdims=True)
    )
    return grad_in, grad_gain, grad_shift


def flip(values, offset, axis="mp"):
    size = lax.axis_size(axis)
    return lax.ppermute(values, axis, [(i, i ^ offset) for i in range(size)])


def twin(values):
    return flip(values, 1, "dp")


def bits_of(count, reverse):
    bits = [1 << b for b in range(count.bit_length() - 1)]
    return bits[::-1] if reverse else bits


def gather(piece, reverse, axis="mp", unit=1):
    slots = {0: piece}
    for bit in bits_of(lax.axis_size(axis) // unit, reverse):
        for slot in list(slots):
            slots[slot | bit] = flip(slots[slot], bit * unit, axis)
    return [slots[s] for s in range(len(slots))]


def add(left, right):
    return left + right


def scatter_step(slots, bit, axis="mp", unit=1):
    return {
        s: add(value, flip(slots[s | bit], bit * unit, axis)) for s, value in slots.items() if not s & bit
    }


def scatter(slots, reverse, axis="mp", unit=1):
    slots = dict(slots)
    for bit in bits_of(lax.axis_size(axis) // unit, reverse):
        slots = scatter_step(slots, bit, axis, unit)
    return slots[0]


def clip_offsets():
    return [bit * 2 for bit in bits_of(lax.axis_size("dp") // 2, False)]


def even_clips():
    return lax.axis_index("dp") // 2 % 2 == 0


def clips_first(low, high):
    even = even_clips()
    return jnp.where(even, low, high), flip(jnp.where(even, high, low), clip_offsets()[0], "dp")


def clips_between(mine, arrived):
    mine = add(mine, arrived)
    for offset in clip_offsets()[1:-1]:
        mine = add(mine, flip(mine, offset, "dp"))
    return mine


def send_far_clips(mine):
    return flip(mine, clip_offsets()[-1], "dp")


def clips_next(mine, arrived):
    mine = clips_between(mine, arrived)
    return mine, send_far_clips(mine)


def clips_last(mine, arrived):
    mine = add(mine, arrived)
    return mine, flip(mine, clip_offsets()[0], "dp")


def clips_joined(mine, other):
    even = even_clips()
    return jnp.concatenate([jnp.where(even, mine, other), jnp.where(even, other, mine)], axis=0)


def over_all(values, steps):
    for axis, offset in steps:
        values = values + flip(values, offset, axis)
    return values


def send_positions(rows):
    me, size = lax.axis_index("mp"), lax.axis_size("mp")
    here = POS // size
    view = rows.reshape(rows.shape[0] // POS, POS, D)
    parts = []
    for slot in range(size):
        part = lax.dynamic_slice_in_dim(view, (me ^ slot) * here, here, axis=1)
        parts.append(flip(part, slot) if slot else part)
    return parts


def join_positions(parts):
    here = parts[0].shape[1]
    whole = jnp.concatenate(parts, axis=0).reshape(FRAMES, here // GROUP, GROUP, D)
    return whole.transpose(1, 0, 2, 3).reshape(FRAMES * here, D)


def send_frames(rows):
    size = lax.axis_size("mp")
    frames_here = FRAMES // size
    view = rows.reshape(rows.shape[0] // BLOCK, size, frames_here, GROUP, D)
    return [flip(view[:, slot], slot) if slot else view[:, slot] for slot in range(size)]


def join_frames(parts):
    me = lax.axis_index("mp")
    groups, frames_here = parts[0].shape[:2]
    here = groups * GROUP
    whole = jnp.zeros((frames_here, POS, D), parts[0].dtype)
    for slot, part in enumerate(parts):
        part = part.transpose(1, 0, 2, 3).reshape(frames_here, here, D)
        whole = lax.dynamic_update_slice_in_dim(whole, part, (me ^ slot) * here, axis=1)
    return whole.reshape(frames_here * POS, D)


def nn(left, right):
    return lax.dot_general(left, right, (((1,), (0,)), ((), ())), preferred_element_type=F32)


def nt(left, right):
    return lax.dot_general(left, right, (((1,), (1,)), ((), ())), preferred_element_type=F32)


def tn(left, right):
    return lax.dot_general(left, right, (((0,), (0,)), ((), ())), preferred_element_type=F32)


def flatten(slots):
    return jax.tree.leaves(slots), jax.tree.map(lambda x: 0, slots)


def whole_spec(array):
    return pl.BlockSpec(array.shape, lambda i: (0,) * array.ndim, pipeline_mode=pl.Buffered(1))


def rows_spec(width):
    return pl.BlockSpec((BLOCK, width), lambda i: (i, 0))


def columns_spec(height, index=0):
    return pl.BlockSpec((height, BLOCK), lambda i: (index, i))


def part_spec(shape, index):
    return pl.BlockSpec(shape, lambda i: (index, 0), pipeline_mode=pl.Buffered(1))


def rows_of(refs):
    return [ref.at[i] for ref in refs for i in range(ref.shape[0])]


def load_weights(slots, qkv, out):
    part = slots[0][0][0].shape[1]
    width = 2 * part

    @pl.when(pl.program_id(0) == 0)
    def _():
        for index, parts in enumerate(slots):
            for half, refs in enumerate(parts):
                *three, o = rows_of(refs)
                for which, ref in enumerate(three):
                    at = 3 * width * index + width * which + part * half
                    qkv[at : at + part, :] = ref[...]
                at = width * index + part * half
                out[at : at + part, :] = o[...]


def take(refs, shapes):
    return jax.tree.map(lambda _: refs.pop(0), shapes)


def heads_apart(rows):
    owner = lax.broadcasted_iota(jnp.int32, rows.shape, 0) // HEAD_DIM
    return jnp.concatenate(
        [jnp.where(owner == h, rows, 0).astype(BF16) for h in range(rows.shape[0] // HEAD_DIM)], axis=1
    )


def attend_kernel(masked, shapes, senders, *refs):
    refs = list(refs)
    mask = refs.pop(0) if masked else None
    if senders:
        norms = refs.pop(0)
        arrived = [refs.pop(0) for _ in range(senders)]
    else:
        n_ref = refs.pop(0)
    slots, count = take(refs, shapes), len(shapes)
    acc_ref = None if senders else refs.pop(0)
    out_ref, qkv_ref, ctx_ref, lse_ref = (refs.pop(0) for _ in range(4))
    if senders:
        h_ref, n_ref, next_ref = (refs.pop(0) for _ in range(3))
    w_qkv, w_out = refs
    if senders:
        hidden = jnp.concatenate([x[...].reshape(-1, D) for x in arrived], axis=0)
        h_ref[...] = hidden
        hidden = hidden.astype(F32)
        n_ref[...] = norm_rows(hidden, norms[0:1], norms[1:2])[0].astype(BF16)
    else:
        hidden = acc_ref[...]
    load_weights(slots, w_qkv, w_out)
    width = w_out.shape[0] // count
    heads = width // HEAD_DIM
    together = min(4, heads)
    group = together * HEAD_DIM
    for slot in range(count):
        base = 3 * width * slot
        qkv = nt(w_qkv[base : base + 3 * width, :], n_ref[...])
        qkv_ref[base : base + width, :] = (qkv[:width] * HEAD_DIM**-0.5).astype(BF16)
        qkv_ref[base + width : base + 3 * width, :] = qkv[width:].astype(BF16)
        keys = qkv[width : 2 * width].T.astype(BF16)
        for at in range(0, width, group):
            q = heads_apart(qkv_ref[base + at : base + at + group, :])
            logits = nn(keys[:, at : at + group], q)
            if masked:
                logits = logits + jnp.concatenate([mask[...]] * together, axis=1)
            highest = jnp.max(logits, axis=0, keepdims=True)
            raised = jnp.exp(logits - highest)
            total = jnp.sum(raised, axis=0, keepdims=True)
            log_total = highest + jnp.log(total)
            inverse = 1.0 / total
            raised = raised.astype(BF16)
            for head in range(together):
                columns = slice(head * BLOCK, (head + 1) * BLOCK)
                row = slot * LSE_ROWS + at // HEAD_DIM + head
                lse_ref[row : row + 1, :] = log_total[:, columns]
                start = base + 2 * width + at + head * HEAD_DIM
                values = qkv_ref[start : start + HEAD_DIM, :]
                start = slot * width + at + head * HEAD_DIM
                ctx_ref[start : start + HEAD_DIM, :] = (
                    nn(values, raised[:, columns]) * inverse[:, columns]
                ).astype(BF16)
    hidden = hidden + tn(ctx_ref[...], w_out[...])
    out_ref[...] = hidden.astype(out_ref.dtype)
    if senders:
        next_ref[...] = norm_rows(hidden, norms[2:3], norms[3:4])[0].astype(BF16)


def attend_slots(normed, slots, acc, mask, out_type=F32):
    return attend_call(normed.shape[0], [normed], slots, [acc], mask, [], out_type)


def attend_arrived(arrived, norms, slots, mask):
    rows = sum(x.shape[0] * x.shape[1] for x in arrived)
    return attend_call(rows, arrived, slots, [], mask, [norms], F32)


def attend_call(rows, inputs, slots, acc, mask, norms, out_type):
    flat, shapes = flatten(slots)
    width = len(slots) * 2 * flat[0].shape[1]
    lse_rows = LSE_ROWS * len(slots)
    first = ([] if mask is None else [mask]) + norms
    args = first + inputs + flat + acc
    arrived_spec = [pl.BlockSpec((x.shape[0], GROUP, D), lambda i: (0, i, 0)) for x in inputs]
    return pl.pallas_call(
        functools.partial(attend_kernel, mask is not None, shapes, len(inputs) if norms else 0),
        grid=(rows // BLOCK,),
        in_specs=[whole_spec(x) for x in first]
        + (arrived_spec if norms else [rows_spec(D)])
        + [whole_spec(x) for x in flat]
        + [rows_spec(D)] * len(acc),
        out_specs=[rows_spec(D), columns_spec(3 * width), columns_spec(width), columns_spec(lse_rows)]
        + [rows_spec(D)] * (3 * len(norms)),
        out_shape=[
            jax.ShapeDtypeStruct((rows, D), out_type),
            jax.ShapeDtypeStruct((3 * width, rows), BF16),
            jax.ShapeDtypeStruct((width, rows), BF16),
            jax.ShapeDtypeStruct((lse_rows, rows), F32),
        ]
        + [jax.ShapeDtypeStruct((rows, D), BF16)] * (3 * len(norms)),
        scratch_shapes=[pltpu.VMEM((3 * width, D), BF16), pltpu.VMEM((width, D), BF16)],
        compiler_params=pltpu.CompilerParams(vmem_limit_bytes=VMEM),
        cost_estimate=pl.CostEstimate(
            flops=2 * rows * D * width * 4 // COST, bytes_accessed=1 << 20, transcendentals=0
        ),
        name="attend",
    )(*args)


def finish(refs, gradient):
    gain, h_ref, past, *totals, sums, block_sums = refs

    @pl.when(pl.program_id(0) == 0)
    def _():
        sums[...] = jnp.zeros_like(sums)

    grad_in, grad_gain, grad_shift = norm_back(gradient, h_ref[...].astype(F32), gain[...])
    sums[0:1] += grad_gain
    sums[1:2] += grad_shift
    grad_in = past[...].astype(F32) + grad_in
    for total in totals:
        total[...] = grad_in.astype(total.dtype)
    block_sums[...] = jnp.broadcast_to(jnp.sum(grad_in, axis=0, keepdims=True), block_sums.shape)


def finish_specs(rows, types):
    steps = rows // BLOCK
    once = pl.BlockSpec((8, D), lambda i: (0, 0))
    return (
        [pl.BlockSpec((1, D), lambda i: (0, 0)), rows_spec(D), rows_spec(D)],
        [rows_spec(D)] * len(types) + [once, pl.BlockSpec((8, D), lambda i: (i, 0))],
        [jax.ShapeDtypeStruct((rows, D), t) for t in types]
        + [jax.ShapeDtypeStruct((8, D), F32), jax.ShapeDtypeStruct((8 * steps, D), F32)],
    )


def back_kernel(masked, shapes, steps, types, *refs):
    refs = list(refs)
    mask = refs.pop(0) if masked else None
    n_ref, g_ref, qkv_ref, ctx_ref, lse_ref = (refs.pop(0) for _ in range(5))
    slots, count = take(refs, shapes), len(shapes)
    acc_ref = refs.pop(0)
    last = [refs.pop(0) for _ in range(3)] if types else []
    last += [refs.pop(0) for _ in range(len(types) + 2 if types else 1)]
    grads = [refs.pop(0) for _ in range(2)]
    w_qkv, w_out, d_all = refs
    load_weights(slots, w_qkv, w_out)
    width = w_out.shape[0] // count
    heads = width // HEAD_DIM
    step = pl.program_id(0)
    rows = pl.ds(pl.multiple_of(step * BLOCK, BLOCK), BLOCK)
    together = min(4, heads)
    group = together * HEAD_DIM
    for slot in range(count):
        base = 3 * width * slot
        d_ctx = nt(w_out[slot * width : (slot + 1) * width, :], g_ref[rows, :]).astype(BF16)
        keys = qkv_ref[base + width : base + 2 * width, :].T
        values = qkv_ref[base + 2 * width : base + 3 * width, :].T
        for at in range(0, width, group):
            q = qkv_ref[base + at : base + at + group, :]
            d_group = d_ctx[at : at + group]
            logits = nn(keys[:, at : at + group], heads_apart(q))
            if masked:
                logits = logits + jnp.concatenate([mask[...]] * together, axis=1)
            d_p = nn(values[:, at : at + group], heads_apart(d_group))
            ctx = ctx_ref[slot * width + at : slot * width + at + group, rows]
            product = d_group.astype(F32) * ctx.astype(F32)
            split = [slice(h * HEAD_DIM, (h + 1) * HEAD_DIM) for h in range(together)]
            row = slot * LSE_ROWS + at // HEAD_DIM
            lse = jnp.concatenate([lse_ref[row + h : row + h + 1, :] for h in range(together)], axis=1)
            total = jnp.concatenate([jnp.sum(product[s], axis=0, keepdims=True) for s in split], axis=1)
            p = jnp.exp(logits - lse)
            ds = (p * (d_p - total)).astype(BF16)
            p = p.astype(BF16)
            for head in range(together):
                columns = slice(head * BLOCK, (head + 1) * BLOCK)
                start = base + at + head * HEAD_DIM
                key = qkv_ref[width + start : width + start + HEAD_DIM, :]
                d_all[start : start + HEAD_DIM, rows] = (
                    nn(key, ds[:, columns]) * HEAD_DIM**-0.5
                ).astype(BF16)
                start = start + width
                d_all[start : start + HEAD_DIM, rows] = nt(q[split[head]], ds[:, columns]).astype(BF16)
                start = start + width
                d_all[start : start + HEAD_DIM, rows] = nt(
                    d_group[split[head]], p[:, columns]
                ).astype(BF16)
    total = acc_ref[...] + tn(d_all[:, rows], w_qkv[...])
    if types:
        finish(last, total)
    else:
        last[0][...] = total

    @pl.when(step == steps - 1)
    def _():
        part = width // 2
        for at in range(0, D, BLOCK):
            columns = slice(at, at + BLOCK)
            d_w = nn(d_all[...], n_ref[:, columns]).astype(BF16)
            d_o = nn(ctx_ref[...], g_ref[:, columns]).astype(BF16)
            for index in range(count):
                for half, ref in enumerate(grads):
                    for which in range(3):
                        at = 3 * width * index + width * which + part * half
                        ref[4 * index + which, :, columns] = d_w[at : at + part]
                    at = width * index + part * half
                    ref[4 * index + 3, :, columns] = d_o[at : at + part]


def back_slots(normed, grad, kept, slots, acc, mask, last=(), types=()):
    rows = normed.shape[0]
    (qkv, ctx, lse), place = kept
    flat, shapes = flatten(slots)
    part = flat[0].shape[1]
    width = len(slots) * 2 * part
    grads = [jax.ShapeDtypeStruct((4 * len(slots), part, D), BF16)] * 2
    lse_rows, index = LSE_ROWS * len(slots), place // len(slots)
    masked = mask is not None
    first = [mask] if masked else []
    args = first + [normed, grad, qkv, ctx, lse] + flat + [acc] + list(last)
    taken, given, shapes_given = finish_specs(rows, types)
    if not types:
        taken, given, shapes_given = [], [rows_spec(D)], [jax.ShapeDtypeStruct((rows, D), F32)]
    out = pl.pallas_call(
        functools.partial(back_kernel, masked, shapes, rows // BLOCK, types),
        grid=(rows // BLOCK,),
        in_specs=[whole_spec(x) for x in first]
        + [whole_spec(normed), whole_spec(grad)]
        + [columns_spec(3 * width, index), part_spec((width, rows), index), columns_spec(lse_rows, index)]
        + [whole_spec(x) for x in flat]
        + [rows_spec(D)]
        + taken,
        out_specs=given + [whole_spec(x) for x in grads],
        out_shape=shapes_given + grads,
        scratch_shapes=[
            pltpu.VMEM((3 * width, D), BF16),
            pltpu.VMEM((width, D), BF16),
            pltpu.VMEM((3 * width, rows), BF16),
        ],
        compiler_params=pltpu.CompilerParams(vmem_limit_bytes=VMEM_LAST if types and masked else VMEM),
        cost_estimate=pl.CostEstimate(
            flops=4 * rows * D * width * 4 // COST, bytes_accessed=1 << 20, transcendentals=0
        ),
        name="attend_back",
    )(*args)
    return out[:-2] if types else out[0], out[-2:]


def gelu_both(u):
    c, cube = (2.0 / 3.141592653589793) ** 0.5, 0.044715
    square = u * u
    t = jnp.tanh(c * u * (1.0 + cube * square))
    half = 0.5 * (1.0 + t)
    return u * half, half + 0.5 * u * (1.0 - t * t) * (c + 3.0 * c * cube * square)


def ff_kernel(shapes, steps, types, *refs):
    refs = list(refs)
    n_ref, g_ref = refs.pop(0), refs.pop(0)
    pieces = [rows_of(x) for x in take(refs, shapes)]
    mix_ref, dn_ref = refs.pop(0), refs.pop(0)
    last = [refs.pop(0) for _ in range(3)] if types else []
    mix_out = refs.pop(0)
    last += [refs.pop(0) for _ in range(len(types) + 2 if types else 1)]
    grads = [rows_of([refs.pop(0)]) for _ in range(2)]
    hid_all, du_all = refs
    part = hid_all.shape[0] // 2
    step = pl.program_id(0)
    rows = pl.ds(pl.multiple_of(step * BLOCK, BLOCK), BLOCK)
    mix, dn = mix_ref[...], dn_ref[...]
    for index, (w_in, w_out) in enumerate(pieces):
        low = slice(index * part, (index + 1) * part)
        value, slope = gelu_both(nt(w_in[...], n_ref[rows, :]))
        hidden = value.astype(BF16)
        du = (slope * nt(w_out[...], g_ref[rows, :])).astype(BF16)
        hid_all[low, rows] = hidden
        du_all[low, rows] = du
        mix = mix + tn(hidden, w_out[...])
        dn = dn + tn(du, w_in[...])
    mix_out[...] = mix.astype(mix_out.dtype)
    if types:
        finish(last, dn)
    else:
        last[0][...] = dn

    @pl.when(step == steps - 1)
    def _():
        for at in range(0, D, BLOCK):
            columns = slice(at, at + BLOCK)
            for index, (d_in, d_out) in enumerate(grads):
                low = slice(index * part, (index + 1) * part)
                d_in[:, columns] = nn(du_all[low, :], n_ref[:, columns]).astype(BF16)
                d_out[:, columns] = nn(hid_all[low, :], g_ref[:, columns]).astype(BF16)


def ff_slot(normed, grad, pieces, mix, dn, last=(), types=()):
    rows = normed.shape[0]
    flat, shapes = flatten(pieces)
    part = flat[0].shape[1]
    width = 2 * part
    grads = [jax.ShapeDtypeStruct((2, part, D), BF16)] * 2
    taken, given, shapes_given = finish_specs(rows, types)
    if not types:
        taken, given, shapes_given = [], [rows_spec(D)], [jax.ShapeDtypeStruct((rows, D), F32)]
    out = pl.pallas_call(
        functools.partial(ff_kernel, shapes, rows // BLOCK, types),
        grid=(rows // BLOCK,),
        in_specs=[whole_spec(normed), whole_spec(grad)]
        + [whole_spec(x) for x in flat]
        + [rows_spec(D), rows_spec(D)]
        + taken,
        out_specs=[rows_spec(D)] + given + [whole_spec(x) for x in grads],
        out_shape=[jax.ShapeDtypeStruct((rows, D), BF16 if types else F32)] + shapes_given + grads,
        scratch_shapes=[pltpu.VMEM((width, rows), BF16), pltpu.VMEM((width, rows), BF16)],
        compiler_params=pltpu.CompilerParams(vmem_limit_bytes=VMEM),
        cost_estimate=pl.CostEstimate(
            flops=12 * rows * D * width // COST, bytes_accessed=1 << 20, transcendentals=0
        ),
        name="feed_forward",
    )(normed, grad, *flat, mix, dn, *last)
    return out[0], out[1:-2] if types else out[1], out[-2:]


def after(values, first):
    return lax.optimization_barrier((values, first))[0]


def hold(values, flights):
    return lax.optimization_barrier((values, flights))


def halves_of(array, axis):
    half = array.shape[axis] // 2
    core = lax.axis_index("dp") % 2
    return [
        lax.dynamic_slice_in_dim(array, at * half, half, axis=axis) for at in (core, 1 - core)
    ]


def attention_pieces(weight_qkv, weight_out):
    qkv = weight_qkv.transpose(0, 2, 1)
    whole = jnp.concatenate([qkv, weight_out[None]], axis=0)
    return halves_of(whole, 1)


def ff_pieces(weight_in, weight_out):
    return halves_of(jnp.stack([weight_in.T, weight_out]), 1)


def low_high(piece):
    half = piece.shape[0] // 2
    return [piece[:half], piece[half:]]


def near(piece):
    if lax.axis_size("mp") == 4:
        return {1: [flip(piece, 1)], 2: [flip(piece, 2)]}
    return {}


def far(piece, slots):
    size = lax.axis_size("mp")
    if size == 4:
        return {3: [flip(low_high(slots[1][0])[0], 2), flip(low_high(slots[2][0])[1], 1)]}
    low, high = low_high(piece)
    return {s: [x, y] for s, (x, y) in enumerate(zip(gather(low, False), gather(high, True))) if s}


def twins(arrays):
    return [twin(x) for x in arrays]


def pair_sums(grads, received):
    return [add(x, y) for x, y in zip(low_high(grads[0]), low_high(received))]


def send_far(sums):
    if lax.axis_size("mp") != 4:
        return []
    return [flip(sums[3][0], 1), flip(sums[3][1], 2)]


def send_plain(sums):
    if lax.axis_size("mp") != 4:
        return []
    return [flip(sums[1][0], 1), flip(sums[2][1], 2)]


def send_rest(sums, far_sums):
    if lax.axis_size("mp") != 4:
        return []
    low_two, high_one = far_sums
    return [flip(add(sums[1][1], high_one), 1), flip(add(sums[2][0], low_two), 2)]


def send_both(sums, far_sums):
    if lax.axis_size("mp") != 4:
        return []
    low_two, high_one = far_sums
    ahead = jnp.concatenate([sums[1][0], add(sums[1][1], high_one)], axis=0)
    across = jnp.concatenate([add(sums[2][0], low_two), sums[2][1]], axis=0)
    return [flip(ahead, 1), flip(across, 2)]


def settle_both(sums, both):
    if lax.axis_size("mp") != 4:
        return settle(sums, [], [])
    (low_one, high_one), (low_two, high_two) = low_high(both[0]), low_high(both[1])
    return settle(sums, [low_one, high_two], [high_one, low_two])


def settle(sums, plain, rest):
    if lax.axis_size("mp") != 4:
        return [scatter({s: x[i] for s, x in sums.items()}, bool(i)) for i in range(2)]
    terms = [(sums[0][0], plain[0], rest[1]), (sums[0][1], plain[1], rest[0])]
    return [sum(x.astype(F32) for x in three).astype(BF16) for three in terms]


def halves_kernel(core, mine, other, transposed, straight):
    count, half = mine.shape[0] - 1, mine.shape[1]
    first = core[0] == 0
    for which in range(count + 1):
        parts = [x[which].astype(F32) for x in (mine, other)]
        parts = [jnp.where(first, *parts), jnp.where(first, *parts[::-1])]
        if which < count:
            transposed[which] = jnp.concatenate([x.T for x in parts], axis=1)
        else:
            for at, part in enumerate(parts):
                straight[at * half : (at + 1) * half, :] = part


def both_halves(mine, other):
    count, half = mine.shape[0] - 1, mine.shape[1]
    taken = pl.BlockSpec((count + 1, half, BLOCK), lambda i: (0, 0, i))
    return pl.pallas_call(
        halves_kernel,
        grid=(D // BLOCK,),
        in_specs=[pl.BlockSpec(memory_space=pltpu.SMEM), taken, taken],
        out_specs=[
            pl.BlockSpec((count, BLOCK, 2 * half), lambda i: (0, i, 0)),
            pl.BlockSpec((2 * half, BLOCK), lambda i: (0, i)),
        ],
        out_shape=[
            jax.ShapeDtypeStruct((count, D, 2 * half), F32),
            jax.ShapeDtypeStruct((2 * half, D), F32),
        ],
        compiler_params=pltpu.CompilerParams(vmem_limit_bytes=VMEM),
        cost_estimate=pl.CostEstimate(flops=1 << 20, bytes_accessed=1 << 20, transcendentals=0),
        name="halves",
    )((lax.axis_index("dp") % 2).reshape(1), mine, other)


def shards(
    tokens,
    action_ids,
    clip_lengths,
    action_table,
    norm_gains,
    norm_shifts,
    spatial_qkv,
    spatial_out,
    temporal_qkv,
    temporal_out,
    ff_in,
    ff_out,
    out_grad,
):
    rows_here = tokens.shape[0]
    frames_here = rows_here // POS
    me, size = lax.axis_index("mp"), lax.axis_size("mp")
    frame_ids = lax.dynamic_slice_in_dim(action_ids.reshape(-1), me * frames_here, frames_here)
    one_hot = (
        frame_ids[:, None] == lax.broadcasted_iota(jnp.int32, (frames_here, ACTIONS), 1)
    ).astype(F32)
    per_frame = jnp.dot(one_hot, action_table, precision=lax.Precision.HIGHEST)
    embedded = jnp.broadcast_to(per_frame[:, None, :], (frames_here, POS, D)).reshape(rows_here, D)

    row = jnp.arange(BLOCK)
    frame_of = ((row // GROUP // frames_here) ^ me) * frames_here + row // GROUP % frames_here
    allowed = (
        (row[:, None] % GROUP == row[None] % GROUP)
        & (frame_of[:, None] <= frame_of[None])
        & (frame_of[:, None] < clip_lengths[0])
    )
    mask = jnp.where(allowed, 0.0, -1e9).astype(F32)

    others = [[1, 2], [3]] if size == 4 else [list(range(1, size))]

    own, other = attention_pieces(spatial_qkv, spatial_out)
    close = near(own)
    first = tokens.astype(F32) + embedded
    normed_a = norm_rows(first, norm_gains[0], norm_shifts[0])[0].astype(BF16)
    temporal_own, temporal_other = attention_pieces(*after((temporal_qkv, temporal_out), normed_a))
    spatial = {0: [[own], [other]]}
    kept_a = {}
    second, *kept = attend_slots(normed_a, [spatial[0]], first, None)
    kept_a[0] = (kept, 0)
    (second, temporal_own, temporal_other), close = hold((second, temporal_own, temporal_other), close)
    distant = far(own, close)
    near_b = near(temporal_own)
    close = {s: [x, twins(x)] for s, x in close.items()}
    second, close = hold(second, close)
    if close:
        spatial |= close
        second, *kept = attend_slots(normed_a, [spatial[s] for s in others[0]], second, None)
        kept_a[1] = (kept, 0)
    second, distant = hold(second, distant)
    distant = {s: [x, twins(x)] for s, x in distant.items()}
    second, distant = hold(second, distant)
    spatial |= distant
    second, *kept = attend_slots(normed_a, [spatial[s] for s in others[-1]], second, None, BF16)
    kept_a[3] = (kept, 0)
    second, near_b = hold(second, near_b)

    distant = far(temporal_own, near_b)
    near_b = {s: [x, twins(x)] for s, x in near_b.items()}
    parts = send_positions(second)
    own, other = ff_pieces(*after((ff_in, ff_out), parts[0]))
    parts, (own, other, near_b, distant) = hold(parts, (own, other, near_b, distant))
    grad_parts = send_positions(after(out_grad, parts))
    distant = {s: [x, twins(x)] for s, x in distant.items()}
    (parts, own, other), distant = hold((parts, own, other), distant)
    close = near(own)
    temporal = {0: [[temporal_own], [temporal_other]]} | near_b | distant
    order_b = [s for group in others for s in group] + [0]
    norms = jnp.concatenate([norm_gains[1:2], norm_shifts[1:2], norm_gains[2:], norm_shifts[2:]], axis=0)
    third, *kept, second, normed_b, normed_c = attend_arrived(
        parts, norms, [temporal[s] for s in order_b], mask
    )
    kept_b = [(kept, 0), (kept, 2)] if size == 4 else [(kept, 0), (kept, size - 1)]
    (third, normed_c), grad_parts = hold((third, normed_c), grad_parts)

    grad_result = join_positions(grad_parts)
    result, grad_normed = third, jnp.zeros((rows_here, D), F32)
    grads = {}

    def feed(slot, pieces, flights):
        nonlocal result, grad_normed
        last, types = ((norm_gains[2:], third, grad_result), (F32, BF16)) if slot == size - 1 else ((), ())
        result, grad_normed, grads[slot] = ff_slot(
            normed_c, grad_result, pieces, result, grad_normed, last, types
        )
        (result, grad_normed, grads[slot]), flights = hold((result, grad_normed, grads[slot]), flights)
        return flights

    def swap(slots):
        return {s: twin(grads[s][1]) for s in slots}

    received, sums_c, plain_c = {}, {}, []

    def sum_up(*slots):
        for s in slots:
            sums_c[s] = pair_sums(grads[s], received[s])

    if size == 4:
        close = feed(0, [[own], [other]], close)
        distant = far(own, close)
        twin_one, twin_two = twins(close[1]), twins(close[2])
        result, twin_one = hold(result, twin_one)
        distant, twin_two, got = feed(1, [close[1], twin_one], (distant, twin_two, swap([0])))
        received |= got
        twin_three, got = feed(2, [close[2], twin_two], (twins(distant[3]), swap([1])))
        received |= got | swap([2])
        sum_up(0, 1, 2)
        result, (sums_c[1][0], sums_c[2][1]) = hold(result, (sums_c[1][0], sums_c[2][1]))
        plain_c = feed(3, [distant[3], twin_three], send_plain(sums_c))
    else:
        distant = feed(0, [[own], [other]], far(own, close))
        for slot in range(1, size):
            feed(slot, [distant[slot], twins(distant[slot])], [])
        received = swap(range(size - 1))
        sum_up(*range(size - 1))
    received |= swap([size - 1])
    sum_up(size - 1)
    grad_third, grad_sent, norm_sums_c, _ = grad_normed

    def back(normed, gradient, kept, slots, mask, steps, sums, plans, last, types):
        mine, received, got, sums_here = {}, {}, [], plans[-1]
        total = jnp.zeros((rows_here, D), F32)
        if size == 4:
            total, sums[3] = hold(total, sums[3])
        swapped = {}
        for at, group in enumerate(steps):
            flights = plans[at](sums, got) if size == 4 else []
            end = (last, types) if at == len(steps) - 1 else ()
            total, found = back_slots(
                normed, gradient, kept[at], [slots[s] for s in group], total, mask, *end
            )
            (total, found), (flights, swapped) = hold((total, found), (flights, swapped))
            for place, s in enumerate(swapped and steps[at - 1]):
                one = slice(4 * place, 4 * place + 4)
                sums_here[s] = pair_sums([mine[at - 1][one]], swapped[0][one])
            mine[at] = found[0]
            swapped = [twin(found[1])]
            got.append(flights)
        for place, s in enumerate(steps[-1]):
            one = slice(4 * place, 4 * place + 4)
            sums_here[s] = pair_sums([found[0][one]], swapped[0][one])
        return total, got

    sums_b, sums_a = {}, {}
    (grad_second, norm_sums_b, _), got = back(
        normed_b, grad_sent, kept_b, temporal, mask, [[1, 2], [3, 0]] if size == 4 else others + [[0]], sums_c,
        [lambda sums, got: send_far(sums), lambda sums, got: send_rest(sums, got[0]), sums_b],
        (norm_gains[1:2], second, grad_third), (BF16,),
    )
    rest_c = got[1] if size == 4 else []
    parts = send_frames(grad_second)
    sum_c, on_way_c = clips_first(*settle(sums_c, plain_c, rest_c))
    (parts, sum_c, sums_b), on_way_c = hold((parts, sum_c, sums_b), on_way_c)
    sum_c = clips_between(sum_c, on_way_c)
    grad_second = join_frames(parts)
    cut = sum_c.shape[1] * 3 // 8
    pieces_c = [sum_c[:, :cut], sum_c[:, cut:]]

    def first_flights(sums, got):
        return send_far(sums), send_far_clips(pieces_c[0])

    def second_flights(sums, got):
        return send_both(sums, got[0][0]), send_far_clips(after(pieces_c[1], got[0][1]))

    def third_flights(sums, got):
        nonlocal sum_c
        sum_c, on_way = clips_last(sum_c, jnp.concatenate([got[0][1], got[1][1]], axis=1))
        return send_far(sums_a), on_way

    steps = others[::-1] + [[0]]
    kept_a = [kept_a[3], kept_a[1], kept_a[0]] if size == 4 else [kept_a[3], kept_a[0]]
    (grad_first, norm_sums_a, frame_grads), got = back(
        normed_a, grad_second, kept_a, spatial, None, steps, sums_b,
        [first_flights, second_flights, third_flights, sums_a],
        (norm_gains[:1], first, grad_second), (F32,),
    )
    if size == 4:
        far_a, on_way_c = got[2]
        both_b = got[1][0]
    else:
        far_a = both_b = []
        sum_c, on_way_c = clips_last(sum_c, send_far_clips(sum_c))

    small = jnp.concatenate(
        [x[i : i + 1] for i in range(2) for x in (norm_sums_a, norm_sums_b, norm_sums_c)]
        + [jnp.dot(one_hot.T, frame_grads[::8], precision=lax.Precision.HIGHEST)],
        axis=0,
    )
    both_a = send_both(sums_a, far_a)
    sum_b, on_way_b = clips_first(*settle_both(sums_b, both_b))
    sum_b = clips_between(sum_b, on_way_b)
    cut = sum_b.shape[1] // 2
    first_b = send_far_clips(sum_b[:, :cut])
    small = over_all(small, [("dp", 1)])
    (small, sum_b, sums_a[0]), (both_a, first_b) = hold((small, sum_b, sums_a[0]), (both_a, first_b))
    sum_a, on_way_a = clips_first(*settle_both(sums_a, both_a))
    last_b = send_far_clips(sum_b[:, cut:])
    whole_c = clips_joined(sum_c, on_way_c)
    other_c = twin(whole_c)
    small = over_all(small, [("mp", x) for x in bits_of(size, False)])
    small = over_all(small, [("dp", x) for x in clip_offsets()[1:]])
    (small, sum_a, sum_b, result), (on_way_a, other_c, last_b) = hold(
        (small, sum_a, sum_b, result), (on_way_a, other_c, last_b)
    )
    sum_a, on_way_a = clips_next(sum_a, on_way_a)
    sum_b, on_way_b = clips_last(sum_b, jnp.concatenate([first_b, last_b], axis=1))
    parts = send_frames(result)
    grad_ff_in, grad_ff_out = both_halves(whole_c, other_c)
    (grad_ff_in, grad_ff_out, sum_a, sum_b), (on_way_a, on_way_b, parts) = hold(
        (grad_ff_in, grad_ff_out, sum_a, sum_b), (on_way_a, on_way_b, parts)
    )
    sum_a, on_way_a = clips_last(sum_a, on_way_a)
    whole_b = clips_joined(sum_b, on_way_b)
    grad_tqkv, grad_tout = both_halves(whole_b, twin(whole_b))
    mixed = join_frames(parts)
    small = over_all(after(small, sum_a), [("dp", clip_offsets()[0])])
    (small, grad_tqkv, grad_tout, mixed, sum_a), on_way_a = hold(
        (small, grad_tqkv, grad_tout, mixed, sum_a), on_way_a
    )
    whole_a = clips_joined(sum_a, on_way_a)
    grad_sqkv, grad_sout = both_halves(whole_a, twin(whole_a))
    grad_ff_in = grad_ff_in[0]
    gains_sum, shifts_sum, table_sum = small[:3], small[3:6], small[6:]
    return (
        mixed,
        grad_first,
        table_sum,
        gains_sum,
        shifts_sum,
        grad_sqkv,
        grad_sout,
        grad_tqkv,
        grad_tout,
        grad_ff_in,
        grad_ff_out,
    )


def solution(mesh):
    return jax.shard_map(
        shards,
        mesh=mesh,
        in_specs=(
            P(("dp", "mp"), None),
            P("dp", None),
            P("dp"),
            P(),
            P(),
            P(),
            P(None, None, "mp"),
            P("mp", None),
            P(None, None, "mp"),
            P("mp", None),
            P(None, "mp"),
            P("mp", None),
            P(("dp", "mp"), None),
        ),
        out_specs=(
            P(("dp", "mp"), None),
            P(("dp", "mp"), None),
            P(),
            P(),
            P(),
            P(None, None, "mp"),
            P("mp", None),
            P(None, None, "mp"),
            P("mp", None),
            P(None, "mp"),
            P("mp", None),
        ),
        check_vma=False,
    )
```
